128 devices in a mesh: member: 8 (over x, core), slab: 16 (over z, y).
Axes of the slice: x: 4, y: 4, z: 4, core: 2. Of those that a mesh axis runs over, the one named last changes fastest.
Arguments:
- nonnegative_volumes: float32 [8, 64, 128, 128], P('member', 'slab'), may hold values from 0.25 to 4
- reaction: float32 [64, 128, 128], P('slab'), may hold values from 0.02 to 0.2
- diffusivity: float32 [3], replicated, may hold values from 4 to 32
- member_weights: float32 [8], P('member'), may hold values from 0.5 to 2
Outputs:
- wasserstein_centroid: float32 [64, 128, 128], P('slab')
- final_multipliers: float32 [8, 64, 128, 128], P('member', 'slab')
The draws below stay inside these ranges and needn't reach their ends.
All inputs are finite; a program needn't handle non-finite values.
Results may differ from the reference program's by a relative error of at most 0.0001.
Values sent between devices are 32-bit elements; how exact they have to be, the bound alone decides.
A program may use at most 128 MiB of HBM per device.

```python
import math
import jax
import jax.numpy as jnp

NX = 128
NY = 128
ITERS = 3
LEVELS = 4
PRE = 2
POST = 2
COARSE_SWEEPS = 8
NZ = 64
MEMBERS = 8


def block_scale(rng, dims, cuts, low, largest):
    def one(position, blocks):
        steps = jax.random.uniform(jax.random.fold_in(jax.random.fold_in(rng, 6), position), (blocks,), jnp.float32, low / len(cuts), largest / len(cuts))
        return jnp.repeat(jnp.exp(steps), dims[position] // blocks).reshape((-1,) + (1,) * (len(dims) - position - 1))

    level = one(*cuts[0])
    for cut in cuts[1:]:
        level = level * one(*cut)
    return level


def setup_inputs(seed: int = 0) -> dict:
    seeds = jax.random.split(jax.random.key(seed), 5)
    return {
        "nonnegative_volumes": jnp.clip(jnp.exp(math.log(4.0) - 2.7725887 * jax.random.uniform(seeds[0], (MEMBERS, NZ, NY, NX), jnp.float32) ** block_scale(seeds[0], (MEMBERS, NZ, NY, NX), ((0, 8), (1, 16)), -0.2, 0.2)), 0.25, 4.0),
        "reaction": jnp.clip(jnp.exp(math.log(0.2) - 2.3025851 * jax.random.uniform(seeds[1], (NZ, NY, NX), jnp.float32) ** block_scale(seeds[1], (NZ, NY, NX), ((0, 16),), -0.2, 0.2)), 0.02, 0.2),
        "diffusivity": jnp.clip(jnp.exp(jax.random.uniform(seeds[2], (3,), jnp.float32, math.log(4.0), math.log(32.0))), 4.0, 32.0),
        "member_weights": jnp.clip(jnp.exp(math.log(2.0) - 1.3862944 * jax.random.uniform(seeds[3], (MEMBERS,), jnp.float32) ** block_scale(seeds[3], (MEMBERS,), ((0, 8),), -0.2, 0.2)), 0.5, 2.0),
    }


OMEGA = 0.8


def restrict(array):
    zdim, ydim, xdim = array.shape
    folded = array.reshape(zdim // 2, 2, ydim, xdim)
    summed = folded[:, 0] + folded[:, 1]
    folded = summed.reshape(zdim // 2, ydim // 2, 2, xdim)
    summed = folded[:, :, 0] + folded[:, :, 1]
    folded = summed.reshape(zdim // 2, ydim // 2, xdim // 2, 2)
    summed = folded[..., 0] + folded[..., 1]
    return summed * 0.125


def prolong(array):
    zdim, ydim, xdim = array.shape
    spread = jnp.broadcast_to(array[:, None, :, None, :, None], (zdim, 2, ydim, 2, xdim, 2))
    return spread.reshape(2 * zdim, 2 * ydim, 2 * xdim)


def stencil(padded, reaction_level, coupling):
    field = padded[1:-1]
    padded_side = jnp.pad(field, ((0, 0), (1, 1), (1, 1)))
    second_z = 2.0 * field - padded[2:] - padded[:-2]
    second_y = 2.0 * field - padded_side[:, 2:, 1:-1] - padded_side[:, :-2, 1:-1]
    second_x = 2.0 * field - padded_side[:, 1:-1, 2:] - padded_side[:, 1:-1, :-2]
    return reaction_level * field + coupling[0] * second_z + coupling[1] * second_y + coupling[2] * second_x


def apply_operator(field, multigrid_depth, reactions, couplings):
    padded = jnp.pad(field, ((1, 1), (0, 0), (0, 0)))
    return stencil(padded, reactions[multigrid_depth], couplings[multigrid_depth])


def vcycle(source, multigrid_depth, reactions, couplings, diagonals):
    diagonal = diagonals[multigrid_depth]
    iterate = OMEGA * source / diagonal
    if multigrid_depth == LEVELS - 1:
        for repeat in range(COARSE_SWEEPS - 1):
            iterate = iterate + OMEGA * (source - apply_operator(iterate, multigrid_depth, reactions, couplings)) / diagonal
        return iterate
    for repeat in range(PRE - 1):
        iterate = iterate + OMEGA * (source - apply_operator(iterate, multigrid_depth, reactions, couplings)) / diagonal
    residual = source - apply_operator(iterate, multigrid_depth, reactions, couplings)
    correction = vcycle(restrict(residual), multigrid_depth + 1, reactions, couplings, diagonals)
    iterate = iterate + prolong(correction)
    for repeat in range(POST):
        iterate = iterate + OMEGA * (source - apply_operator(iterate, multigrid_depth, reactions, couplings)) / diagonal
    return iterate


def reference(nonnegative_volumes, reaction, diffusivity, member_weights):
    reactions = [reaction]
    for multigrid_depth in range(1, LEVELS):
        reactions.append(restrict(reactions[-1]))
    couplings = [diffusivity * (0.25 ** multigrid_depth) for multigrid_depth in range(LEVELS)]
    diagonals = [reactions[multigrid_depth] + 2.0 * (couplings[multigrid_depth][0] + couplings[multigrid_depth][1] + couplings[multigrid_depth][2]) for multigrid_depth in range(LEVELS)]

    def gibbs_smoother(source):
        return vcycle(source, 0, reactions, couplings, diagonals)

    smooth_each_volume = jax.vmap(gibbs_smoother)
    final_multipliers = jnp.ones_like(nonnegative_volumes)
    weight_total = jnp.sum(member_weights)
    wasserstein_centroid = jnp.zeros_like(nonnegative_volumes[0])
    for repeat in range(ITERS):
        companion_multiplier = nonnegative_volumes / smooth_each_volume(final_multipliers)
        desired_mass_vector = final_multipliers * smooth_each_volume(companion_multiplier)
        log_total = jnp.sum(member_weights[:, None, None, None] * jnp.log(desired_mass_vector), axis=0)
        wasserstein_centroid = jnp.exp(log_total / weight_total)
        final_multipliers = final_multipliers * wasserstein_centroid[None] / desired_mass_vector
    return wasserstein_centroid, final_multipliers
```

```python
import jax
import jax.numpy as jnp
from jax import lax
from jax.experimental import pallas as pl
from jax.experimental.pallas import tpu as pltpu
from jax.sharding import PartitionSpec as P

ITERS = 3
COARSE_SWEEPS = 8
OMEGA = 0.8
LANES = 128
NZ, NY = 64, 128
F32 = jnp.float32
MESH = pl.DeviceIdType.MESH
DIRECTIONS = ((-1, 0), (1, 0), (0, -1), (0, 1), (-1, -1), (-1, 1), (1, -1), (1, 1))

GEOMETRY = (
    dict(own_z=4, own_y=16, nz=16, ny=32, hz=3, planes=24, rows=64),
    dict(own_z=5, own_y=16, nz=8, ny=16, hz=4, planes=18, rows=48),
)


def dot(a, b):
    return jnp.dot(a, b, precision=lax.Precision.HIGHEST, preferred_element_type=F32)


def flat(a):
    return a.reshape(-1, LANES)


def lane_roll(a, shift):
    return pltpu.roll(flat(a), shift % LANES, 1).reshape(a.shape)


def kernel(
    vol_ref, reaction_ref, diff_ref, weight_ref, cent_out, mult_out,
    S0, D0, DG0, U0a, U0b, C0, T0,
    S1, D1, DG1, U1a, U1b, C1, T1,
    G, S2, D2, DG2, U2, T2, C2, D3,
    VB, MB, LB, XB, HB, PB, CB, WS, WB, IW,
    Rx, Rx1, R3a, R3b, P3a, P3b, PM, P0, PP, Px,
    h0_send, h0_recv, h1_send, h1_recv, g_send, g_recv,
    ra_send, ra_recv, va_send, va_recv, w_send, w_recv,
    x_send, x_recv, p_send, p_recv, c_send, c_recv, f_send, f_recv, o_send, o_recv,
):
    member, slab = lax.axis_index("member"), lax.axis_index("slab")
    cz, cy = slab // 4, lax.rem(slab, 4)
    mx, mc = member // 2, lax.rem(member, 2)

    def at_slab(dz, dy):
        return lax.rem(cz + dz + 4, 4) * 4 + lax.rem(cy + dy + 4, 4)

    def remote(src, dst, send, recv, to):
        return pltpu.make_async_remote_copy(
            src_ref=src, dst_ref=dst, send_sem=send, recv_sem=recv, device_id=to, device_id_type=MESH
        )

    barrier = pltpu.get_barrier_semaphore()
    for d in range(1, 16):
        pl.semaphore_signal(barrier, inc=1, device_id=(member, at_slab(d // 4, d % 4)), device_id_type=MESH)
    for d in range(1, 8):
        pl.semaphore_signal(barrier, inc=1, device_id=(lax.rem(member + d, 8), slab), device_id_type=MESH)
    pl.semaphore_wait(barrier, 22)

    def halo(level, slot):
        g = GEOMETRY[level]
        ref, send, recv = ((S0, h0_send, h0_recv), (S1, h1_send, h1_recv))[level]
        copies = []
        for k, (dz, dy) in enumerate(DIRECTIONS):
            oz, oy, nz, ny, hz = g["own_z"], g["own_y"], g["nz"], g["ny"], g["hz"]
            zs, zn, zd = {-1: (oz, hz, oz + nz), 0: (oz, nz, oz), 1: (oz + nz - hz, hz, oz - hz)}[dz]
            ys, yn, yd = {-1: (oy, 8, oy + ny), 0: (oy, ny, oy), 1: (oy + ny - 8, 8, oy - 8)}[dy]
            copies.append(
                remote(
                    ref.at[slot, pl.ds(zs, zn), pl.ds(ys, yn)],
                    ref.at[slot, pl.ds(zd, zn), pl.ds(yd, yn)],
                    send.at[slot, k], recv.at[slot, k], (member, at_slab(dz, dy)),
                )
            )
        return copies

    def gather(slot):
        return [
            remote(G.at[slot, slab], G.at[slot, slab], g_send.at[slot, d], g_recv.at[slot, d], (member, at_slab(d // 4, d % 4)))
            for d in range(1, 16)
        ]

    def begin(copies):
        for c in copies:
            c.start()

    def finish(copies):
        for c in copies:
            c.wait()

    def to_blocks(src, dst, dst_z, dst_y, send, recv):
        copies = []
        for d in range(1, 4):
            to = lax.rem(cy + d, 4)
            copies.append(
                remote(
                    src.at[:, pl.ds(pl.multiple_of(32 * to, 32), 32)],
                    dst.at[pl.ds(dst_z + 4 * cy, 4), pl.ds(dst_y, 32)],
                    send.at[d - 1], recv.at[d - 1], (member, cz * 4 + to),
                )
            )
        return copies

    def to_slabs(src, src_z, src_y, dst, send, recv):
        copies = []
        for d in range(1, 4):
            to = lax.rem(cy + d, 4)
            copies.append(
                remote(
                    src.at[pl.ds(src_z + 4 * to, 4), pl.ds(src_y, 32)],
                    dst.at[:, pl.ds(pl.multiple_of(32 * cy, 32), 32)],
                    send.at[d - 1], recv.at[d - 1], (member, cz * 4 + to),
                )
            )
        return copies

    reaction_moves = to_blocks(reaction_ref, S0.at[1], 4, 16, ra_send, ra_recv)
    volume_moves = to_blocks(vol_ref, VB, 0, 0, va_send, va_recv)
    begin(reaction_moves)
    begin(volume_moves)
    WS[...] = jnp.full((8, LANES), weight_ref[0], F32)
    weight_moves = [
        remote(WS, WB.at[d], w_send.at[d - 1], w_recv.at[d - 1], (lax.rem(member + d, 8), slab)) for d in range(1, 8)
    ]
    begin(weight_moves)

    coupling = [[diff_ref[i] * (0.25**level) for i in range(3)] for level in range(4)]
    center = [2.0 * (c[0] + c[1] + c[2]) for c in coupling]

    lane = lax.broadcasted_iota(jnp.int32, (1, LANES), 1)
    one, zero = jnp.ones((1, LANES), F32), jnp.zeros((1, LANES), F32)

    def lane_mask(keep):
        return jnp.where(keep, one, zero)

    row_i = lax.broadcasted_iota(jnp.int32, (LANES, LANES), 0)
    col_i = lax.broadcasted_iota(jnp.int32, (LANES, LANES), 1)

    def half(a):
        return lax.shift_right_logical(a, 1)

    def matrix(keep, value=1.0):
        return jnp.where(keep, jnp.full((LANES, LANES), value, F32), jnp.zeros((LANES, LANES), F32))

    col_chunk, col_in = col_i & ~31, col_i & 31
    row_chunk, row_in = row_i & ~31, row_i & 31
    Rx[...] = matrix(half(row_i) == col_i, 0.125)
    Rx1[...] = matrix((row_i < 64) & (half(row_i) + 32 * cz == col_i), 0.125)
    R3a[...] = matrix(row_chunk + half(row_in) == col_i, 0.125)
    R3b[...] = matrix(row_chunk + 16 + half(row_in) == col_i, 0.125)
    P3a[...] = matrix(row_i == col_chunk + half(col_in))
    P3b[...] = matrix(row_i == col_chunk + 16 + half(col_in))
    widen = (col_i < 64)
    PM[...] = matrix(widen & (row_i == half(col_i) + 32 * (cz - 1)) & (row_i >= 0))
    P0[...] = matrix(widen & (row_i == half(col_i) + 32 * cz))
    PP[...] = matrix(widen & (row_i == half(col_i) + 32 * (cz + 1)))
    Px[...] = matrix(row_i == half(col_i))

    left = [lane_mask(lane > 0) * coupling[0][2], None, lane_mask((lane & 31) > 0) * coupling[2][2], lane_mask((lane & 15) > 0) * coupling[3][2]]
    right = [lane_mask(lane < 127) * coupling[0][2], None, lane_mask((lane & 31) < 31) * coupling[2][2], lane_mask((lane & 15) < 15) * coupling[3][2]]

    for ref in (U0a, U0b):
        ref[:, 0:8, :] = jnp.zeros((24, 8, LANES), F32)
        ref[:, 56:64, :] = jnp.zeros((24, 8, LANES), F32)
    for ref in (U1a, U1b):
        ref[:, 0:8, :] = jnp.zeros((18, 8, LANES), F32)
        ref[:, 40:48, :] = jnp.zeros((18, 8, LANES), F32)
    U2[:, 0:8, :] = jnp.zeros((4, 8, LANES), F32)
    U2[:, 40:48, :] = jnp.zeros((4, 8, LANES), F32)
    S0[0, 1:23, 8:56, :] = jnp.ones((22, 48, LANES), F32)

    def neighbours(level, u, z, n, lo, rows):
        c = coupling[level]
        mid = u[pl.ds(z, n), lo : lo + rows, :]
        total = c[0] * (u[pl.ds(z - 1, n), lo : lo + rows, :] + u[pl.ds(z + 1, n), lo : lo + rows, :])
        total += c[1] * (u[pl.ds(z, n), lo - 1 : lo + rows - 1, :] + u[pl.ds(z, n), lo + 1 : lo + rows + 1, :])
        if level == 0:
            total += left[0] * lane_roll(mid, 1) + right[0] * lane_roll(mid, -1)
        else:
            total += c[2] * (lane_roll(mid, 1) + lane_roll(mid, -1))
        return mid, total

    def over(z0, count, step, body):
        def one_step(i, _):
            body(z0 + i * step)
            return 0

        lax.fori_loop(0, count // step, one_step, 0)

    def sweep(level, u, s, slot, d, z, n, lo, rows):
        mid, total = neighbours(level, u, z, n, lo, rows)
        return (1.0 - OMEGA) * mid + d[pl.ds(z, n), lo : lo + rows, :] * (s[slot, pl.ds(z, n), lo : lo + rows, :] + total)

    def residual(level, u, s, slot, dg, z, n, lo, rows, z_own):
        mid, total = neighbours(level, u, z, n, lo, rows)
        return s[slot, pl.ds(z, n), lo : lo + rows, :] - dg[pl.ds(z - z_own, n)] * mid + total

    def restrict0(fine, slot):
        def body(z):
            a = fine(z)
            i = (z - 4) // 2
            for k in range(2):
                T0[i + k] = a[2 * k] + a[2 * k + 1]

        over(4, 16, 4, body)

        def rows(i):
            e = T0[pl.ds(i, 4), pl.ds(0, 16, stride=2), :] + T0[pl.ds(i, 4), pl.ds(1, 16, stride=2), :]
            S1[slot, pl.ds(5 + i, 4), 16:32, :] = dot(flat(e), Rx[...]).reshape(4, 16, LANES)

        over(0, 8, 4, rows)

    def restrict1(fine, slot):
        a = fine(5)
        for k in range(4):
            T1[k] = a[2 * k] + a[2 * k + 1]
        e = T1[:, pl.ds(0, 8, stride=2), :] + T1[:, pl.ds(1, 8, stride=2), :]
        G[slot, slab] = dot(flat(e), Rx1[...]).reshape(4, 8, LANES)

    def gathered(slot):
        for j in range(4):
            total = G[slot, j] + G[slot, 4 + j] + G[slot, 8 + j] + G[slot, 12 + j]
            S2[:, 8 * j : 8 * j + 8, :] = total

    def restrict2(a):
        T2[0] = a[0] + a[1]
        T2[1] = a[2] + a[3]
        e = T2[:, pl.ds(0, 16, stride=2), :] + T2[:, pl.ds(1, 16, stride=2), :]
        return dot(e[0], R3a[...]) + dot(e[1], R3b[...])

    first_chunk, last_chunk = lane_mask(lane >= 32), lane_mask(lane < 96)

    def neighbours2():
        c = coupling[2]
        mid = U2[:, 8:40, :]
        before = jnp.concatenate([(lane_roll(mid[3], 32) * first_chunk)[None], mid[:3]], axis=0)
        after = jnp.concatenate([mid[1:], (lane_roll(mid[0], -32) * last_chunk)[None]], axis=0)
        total = c[0] * (before + after) + c[1] * (U2[:, 7:39, :] + U2[:, 9:41, :])
        total += left[2] * lane_roll(mid, 1) + right[2] * lane_roll(mid, -1)
        return mid, total

    def sweep2():
        mid, total = neighbours2()
        U2[:, 8:40, :] = (1.0 - OMEGA) * mid + D2[...] * (S2[...] + total)

    row16 = lax.broadcasted_iota(jnp.int32, (16, LANES), 0)
    zeros16, ones16 = jnp.zeros((16, LANES), F32), jnp.ones((16, LANES), F32)
    up3 = jnp.where(row16 > 0, ones16, zeros16) * coupling[3][1]
    down3 = jnp.where(row16 < 15, ones16, zeros16) * coupling[3][1]
    before3 = lane_mask(lane >= 16) * coupling[3][0]
    after3 = lane_mask(lane < 112) * coupling[3][0]

    def level3(s):
        d = D3[...]
        u = d * s
        for _ in range(COARSE_SWEEPS - 1):
            total = before3 * lane_roll(u, 16) + after3 * lane_roll(u, -16)
            total += up3 * pltpu.roll(u, 1, 0) + down3 * pltpu.roll(u, 15, 0)
            total += left[3] * lane_roll(u, 1) + right[3] * lane_roll(u, -1)
            u = (1.0 - OMEGA) * u + d * (s + total)
        return u

    def inside(level, z, n, lo, rows):
        g = GEOMETRY[level]
        zi = lax.broadcasted_iota(jnp.int32, (n, rows, LANES), 0) + (z - g["own_z"] + g["nz"] * cz)
        yi = lax.broadcasted_iota(jnp.int32, (n, rows, LANES), 1) + (lo - g["own_y"] + g["ny"] * cy)
        keep = (zi >= 0) & (zi < 4 * g["nz"]) & (yi >= 0) & (yi < 4 * g["ny"])
        if level:
            keep = keep & (lax.broadcasted_iota(jnp.int32, (n, rows, LANES), 2) < 64)
        return keep

    finish(reaction_moves)
    S0[1, pl.ds(4 + 4 * cy, 4), 16:48, :] = reaction_ref[:, pl.ds(pl.multiple_of(32 * cy, 32), 32), :]
    begin(halo(0, 1))
    restrict0(lambda z: S0[1, pl.ds(z, 4), 16:48, :], 1)
    begin(halo(1, 1))
    restrict1(lambda z: S1[1, pl.ds(z, 8), 16:32, :], 1)
    begin(gather(1))
    VB[pl.ds(4 * cy, 4)] = vol_ref[:, pl.ds(pl.multiple_of(32 * cy, 32), 32), :]

    def diag0(z):
        DG0[pl.ds(z - 4, 4)] = S0[1, pl.ds(z, 4), 16:48, :] + center[0]

    over(4, 16, 4, diag0)
    DG1[...] = S1[1, 5:13, 16:32, :] + center[1]
    finish(halo(0, 1))

    def dinv0(z):
        D0[pl.ds(z, 2), 8:56, :] = jnp.where(
            inside(0, z, 2, 8, 48), OMEGA / (S0[1, pl.ds(z, 2), 8:56, :] + center[0]), jnp.zeros((2, 48, LANES), F32)
        )

    over(1, 22, 2, dinv0)
    finish(halo(1, 1))

    def dinv1(z):
        D1[pl.ds(z, 2), 8:40, :] = jnp.where(
            inside(1, z, 2, 8, 32), OMEGA / (S1[1, pl.ds(z, 2), 8:40, :] + center[1]), jnp.zeros((2, 32, LANES), F32)
        )

    over(1, 16, 2, dinv1)
    finish(gather(1))
    gathered(1)
    DG2[...] = S2[...] + center[2]
    D2[...] = OMEGA / DG2[...]
    D3[...] = OMEGA / (restrict2(S2[...]) + center[3])
    finish(volume_moves)
    finish(weight_moves)
    weight_total = WS[...]
    for d in range(1, 8):
        weight_total += WB[d]
    IW[...] = 1.0 / weight_total

    def vcycle(slot, use):
        def first0(z):
            U0a[pl.ds(z, 2), 8:56, :] = D0[pl.ds(z, 2), 8:56, :] * S0[slot, pl.ds(z, 2), 8:56, :]

        over(1, 22, 2, first0)

        def pre0(z):
            U0b[pl.ds(z, 4), 8:56, :] = sweep(0, U0a, S0, slot, D0, z, 4, 8, 48)

        over(2, 20, 4, pre0)
        restrict0(lambda z: residual(0, U0b, S0, slot, DG0, z, 4, 16, 32, 4), slot)
        begin(halo(1, slot))
        finish(halo(1, slot))

        def first1(z):
            U1a[pl.ds(z, 4), 8:40, :] = D1[pl.ds(z, 4), 8:40, :] * S1[slot, pl.ds(z, 4), 8:40, :]

        over(1, 16, 4, first1)

        def pre1(z):
            U1b[pl.ds(z, 7), 8:40, :] = sweep(1, U1a, S1, slot, D1, z, 7, 8, 32)

        over(2, 14, 7, pre1)
        restrict1(lambda z: residual(1, U1b, S1, slot, DG1, z, 8, 16, 16, 5), slot)
        begin(gather(slot))
        finish(gather(slot))
        gathered(slot)

        U2[:, 8:40, :] = D2[...] * S2[...]
        sweep2()
        mid, total = neighbours2()
        s3 = restrict2(S2[...] - DG2[...] * mid + total)
        u3 = level3(s3)
        for k, matrix_ref in ((0, P3a), (1, P3b)):
            p = dot(u3, matrix_ref[...])
            C2[k, pl.ds(0, 16, stride=2), :] = p
            C2[k, pl.ds(1, 16, stride=2), :] = p
        for k in range(4):
            U2[k, 8:40, :] += C2[k // 2]
        sweep2()
        sweep2()

        near = U2[:, pl.ds(pl.multiple_of(8 * cy, 8), 24), :][:, 4:20, :]
        wide = jnp.concatenate(
            [dot(flat(near[2:4]), PM[...]), dot(flat(near), P0[...]), dot(flat(near[0:2]), PP[...])], axis=0
        ).reshape(8, 16, LANES)
        C1[:, pl.ds(0, 16, stride=2), :] = wide
        C1[:, pl.ds(1, 16, stride=2), :] = wide
        for k in range(8):
            U1b[1 + 2 * k, 8:40, :] += C1[k]
            U1b[2 + 2 * k, 8:40, :] += C1[k]

        def post1a(z):
            U1a[pl.ds(z, 6), 8:40, :] = sweep(1, U1b, S1, slot, D1, z, 6, 8, 32)

        over(3, 12, 6, post1a)

        def post1b(z):
            U1b[pl.ds(z, 5), 8:40, :] = sweep(1, U1a, S1, slot, D1, z, 5, 8, 32)

        over(4, 10, 5, post1b)

        def widen0(i):
            wide = dot(flat(U1b[pl.ds(4 + i, 5), 12:36, :]), Px[...]).reshape(5, 24, LANES)
            C0[:, pl.ds(0, 24, stride=2), :] = wide
            C0[:, pl.ds(1, 24, stride=2), :] = wide
            for k in range(5):
                U0b[2 + 2 * (i + k), 8:56, :] += C0[k]
                U0b[3 + 2 * (i + k), 8:56, :] += C0[k]

        over(0, 10, 5, widen0)

        def post0a(z):
            U0a[pl.ds(z, 3), 8:56, :] = sweep(0, U0b, S0, slot, D0, z, 3, 8, 48)

        over(3, 18, 3, post0a)

        def post0b(z):
            use(z, sweep(0, U0a, S0, slot, D0, z, 4, 16, 32))

        over(4, 16, 4, post0b)

    def centroid():
        sibling = (member + 1 - 2 * mc, slab)
        swap = remote(LB.at[pl.ds(8 * (1 - mc), 8)], XB, x_send, x_recv, sibling)
        swap.start()
        swap.wait()
        HB[...] = LB[pl.ds(8 * mc, 8)] + XB[...]
        pieces = []
        for d in range(1, 4):
            to = lax.rem(mx + d, 4)
            pieces.append(
                remote(HB.at[pl.ds(2 * to, 2)], PB.at[d - 1], p_send.at[d - 1], p_recv.at[d - 1], (2 * to + mc, slab))
            )
        begin(pieces)
        finish(pieces)
        total = HB[pl.ds(2 * mx, 2)] + PB[0] + PB[1] + PB[2]
        inverse = jnp.broadcast_to(IW[...][None, None], (2, 4, 8, LANES)).reshape(2, 32, LANES)
        own = 8 * mc + 2 * mx
        CB[pl.ds(own, 2)] = jnp.exp(total * inverse)
        spread, passed = [], []
        for d in range(1, 4):
            to = lax.rem(mx + d, 4)
            spread.append(
                remote(CB.at[pl.ds(own, 2)], CB.at[pl.ds(own, 2)], c_send.at[d - 1], c_recv.at[d - 1], (2 * to + mc, slab))
            )
        for d in range(4):
            at = 8 * mc + 2 * lax.rem(mx - d + 4, 4)
            passed.append(remote(CB.at[pl.ds(at, 2)], CB.at[pl.ds(at, 2)], f_send.at[d], f_recv.at[d], sibling))
        begin(spread)
        passed[0].start()
        for d in range(1, 4):
            spread[d - 1].wait_recv()
            passed[d].start()
        for c in spread:
            c.wait_send()
        finish(passed)

    def half_step(n, _):
        slot = lax.rem(n, 2)

        @pl.when(n > 0)
        def _():
            finish(halo(0, slot))

        def keep(z, h):
            MB[pl.ds(z - 4, 4)] = h

        vcycle(slot, keep)

        @pl.when(slot == 0)
        def _():
            def partner(z):
                S0[1, pl.ds(z, 4), 16:48, :] = VB[pl.ds(z - 4, 4)] / MB[pl.ds(z - 4, 4)]

            over(4, 16, 4, partner)

        @pl.when(slot == 1)
        def _():
            def marginal(z):
                m = S0[0, pl.ds(z, 4), 16:48, :] * MB[pl.ds(z - 4, 4)]
                MB[pl.ds(z - 4, 4)] = m
                LB[pl.ds(z - 4, 4)] = weight_ref[0] * jnp.log(m)

            over(4, 16, 4, marginal)
            centroid()

            def update(z):
                S0[0, pl.ds(z, 4), 16:48, :] = S0[0, pl.ds(z, 4), 16:48, :] * CB[pl.ds(z - 4, 4)] / MB[pl.ds(z - 4, 4)]

            over(4, 16, 4, update)

        @pl.when(n < 2 * ITERS - 1)
        def _():
            begin(halo(0, 1 - slot))

        return 0

    lax.fori_loop(0, 2 * ITERS, half_step, 0)

    moves = to_slabs(CB, 0, 0, cent_out, o_send.at[0], o_recv.at[0]) + to_slabs(
        S0.at[0], 4, 16, mult_out, o_send.at[1], o_recv.at[1]
    )
    begin(moves)
    mine = pl.ds(pl.multiple_of(32 * cy, 32), 32)
    cent_out[:, mine, :] = CB[pl.ds(4 * cy, 4)]
    mult_out[:, mine, :] = S0[0, pl.ds(4 + 4 * cy, 4), 16:48, :]
    finish(moves)


def body(nonnegative_volumes, reaction, diffusivity, member_weights):
    vmem, smem = pl.BlockSpec(memory_space=pltpu.VMEM), pl.BlockSpec(memory_space=pltpu.SMEM)
    field = jax.ShapeDtypeStruct((4, 128, 128), F32)

    def buffer(*shape):
        return pltpu.VMEM((*shape, LANES), F32)

    dma = pltpu.SemaphoreType.DMA
    scratch = [
        buffer(2, 24, 64), buffer(24, 64), buffer(16, 32), buffer(24, 64), buffer(24, 64), buffer(5, 48), buffer(8, 32),
        buffer(2, 18, 48), buffer(18, 48), buffer(8, 16), buffer(18, 48), buffer(18, 48), buffer(8, 32), buffer(4, 16),
        buffer(2, 16, 4, 8), buffer(4, 32), buffer(4, 32), buffer(4, 32), buffer(4, 48), buffer(2, 32), buffer(2, 32), buffer(16),
        buffer(16, 32), buffer(16, 32), buffer(16, 32), buffer(8, 32), buffer(8, 32), buffer(3, 2, 32), buffer(16, 32),
        buffer(8), buffer(8, 8), buffer(8),
        *[buffer(128) for _ in range(10)],
        dma((2, 8)), dma((2, 8)), dma((2, 8)), dma((2, 8)), dma((2, 16)), dma((2, 16)),
        dma((3,)), dma((3,)), dma((3,)), dma((3,)), dma((7,)), dma((7,)),
        dma, dma, dma((3,)), dma((3,)), dma((3,)), dma((3,)), dma((4,)), dma((4,)), dma((2, 3)), dma((2, 3)),
    ]
    centroid, multipliers = pl.pallas_call(
        kernel,
        out_shape=(field, field),
        in_specs=[vmem, vmem, smem, smem],
        out_specs=(vmem, vmem),
        scratch_shapes=scratch,
        compiler_params=pltpu.CompilerParams(collective_id=0, has_side_effects=True, vmem_limit_bytes=40 * 2**20),
    )(nonnegative_volumes[0], reaction, diffusivity, member_weights)
    return centroid, multipliers[None]


def solution(mesh):
    return jax.shard_map(
        body,
        mesh=mesh,
        in_specs=(P("member", "slab", None, None), P("slab", None, None), P(), P("member")),
        out_specs=(P("slab", None, None), P("member", "slab", None, None)),
        check_vma=False,
    )
```

```python
import jax
import jax.numpy as jnp
from jax import lax
from jax.experimental import pallas as pl
from jax.experimental.pallas import tpu as pltpu
from jax.sharding import PartitionSpec as P

ITERS = 3
COARSE_SWEEPS = 8
OMEGA = 0.8
LANES = 128
NZ, NY = 64, 128
F32 = jnp.float32
MESH = pl.DeviceIdType.MESH
DIRECTIONS = ((-1, 0), (1, 0), (0, -1), (0, 1), (-1, -1), (-1, 1), (1, -1), (1, 1))

GEOMETRY = (dict(own_z=4, own_y=16, nz=16, ny=32), dict(own_z=5, own_y=12, nz=8, ny=16))


def dot(a, b):
    return jnp.dot(a, b, precision=lax.Precision.HIGHEST, preferred_element_type=F32)


def flat(a):
    return a.reshape(-1, LANES)


def lane_roll(a, shift):
    return pltpu.roll(flat(a), shift % LANES, 1).reshape(a.shape)


def kernel(
    vol_ref, reaction_ref, diff_ref, weight_ref, cent_out, mult_out,
    S0, SC, D0, DG0, UA, UB, U0a, U0b, C0, T0,
    S1, S1C, D1, DG1, VA, VC, U1a, U1b, C1, T1, LZ, LY, LD,
    G, S2, D2, DG2, U2, T2, C2, D3,
    VB, MB, LB, XB, HB, PB, CB, WS, WB, IW,
    Rx, Rx1, R3, P3, E1, Px,
    h0_send, h0_recv, h1_send, h1_recv, g_send, g_recv,
    ra_send, ra_recv, va_send, va_recv, w_send, w_recv,
    x_send, x_recv, p_send, p_recv, c_send, c_recv, f_send, f_recv, o_send, o_recv,
):
    member, slab = lax.axis_index("member"), lax.axis_index("slab")
    cz, cy = slab // 4, lax.rem(slab, 4)
    mx, mc = member // 2, lax.rem(member, 2)

    def at_slab(dz, dy):
        return lax.rem(cz + dz + 4, 4) * 4 + lax.rem(cy + dy + 4, 4)

    def remote(src, dst, send, recv, to):
        return pltpu.make_async_remote_copy(
            src_ref=src, dst_ref=dst, send_sem=send, recv_sem=recv, device_id=to, device_id_type=MESH
        )

    for ref in (SC, UA, UB, VA, VC, S1C, U0a, U0b, U1a, U1b, U2, LZ, LY, LD, T1):
        ref[...] = jnp.zeros(ref.shape, F32)
    S0[...] = jnp.ones(S0.shape, F32)

    barrier = pltpu.get_barrier_semaphore()
    for d in range(1, 16):
        pl.semaphore_signal(barrier, inc=1, device_id=(member, at_slab(d // 4, d % 4)), device_id_type=MESH)
    for d in range(1, 8):
        pl.semaphore_signal(barrier, inc=1, device_id=(lax.rem(member + d, 8), slab), device_id_type=MESH)
    pl.semaphore_wait(barrier, 22)

    def inner(dz, dy):
        return (cz + dz >= 0) & (cz + dz < 4) & (cy + dy >= 0) & (cy + dy < 4)

    def halo0(slot):
        copies = []
        for k, (dz, dy) in enumerate(DIRECTIONS):
            zs, zn, zd = {-1: (4, 3, 20), 0: (4, 16, 4), 1: (17, 3, 1)}[dz]
            ys, yn, yd = {-1: (16, 8, 48), 0: (16, 32, 16), 1: (40, 8, 8)}[dy]
            copies.append((
                dz, dy,
                remote(
                    S0.at[slot, pl.ds(zs, zn), pl.ds(ys, yn)], S0.at[slot, pl.ds(zd, zn), pl.ds(yd, yn)],
                    h0_send.at[slot, k], h0_recv.at[slot, k], (member, at_slab(dz, dy)),
                ),
            ))
        return copies

    def landing1(k, slot):
        if k < 2:
            return LZ.at[slot, k]
        return LY.at[slot, k - 2] if k < 4 else LD.at[slot, k - 4]

    def halo1(slot):
        copies = []
        for k, (dz, dy) in enumerate(DIRECTIONS):
            z = {-1: pl.ds(4, 5), 0: pl.ds(4, 10), 1: pl.ds(9, 5)}[dz]
            y = {-1: pl.ds(8, 8), 0: pl.ds(8, 24), 1: pl.ds(24, 8)}[dy]
            copies.append((
                dz, dy,
                remote(
                    S1C.at[z, y], landing1(k, slot),
                    h1_send.at[slot, k], h1_recv.at[slot, k], (member, at_slab(dz, dy)),
                ),
            ))
        return copies

    def begin_near(copies):
        for dz, dy, c in copies:
            pl.when(inner(dz, dy))(c.start)

    def finish_near(copies):
        for dz, dy, c in copies:
            pl.when(inner(-dz, -dy))(c.wait_recv)
        for dz, dy, c in copies:
            pl.when(inner(dz, dy))(c.wait_send)

    def gather(slot):
        return [
            remote(
                G.at[slot, slab], G.at[slot, slab],
                g_send.at[slot, d], g_recv.at[slot, d], (member, at_slab(d // 4, d % 4)),
            )
            for d in range(1, 16)
        ]

    def begin(copies):
        for c in copies:
            c.start()

    def finish(copies):
        for c in copies:
            c.wait()

    def to_blocks(src, dst, dst_z, dst_y, send, recv):
        copies = []
        for d in range(1, 4):
            to = lax.rem(cy + d, 4)
            copies.append(
                remote(
                    src.at[:, pl.ds(pl.multiple_of(32 * to, 32), 32)],
                    dst.at[pl.ds(dst_z + 4 * cy, 4), pl.ds(dst_y, 32)],
                    send.at[d - 1], recv.at[d - 1], (member, cz * 4 + to),
                )
            )
        return copies

    def to_slabs(src, src_z, src_y, dst, send, recv):
        copies = []
        for d in range(1, 4):
            to = lax.rem(cy + d, 4)
            copies.append(
                remote(
                    src.at[pl.ds(src_z + 4 * to, 4), pl.ds(src_y, 32)],
                    dst.at[:, pl.ds(pl.multiple_of(32 * cy, 32), 32)],
                    send.at[d - 1], recv.at[d - 1], (member, cz * 4 + to),
                )
            )
        return copies

    reaction_moves = to_blocks(reaction_ref, S0.at[1], 4, 16, ra_send, ra_recv)
    volume_moves = to_blocks(vol_ref, VB, 0, 0, va_send, va_recv)
    begin(reaction_moves)
    begin(volume_moves)
    WS[...] = jnp.full((8, LANES), weight_ref[0], F32)
    weight_moves = [
        remote(WS, WB.at[d], w_send.at[d - 1], w_recv.at[d - 1], (lax.rem(member + d, 8), slab)) for d in range(1, 8)
    ]
    begin(weight_moves)

    coupling = [[diff_ref[i] * (0.25**level) for i in range(3)] for level in range(4)]
    center = [2.0 * (c[0] + c[1] + c[2]) for c in coupling]

    lane = lax.broadcasted_iota(jnp.int32, (1, LANES), 1)
    one, zero = jnp.ones((1, LANES), F32), jnp.zeros((1, LANES), F32)

    def lane_mask(keep):
        return jnp.where(keep, one, zero)

    row_i = lax.broadcasted_iota(jnp.int32, (LANES, LANES), 0)
    col_i = lax.broadcasted_iota(jnp.int32, (LANES, LANES), 1)

    def half(a):
        return lax.shift_right_logical(a, 1)

    def matrix(keep, value=1.0):
        return jnp.where(keep, jnp.full((LANES, LANES), value, F32), jnp.zeros((LANES, LANES), F32))

    Rx[...] = matrix(half(row_i) == col_i, 0.125)
    Px[...] = matrix(row_i == half(col_i))
    for q in range(4):
        block = slice(LANES * q, LANES * q + LANES)
        Rx1[block, :] = matrix((row_i < 64) & (half(row_i) + 32 * q == col_i), 0.125)
        E1[:, block] = matrix((col_i < 64) & (row_i == half(col_i) + 32 * q))
        R3[block, :] = matrix(16 * (2 * q + lax.shift_right_logical(row_i, 6)) + half(row_i & 31) == col_i, 0.125)
        P3[:, block] = matrix(16 * (2 * q + lax.shift_right_logical(col_i, 6)) + half(col_i & 31) == row_i)

    left = [lane_mask(lane > 0) * coupling[0][2], None, lane_mask((lane & 31) > 0) * coupling[2][2], lane_mask((lane & 15) > 0) * coupling[3][2]]
    right = [lane_mask(lane < 127) * coupling[0][2], None, lane_mask((lane & 31) < 31) * coupling[2][2], lane_mask((lane & 15) < 15) * coupling[3][2]]

    def neighbours(level, u, z, n, lo, rows):
        c = coupling[level]
        mid = u[pl.ds(z, n), lo : lo + rows, :]
        total = c[0] * (u[pl.ds(z - 1, n), lo : lo + rows, :] + u[pl.ds(z + 1, n), lo : lo + rows, :])
        total += c[1] * (u[pl.ds(z, n), lo - 1 : lo + rows - 1, :] + u[pl.ds(z, n), lo + 1 : lo + rows + 1, :])
        if level == 0:
            total += left[0] * lane_roll(mid, 1) + right[0] * lane_roll(mid, -1)
        else:
            total += c[2] * (lane_roll(mid, 1) + lane_roll(mid, -1))
        return mid, total

    def over(z0, count, step, body):
        def one_step(i, _):
            body(z0 + i * step)
            return 0

        lax.fori_loop(0, count // step, one_step, 0)

    def sweep(level, u, s, d, z, n, lo, rows):
        mid, total = neighbours(level, u, z, n, lo, rows)
        return (1.0 - OMEGA) * mid + d[pl.ds(z, n), lo : lo + rows, :] * (s[pl.ds(z, n), lo : lo + rows, :] + total)

    def residual(level, u, s, dg, z, n, lo, rows):
        mid, total = neighbours(level, u, z, n, lo, rows)
        return s[pl.ds(z, n), lo : lo + rows, :] - dg[pl.ds(z, n), lo : lo + rows, :] * mid + total

    def restrict0(fine):
        def body(z):
            a = fine(z)
            for k in range(2):
                T0[(z - 2) // 2 + k] = a[2 * k] + a[2 * k + 1]

        over(2, 20, 4, body)

        def rows(i):
            e = T0[pl.ds(i, 5), pl.ds(0, 24, stride=2), :] + T0[pl.ds(i, 5), pl.ds(1, 24, stride=2), :]
            S1C[pl.ds(4 + i, 5), 8:32, :] = dot(flat(e), Rx[...]).reshape(5, 24, LANES)

        over(0, 10, 5, rows)

    def restrict1(fine, slot):
        def body(z):
            a = fine(z)
            for k in range(4):
                T1[(z - 1) // 2 + k, 4:28, :] = a[2 * k] + a[2 * k + 1]

        over(1, 16, 8, body)
        e = T1[:, pl.ds(0, 16, stride=2), :] + T1[:, pl.ds(1, 16, stride=2), :]
        own = jnp.concatenate([e[2], e[3], e[4], e[5]], axis=1)
        sides = jnp.concatenate([e[6], e[7], e[0], e[1]], axis=1)
        m = dot(jnp.concatenate([own, sides], axis=0), Rx1[...]).reshape(2, 16, LANES)
        G[slot, slab, :, 0:8, :] = m[:, 4:12]
        G[slot, slab, :, 8:12, :] = m[:, 12:16]
        G[slot, slab, :, 12:16, :] = m[:, 0:4]

    upper_half, upper_rows = lane >= 64, lax.broadcasted_iota(jnp.int32, (8, LANES), 0) < 4
    nothing = jnp.zeros((8, LANES), F32)

    def gathered(slot):
        def rows(c, j, g):
            below = G[slot, 4 * c + j - 1, g, 8:16, :] if j > 0 else nothing
            above = G[slot, 4 * c + j + 1, g, 8:16, :] if j < 3 else nothing
            return G[slot, 4 * c + j, g, 0:8, :] + jnp.where(upper_rows, below, above)

        for j in range(4):
            side = [nothing] + [rows(c, j, 1) for c in range(4)] + [nothing]
            for c in range(4):
                S2[c, 8 * j : 8 * j + 8, :] = rows(c, j, 0) + jnp.where(upper_half, side[c + 2], side[c])

    def restrict2(a):
        T2[...] = a
        e = T2[:, pl.ds(0, 16, stride=2), :] + T2[:, pl.ds(1, 16, stride=2), :]
        return dot(jnp.concatenate([e[0], e[1], e[2], e[3]], axis=1), R3[...])

    first_chunk, last_chunk = lane < 32, lane >= 96
    plane2 = jnp.zeros((1, 32, LANES), F32)

    def neighbours2():
        c = coupling[2]
        mid = U2[1:5, 8:40, :]
        up, down = lane_roll(mid, 32), lane_roll(mid, -32)
        before = jnp.where(first_chunk, jnp.concatenate([plane2, up[:3]], axis=0), up)
        after = jnp.where(last_chunk, jnp.concatenate([down[1:], plane2], axis=0), down)
        total = c[0] * (before + after) + c[1] * (U2[1:5, 7:39, :] + U2[1:5, 9:41, :])
        total += left[2] * lane_roll(mid, 1) + right[2] * lane_roll(mid, -1)
        return mid, total

    def sweep2():
        mid, total = neighbours2()
        U2[1:5, 8:40, :] = (1.0 - OMEGA) * mid + D2[...] * (S2[...] + total)

    row16 = lax.broadcasted_iota(jnp.int32, (16, LANES), 0)
    zeros16, ones16 = jnp.zeros((16, LANES), F32), jnp.ones((16, LANES), F32)
    up3 = jnp.where(row16 > 0, ones16, zeros16) * coupling[3][1]
    down3 = jnp.where(row16 < 15, ones16, zeros16) * coupling[3][1]
    before3 = lane_mask(lane >= 16) * coupling[3][0]
    after3 = lane_mask(lane < 112) * coupling[3][0]

    def level3(s):
        d = D3[...]
        u = d * s
        for _ in range(COARSE_SWEEPS - 1):
            total = before3 * lane_roll(u, 16) + after3 * lane_roll(u, -16)
            total += up3 * pltpu.roll(u, 1, 0) + down3 * pltpu.roll(u, 15, 0)
            total += left[3] * lane_roll(u, 1) + right[3] * lane_roll(u, -1)
            u = (1.0 - OMEGA) * u + d * (s + total)
        return u

    def inside(level, z, n, lo, rows):
        g = GEOMETRY[level]
        zi = lax.broadcasted_iota(jnp.int32, (n, rows, LANES), 0) + (z - g["own_z"] + g["nz"] * cz)
        yi = lax.broadcasted_iota(jnp.int32, (n, rows, LANES), 1) + (lo - g["own_y"] + g["ny"] * cy)
        keep = (zi >= 0) & (zi < 4 * g["nz"]) & (yi >= 0) & (yi < 4 * g["ny"])
        if level:
            keep = keep & (lax.broadcasted_iota(jnp.int32, (n, rows, LANES), 2) < 64)
        return keep

    finish(reaction_moves)
    mine = pl.ds(pl.multiple_of(32 * cy, 32), 32)
    S0[1, pl.ds(4 + 4 * cy, 4), 16:48, :] = reaction_ref[:, mine, :]
    begin_near(halo0(1))
    SC[4:20, 16:48, :] = S0[1, 4:20, 16:48, :]
    restrict0(lambda z: SC[pl.ds(z, 4), 8:56, :])
    restrict1(lambda z: S1C[pl.ds(z, 8), 8:32, :], 1)
    begin(gather(1))
    begin_near(halo1(1))
    VB[pl.ds(4 * cy, 4)] = vol_ref[:, mine, :]

    def summed1(slot):
        finish_near(halo1(slot))
        S1[1:17, 8:32, :] = S1C[1:17, 8:32, :]
        for k, (dz, dy) in enumerate(DIRECTIONS):
            z = {-1: slice(12, 17), 0: slice(4, 14), 1: slice(1, 6)}[dz]
            y = {-1: slice(24, 32), 0: slice(8, 32), 1: slice(8, 16)}[dy]
            S1[z, y, :] += landing1(k, slot)[...]

    finish_near(halo0(1))

    def diag0(z):
        diag = S0[1, pl.ds(z, 2), 8:56, :] + center[0]
        DG0[pl.ds(z, 2), 8:56, :] = diag
        D0[pl.ds(z, 2), 8:56, :] = jnp.where(inside(0, z, 2, 8, 48), OMEGA / diag, jnp.zeros((2, 48, LANES), F32))

    over(1, 22, 2, diag0)
    summed1(1)

    def diag1(z):
        diag = S1[pl.ds(z, 2), 8:32, :] + center[1]
        DG1[pl.ds(z, 2), 8:32, :] = diag
        D1[pl.ds(z, 2), 8:32, :] = jnp.where(inside(1, z, 2, 8, 24), OMEGA / diag, jnp.zeros((2, 24, LANES), F32))

    over(1, 16, 2, diag1)
    finish(gather(1))
    gathered(1)
    DG2[...] = S2[...] + center[2]
    D2[...] = OMEGA / DG2[...]
    D3[...] = OMEGA / (restrict2(S2[...]) + center[3])
    SC[4:20, 16:48, :] = jnp.ones((16, 32, LANES), F32)
    finish(volume_moves)
    finish(weight_moves)
    weight_total = WS[...]
    for d in range(1, 8):
        weight_total += WB[d]
    IW[...] = 1.0 / weight_total

    def vcycle(n, slot, use):
        UA[4:20, 16:48, :] = D0[4:20, 16:48, :] * SC[4:20, 16:48, :]

        def own0(z):
            UB[pl.ds(z, 3), 8:56, :] = sweep(0, UA, SC, D0, z, 3, 8, 48)

        over(3, 18, 3, own0)
        restrict0(lambda z: residual(0, UB, SC, DG0, z, 4, 8, 48))
        VA[4:14, 8:32, :] = D1[4:14, 8:32, :] * S1C[4:14, 8:32, :]

        def own1(z):
            VC[pl.ds(z, 6), 8:32, :] = sweep(1, VA, S1C, D1, z, 6, 8, 24)

        over(3, 12, 6, own1)
        restrict1(lambda z: residual(1, VC, S1C, DG1, z, 8, 8, 24), slot)
        begin(gather(slot))
        begin_near(halo1(slot))

        @pl.when(n > 0)
        def _():
            finish_near(halo0(slot))

        source0 = S0.at[slot]

        def first0(z):
            U0a[pl.ds(z, 2), 8:56, :] = D0[pl.ds(z, 2), 8:56, :] * source0[pl.ds(z, 2), 8:56, :]

        over(1, 22, 2, first0)

        def pre0(z):
            U0b[pl.ds(z, 4), 8:56, :] = sweep(0, U0a, source0, D0, z, 4, 8, 48)

        over(2, 20, 4, pre0)
        summed1(slot)
        U1a[1:17, 8:32, :] = D1[1:17, 8:32, :] * S1[1:17, 8:32, :]

        def pre1(z):
            U1b[pl.ds(z, 7), 8:32, :] = sweep(1, U1a, S1, D1, z, 7, 8, 24)

        over(2, 14, 7, pre1)

        finish(gather(slot))
        gathered(slot)
        U2[1:5, 8:40, :] = D2[...] * S2[...]
        sweep2()
        mid, total = neighbours2()
        u3 = level3(restrict2(S2[...] - DG2[...] * mid + total))
        p = dot(u3, P3[...])
        for k in range(4):
            C2[k, pl.ds(0, 16, stride=2), :] = p[:, LANES * k : LANES * k + LANES]
            C2[k, pl.ds(1, 16, stride=2), :] = p[:, LANES * k : LANES * k + LANES]
        U2[1:5, 8:40, :] += C2[...]
        sweep2()
        sweep2()

        window = pl.ds(pl.multiple_of(8 * cy, 8), 24)
        own = U2[1 + cz, window, :][4:20]
        sides = jnp.where(upper_half, U2[cz, window, :][4:20], U2[2 + cz, window, :][4:20])
        wide = dot(jnp.concatenate([own, sides], axis=0), E1[...])
        for k in range(8):
            r, q = (0, k - 2) if 2 <= k < 6 else (16, (k - 2) % 4)
            C1[k, pl.ds(0, 16, stride=2), :] = wide[r : r + 16, LANES * q : LANES * q + LANES]
            C1[k, pl.ds(1, 16, stride=2), :] = wide[r : r + 16, LANES * q : LANES * q + LANES]
        for k in range(8):
            U1b[1 + 2 * k, 8:32, :] += C1[k, 4:28, :]
            U1b[2 + 2 * k, 8:32, :] += C1[k, 4:28, :]

        def post1a(z):
            U1a[pl.ds(z, 6), 8:32, :] = sweep(1, U1b, S1, D1, z, 6, 8, 24)

        over(3, 12, 6, post1a)

        def post1b(z):
            U1b[pl.ds(z, 5), 8:32, :] = sweep(1, U1a, S1, D1, z, 5, 8, 24)

        over(4, 10, 5, post1b)

        def widen0(i):
            wide = dot(flat(U1b[pl.ds(4 + i, 5), 8:32, :]), Px[...]).reshape(5, 24, LANES)
            C0[:, pl.ds(0, 24, stride=2), :] = wide
            C0[:, pl.ds(1, 24, stride=2), :] = wide
            for k in range(5):
                U0b[2 + 2 * (i + k), 8:56, :] += C0[k]
                U0b[3 + 2 * (i + k), 8:56, :] += C0[k]

        over(0, 10, 5, widen0)

        def post0a(z):
            U0a[pl.ds(z, 3), 8:56, :] = sweep(0, U0b, source0, D0, z, 3, 8, 48)

        over(3, 18, 3, post0a)

        def post0b(z):
            use(z, sweep(0, U0a, source0, D0, z, 4, 16, 32))

        over(4, 16, 4, post0b)

    def centroid():
        sibling = (member + 1 - 2 * mc, slab)
        swap = remote(LB.at[pl.ds(8 * (1 - mc), 8)], XB, x_send, x_recv, sibling)
        swap.start()
        swap.wait()
        HB[...] = LB[pl.ds(8 * mc, 8)] + XB[...]
        pieces = []
        for d in range(1, 4):
            to = lax.rem(mx + d, 4)
            pieces.append(
                remote(HB.at[pl.ds(2 * to, 2)], PB.at[d - 1], p_send.at[d - 1], p_recv.at[d - 1], (2 * to + mc, slab))
            )
        begin(pieces)
        finish(pieces)
        total = HB[pl.ds(2 * mx, 2)] + PB[0] + PB[1] + PB[2]
        inverse = jnp.broadcast_to(IW[...][None, None], (2, 4, 8, LANES)).reshape(2, 32, LANES)
        own = 8 * mc + 2 * mx
        CB[pl.ds(own, 2)] = jnp.exp(total * inverse)
        spread, passed = [], []
        for d in range(1, 4):
            to = lax.rem(mx + d, 4)
            spread.append(
                remote(CB.at[pl.ds(own, 2)], CB.at[pl.ds(own, 2)], c_send.at[d - 1], c_recv.at[d - 1], (2 * to + mc, slab))
            )
        for d in range(4):
            at = 8 * mc + 2 * lax.rem(mx - d + 4, 4)
            passed.append(remote(CB.at[pl.ds(at, 2)], CB.at[pl.ds(at, 2)], f_send.at[d], f_recv.at[d], sibling))
        begin(spread)
        passed[0].start()
        for d in range(1, 4):
            spread[d - 1].wait_recv()
            passed[d].start()
        for c in spread:
            c.wait_send()
        finish(passed)

    def half_step(n, _):
        slot = lax.rem(n, 2)

        def keep(z, h):
            MB[pl.ds(z - 4, 4)] = h

        vcycle(n, slot, keep)

        @pl.when(slot == 0)
        def _():
            def partner(z):
                p = VB[pl.ds(z - 4, 4)] / MB[pl.ds(z - 4, 4)]
                S0[1, pl.ds(z, 4), 16:48, :] = p
                SC[pl.ds(z, 4), 16:48, :] = p

            over(4, 16, 4, partner)

        @pl.when(slot == 1)
        def _():
            def marginal(z):
                m = S0[0, pl.ds(z, 4), 16:48, :] * MB[pl.ds(z - 4, 4)]
                MB[pl.ds(z - 4, 4)] = m
                LB[pl.ds(z - 4, 4)] = weight_ref[0] * jnp.log(m)

            over(4, 16, 4, marginal)
            centroid()

            def update(z):
                p = S0[0, pl.ds(z, 4), 16:48, :] * CB[pl.ds(z - 4, 4)] / MB[pl.ds(z - 4, 4)]
                S0[0, pl.ds(z, 4), 16:48, :] = p
                SC[pl.ds(z, 4), 16:48, :] = p

            over(4, 16, 4, update)

        @pl.when(n < 2 * ITERS - 1)
        def _():
            begin_near(halo0(1 - slot))

        return 0

    lax.fori_loop(0, 2 * ITERS, half_step, 0)

    moves = to_slabs(CB, 0, 0, cent_out, o_send.at[0], o_recv.at[0]) + to_slabs(
        S0.at[0], 4, 16, mult_out, o_send.at[1], o_recv.at[1]
    )
    begin(moves)
    cent_out[:, mine, :] = CB[pl.ds(4 * cy, 4)]
    mult_out[:, mine, :] = S0[0, pl.ds(4 + 4 * cy, 4), 16:48, :]
    finish(moves)


def body(nonnegative_volumes, reaction, diffusivity, member_weights):
    vmem, smem = pl.BlockSpec(memory_space=pltpu.VMEM), pl.BlockSpec(memory_space=pltpu.SMEM)
    field = jax.ShapeDtypeStruct((4, 128, 128), F32)

    def buffer(*shape):
        return pltpu.VMEM((*shape, LANES), F32)

    dma = pltpu.SemaphoreType.DMA
    scratch = [
        buffer(2, 24, 64), *[buffer(24, 64) for _ in range(7)], buffer(5, 48), buffer(10, 48),
        *[buffer(18, 40) for _ in range(8)], buffer(8, 32), buffer(8, 32), buffer(2, 2, 5, 24), buffer(2, 2, 10, 8), buffer(2, 4, 5, 8),
        buffer(2, 16, 2, 16), buffer(4, 32), buffer(4, 32), buffer(4, 32), buffer(6, 48), buffer(4, 32), buffer(4, 32), buffer(16),
        buffer(16, 32), buffer(16, 32), buffer(16, 32), buffer(8, 32), buffer(8, 32), buffer(3, 2, 32), buffer(16, 32),
        buffer(8), buffer(8, 8), buffer(8),
        buffer(128), buffer(512), buffer(512), pltpu.VMEM((128, 512), F32), pltpu.VMEM((128, 512), F32), buffer(128),
        dma((2, 8)), dma((2, 8)), dma((2, 8)), dma((2, 8)), dma((2, 16)), dma((2, 16)),
        dma((3,)), dma((3,)), dma((3,)), dma((3,)), dma((7,)), dma((7,)),
        dma, dma, dma((3,)), dma((3,)), dma((3,)), dma((3,)), dma((4,)), dma((4,)), dma((2, 3)), dma((2, 3)),
    ]
    centroid, multipliers = pl.pallas_call(
        kernel,
        out_shape=(field, field),
        in_specs=[vmem, vmem, smem, smem],
        out_specs=(vmem, vmem),
        scratch_shapes=scratch,
        compiler_params=pltpu.CompilerParams(collective_id=0, has_side_effects=True, vmem_limit_bytes=40 * 2**20),
    )(nonnegative_volumes[0], reaction, diffusivity, member_weights)
    return centroid, multipliers[None]


def solution(mesh):
    return jax.shard_map(
        body,
        mesh=mesh,
        in_specs=(P("member", "slab", None, None), P("slab", None, None), P(), P("member")),
        out_specs=(P("slab", None, None), P("member", "slab", None, None)),
        check_vma=False,
    )
```

```python
import jax
import jax.numpy as jnp
from jax import lax
from jax.experimental import pallas as pl
from jax.experimental.pallas import tpu as pltpu
from jax.sharding import PartitionSpec as P

ITERS = 3
COARSE_SWEEPS = 8
OMEGA = 0.8
LANES = 128
NZ, NY = 64, 128
F32 = jnp.float32
MESH = pl.DeviceIdType.MESH
DIRECTIONS = ((-1, 0), (1, 0), (0, -1), (0, 1), (-1, -1), (-1, 1), (1, -1), (1, 1))

GEOMETRY = (dict(own_z=4, own_y=16, nz=16, ny=32), dict(own_z=5, own_y=12, nz=8, ny=16))


def dot(a, b):
    return jnp.dot(a, b, precision=lax.Precision.HIGHEST, preferred_element_type=F32)


def flat(a):
    return a.reshape(-1, LANES)


def lane_roll(a, shift):
    return pltpu.roll(flat(a), shift % LANES, 1).reshape(a.shape)


def kernel(
    vol_ref, reaction_ref, diff_ref, weight_ref, cent_out, mult_out,
    S0, SC, D0, DG0, UA, UB, U0a, U0b, C0, T0,
    S1, S1C, D1, DG1, VA, VC, U1a, U1b, C1, T1, LZ, LY, LD,
    G, S2, D2, DG2, U2, T2, C2, D3,
    VB, MB, LB, XB, HB, PB, CB, WS, WB, IW,
    Rx, Rx1, R3, P3, E1, Px,
    h0_send, h0_recv, h1_send, h1_recv, g_send, g_recv,
    ra_send, ra_recv, va_send, va_recv, w_send, w_recv,
    x_send, x_recv, p_send, p_recv, c_send, c_recv, f_send, f_recv, o_send, o_recv,
):
    member, slab = lax.axis_index("member"), lax.axis_index("slab")
    cz, cy = slab // 4, lax.rem(slab, 4)
    mx, mc = member // 2, lax.rem(member, 2)

    def at_slab(dz, dy):
        return lax.rem(cz + dz + 4, 4) * 4 + lax.rem(cy + dy + 4, 4)

    def remote(src, dst, send, recv, to):
        return pltpu.make_async_remote_copy(
            src_ref=src, dst_ref=dst, send_sem=send, recv_sem=recv, device_id=to, device_id_type=MESH
        )

    for ref in (SC, UA, UB, VA, VC, S1C, U0a, U0b, U1a, U1b, U2, LZ, LY, LD, T1):
        ref[...] = jnp.zeros(ref.shape, F32)
    S0[...] = jnp.ones(S0.shape, F32)

    barrier = pltpu.get_barrier_semaphore()
    for d in range(1, 16):
        pl.semaphore_signal(barrier, inc=1, device_id=(member, at_slab(d // 4, d % 4)), device_id_type=MESH)
    for d in range(1, 8):
        pl.semaphore_signal(barrier, inc=1, device_id=(lax.rem(member + d, 8), slab), device_id_type=MESH)
    pl.semaphore_wait(barrier, 22)

    def inner(dz, dy):
        return (cz + dz >= 0) & (cz + dz < 4) & (cy + dy >= 0) & (cy + dy < 4)

    def halo0(slot):
        copies = []
        for k, (dz, dy) in enumerate(DIRECTIONS):
            zs, zn, zd = {-1: (4, 3, 20), 0: (4, 16, 4), 1: (17, 3, 1)}[dz]
            ys, yn, yd = {-1: (16, 8, 48), 0: (16, 32, 16), 1: (40, 8, 8)}[dy]
            copies.append((
                dz, dy,
                remote(
                    S0.at[slot, pl.ds(zs, zn), pl.ds(ys, yn)], S0.at[slot, pl.ds(zd, zn), pl.ds(yd, yn)],
                    h0_send.at[slot, k], h0_recv.at[slot, k], (member, at_slab(dz, dy)),
                ),
            ))
        return copies

    def landing1(k, slot):
        if k < 2:
            return LZ.at[slot, k]
        return LY.at[slot, k - 2] if k < 4 else LD.at[slot, k - 4]

    def halo1(slot):
        copies = []
        for k, (dz, dy) in enumerate(DIRECTIONS):
            z = {-1: pl.ds(4, 5), 0: pl.ds(4, 10), 1: pl.ds(9, 5)}[dz]
            y = {-1: pl.ds(8, 8), 0: pl.ds(8, 24), 1: pl.ds(24, 8)}[dy]
            copies.append((
                dz, dy,
                remote(
                    S1C.at[z, y], landing1(k, slot),
                    h1_send.at[slot, k], h1_recv.at[slot, k], (member, at_slab(dz, dy)),
                ),
            ))
        return copies

    def begin_near(copies):
        for dz, dy, c in copies:
            pl.when(inner(dz, dy))(c.start)

    def finish_near(copies):
        for dz, dy, c in copies:
            pl.when(inner(-dz, -dy))(c.wait_recv)
        for dz, dy, c in copies:
            pl.when(inner(dz, dy))(c.wait_send)

    def gather(slot):
        return [
            remote(
                G.at[slot, slab], G.at[slot, slab],
                g_send.at[slot, d], g_recv.at[slot, d], (member, at_slab(d // 4, d % 4)),
            )
            for d in range(1, 16)
        ]

    def begin(copies):
        for c in copies:
            c.start()

    def finish(copies):
        for c in copies:
            c.wait()

    def to_blocks(src, dst, dst_z, dst_y, send, recv):
        copies = []
        for d in range(1, 4):
            to = lax.rem(cy + d, 4)
            copies.append(
                remote(
                    src.at[:, pl.ds(pl.multiple_of(32 * to, 32), 32)],
                    dst.at[pl.ds(dst_z + 4 * cy, 4), pl.ds(dst_y, 32)],
                    send.at[d - 1], recv.at[d - 1], (member, cz * 4 + to),
                )
            )
        return copies

    def to_slabs(src, src_z, src_y, dst, send, recv):
        copies = []
        for d in range(1, 4):
            to = lax.rem(cy + d, 4)
            copies.append(
                remote(
                    src.at[pl.ds(src_z + 4 * to, 4), pl.ds(src_y, 32)],
                    dst.at[:, pl.ds(pl.multiple_of(32 * cy, 32), 32)],
                    send.at[d - 1], recv.at[d - 1], (member, cz * 4 + to),
                )
            )
        return copies

    reaction_moves = to_blocks(reaction_ref, S0.at[1], 4, 16, ra_send, ra_recv)
    volume_moves = to_blocks(vol_ref, VB, 0, 0, va_send, va_recv)
    begin(reaction_moves)
    begin(volume_moves)
    WS[...] = jnp.full((8, LANES), weight_ref[0], F32)
    weight_moves = [
        remote(WS, WB.at[d], w_send.at[d - 1], w_recv.at[d - 1], (lax.rem(member + d, 8), slab)) for d in range(1, 8)
    ]
    begin(weight_moves)

    coupling = [[diff_ref[i] * (0.25**level) for i in range(3)] for level in range(4)]
    center = [2.0 * (c[0] + c[1] + c[2]) for c in coupling]

    lane = lax.broadcasted_iota(jnp.int32, (1, LANES), 1)
    one, zero = jnp.ones((1, LANES), F32), jnp.zeros((1, LANES), F32)

    def lane_mask(keep):
        return jnp.where(keep, one, zero)

    row_i = lax.broadcasted_iota(jnp.int32, (LANES, LANES), 0)
    col_i = lax.broadcasted_iota(jnp.int32, (LANES, LANES), 1)

    def half(a):
        return lax.shift_right_logical(a, 1)

    def matrix(keep, value=1.0):
        return jnp.where(keep, jnp.full((LANES, LANES), value, F32), jnp.zeros((LANES, LANES), F32))

    Rx[...] = matrix(half(row_i) == col_i, 0.125)
    Px[...] = matrix(row_i == half(col_i))
    for q in range(4):
        block = slice(LANES * q, LANES * q + LANES)
        Rx1[block, :] = matrix((row_i < 64) & (half(row_i) + 32 * q == col_i), 0.125)
        E1[:, block] = matrix((col_i < 64) & (row_i == half(col_i) + 32 * q))
        R3[block, :] = matrix(16 * (2 * q + lax.shift_right_logical(row_i, 6)) + half(row_i & 31) == col_i, 0.125)
        P3[:, block] = matrix(16 * (2 * q + lax.shift_right_logical(col_i, 6)) + half(col_i & 31) == row_i)

    left = [lane_mask(lane > 0) * coupling[0][2], None, lane_mask((lane & 31) > 0) * coupling[2][2], lane_mask((lane & 15) > 0) * coupling[3][2]]
    right = [lane_mask(lane < 127) * coupling[0][2], None, lane_mask((lane & 31) < 31) * coupling[2][2], lane_mask((lane & 15) < 15) * coupling[3][2]]

    def neighbours(level, u, z, n, lo, rows):
        c = coupling[level]
        mid = u[pl.ds(z, n), lo : lo + rows, :]
        total = c[0] * (u[pl.ds(z - 1, n), lo : lo + rows, :] + u[pl.ds(z + 1, n), lo : lo + rows, :])
        total += c[1] * (u[pl.ds(z, n), lo - 1 : lo + rows - 1, :] + u[pl.ds(z, n), lo + 1 : lo + rows + 1, :])
        if level == 0:
            total += left[0] * lane_roll(mid, 1) + right[0] * lane_roll(mid, -1)
        else:
            total += c[2] * (lane_roll(mid, 1) + lane_roll(mid, -1))
        return mid, total

    def over(z0, count, step, body):
        for z in range(z0, z0 + count, step):
            body(z)

    def sweep(level, u, s, d, z, n, lo, rows):
        mid, total = neighbours(level, u, z, n, lo, rows)
        return (1.0 - OMEGA) * mid + d[pl.ds(z, n), lo : lo + rows, :] * (s[pl.ds(z, n), lo : lo + rows, :] + total)

    def residual(level, u, s, dg, z, n, lo, rows):
        mid, total = neighbours(level, u, z, n, lo, rows)
        return s[pl.ds(z, n), lo : lo + rows, :] - dg[pl.ds(z, n), lo : lo + rows, :] * mid + total

    def restrict0(fine):
        def body(z):
            a = fine(z)
            for k in range(2):
                T0[(z - 2) // 2 + k] = a[2 * k] + a[2 * k + 1]

        over(2, 20, 4, body)

        def rows(i):
            e = T0[pl.ds(i, 5), pl.ds(0, 24, stride=2), :] + T0[pl.ds(i, 5), pl.ds(1, 24, stride=2), :]
            S1C[pl.ds(4 + i, 5), 8:32, :] = dot(flat(e), Rx[...]).reshape(5, 24, LANES)

        over(0, 10, 5, rows)

    def restrict1(fine, slot):
        def body(z):
            a = fine(z)
            for k in range(4):
                T1[(z - 1) // 2 + k, 4:28, :] = a[2 * k] + a[2 * k + 1]

        over(1, 16, 8, body)
        e = T1[:, pl.ds(0, 16, stride=2), :] + T1[:, pl.ds(1, 16, stride=2), :]
        own = jnp.concatenate([e[2], e[3], e[4], e[5]], axis=1)
        sides = jnp.concatenate([e[6], e[7], e[0], e[1]], axis=1)
        m = dot(jnp.concatenate([own, sides], axis=0), Rx1[...]).reshape(2, 16, LANES)
        G[slot, slab, :, 0:8, :] = m[:, 4:12]
        G[slot, slab, :, 8:12, :] = m[:, 12:16]
        G[slot, slab, :, 12:16, :] = m[:, 0:4]

    upper_half, upper_rows = lane >= 64, lax.broadcasted_iota(jnp.int32, (8, LANES), 0) < 4
    nothing = jnp.zeros((8, LANES), F32)

    def gathered(slot):
        def rows(c, j, g):
            below = G[slot, 4 * c + j - 1, g, 8:16, :] if j > 0 else nothing
            above = G[slot, 4 * c + j + 1, g, 8:16, :] if j < 3 else nothing
            return G[slot, 4 * c + j, g, 0:8, :] + jnp.where(upper_rows, below, above)

        for j in range(4):
            side = [nothing] + [rows(c, j, 1) for c in range(4)] + [nothing]
            for c in range(4):
                S2[c, 8 * j : 8 * j + 8, :] = rows(c, j, 0) + jnp.where(upper_half, side[c + 2], side[c])

    def restrict2(a):
        T2[...] = a
        e = T2[:, pl.ds(0, 16, stride=2), :] + T2[:, pl.ds(1, 16, stride=2), :]
        return dot(jnp.concatenate([e[0], e[1], e[2], e[3]], axis=1), R3[...])

    first_chunk, last_chunk = lane < 32, lane >= 96
    plane2 = jnp.zeros((1, 32, LANES), F32)

    def neighbours2():
        c = coupling[2]
        mid = U2[1:5, 8:40, :]
        up, down = lane_roll(mid, 32), lane_roll(mid, -32)
        before = jnp.where(first_chunk, jnp.concatenate([plane2, up[:3]], axis=0), up)
        after = jnp.where(last_chunk, jnp.concatenate([down[1:], plane2], axis=0), down)
        total = c[0] * (before + after) + c[1] * (U2[1:5, 7:39, :] + U2[1:5, 9:41, :])
        total += left[2] * lane_roll(mid, 1) + right[2] * lane_roll(mid, -1)
        return mid, total

    def sweep2():
        mid, total = neighbours2()
        U2[1:5, 8:40, :] = (1.0 - OMEGA) * mid + D2[...] * (S2[...] + total)

    row16 = lax.broadcasted_iota(jnp.int32, (16, LANES), 0)
    zeros16, ones16 = jnp.zeros((16, LANES), F32), jnp.ones((16, LANES), F32)
    up3 = jnp.where(row16 > 0, ones16, zeros16) * coupling[3][1]
    down3 = jnp.where(row16 < 15, ones16, zeros16) * coupling[3][1]
    before3 = lane_mask(lane >= 16) * coupling[3][0]
    after3 = lane_mask(lane < 112) * coupling[3][0]

    def level3(s):
        d = D3[...]
        u = d * s
        for _ in range(COARSE_SWEEPS - 1):
            total = before3 * lane_roll(u, 16) + after3 * lane_roll(u, -16)
            total += up3 * pltpu.roll(u, 1, 0) + down3 * pltpu.roll(u, 15, 0)
            total += left[3] * lane_roll(u, 1) + right[3] * lane_roll(u, -1)
            u = (1.0 - OMEGA) * u + d * (s + total)
        return u

    def inside(level, z, n, lo, rows):
        g = GEOMETRY[level]
        zi = lax.broadcasted_iota(jnp.int32, (n, rows, LANES), 0) + (z - g["own_z"] + g["nz"] * cz)
        yi = lax.broadcasted_iota(jnp.int32, (n, rows, LANES), 1) + (lo - g["own_y"] + g["ny"] * cy)
        keep = (zi >= 0) & (zi < 4 * g["nz"]) & (yi >= 0) & (yi < 4 * g["ny"])
        if level:
            keep = keep & (lax.broadcasted_iota(jnp.int32, (n, rows, LANES), 2) < 64)
        return keep

    finish(reaction_moves)
    mine = pl.ds(pl.multiple_of(32 * cy, 32), 32)
    S0[1, pl.ds(4 + 4 * cy, 4), 16:48, :] = reaction_ref[:, mine, :]
    begin_near(halo0(1))
    SC[4:20, 16:48, :] = S0[1, 4:20, 16:48, :]
    restrict0(lambda z: SC[pl.ds(z, 4), 8:56, :])
    restrict1(lambda z: S1C[pl.ds(z, 8), 8:32, :], 1)
    begin(gather(1))
    begin_near(halo1(1))
    VB[pl.ds(4 * cy, 4)] = vol_ref[:, mine, :]

    def summed1(slot):
        finish_near(halo1(slot))
        S1[1:17, 8:32, :] = S1C[1:17, 8:32, :]
        for k, (dz, dy) in enumerate(DIRECTIONS):
            z = {-1: slice(12, 17), 0: slice(4, 14), 1: slice(1, 6)}[dz]
            y = {-1: slice(24, 32), 0: slice(8, 32), 1: slice(8, 16)}[dy]
            S1[z, y, :] += landing1(k, slot)[...]

    finish_near(halo0(1))

    def diag0(z):
        diag = S0[1, pl.ds(z, 2), 8:56, :] + center[0]
        DG0[pl.ds(z, 2), 8:56, :] = diag
        D0[pl.ds(z, 2), 8:56, :] = jnp.where(inside(0, z, 2, 8, 48), OMEGA / diag, jnp.zeros((2, 48, LANES), F32))

    over(1, 22, 2, diag0)
    summed1(1)

    def diag1(z):
        diag = S1[pl.ds(z, 2), 8:32, :] + center[1]
        DG1[pl.ds(z, 2), 8:32, :] = diag
        D1[pl.ds(z, 2), 8:32, :] = jnp.where(inside(1, z, 2, 8, 24), OMEGA / diag, jnp.zeros((2, 24, LANES), F32))

    over(1, 16, 2, diag1)
    finish(gather(1))
    gathered(1)
    DG2[...] = S2[...] + center[2]
    D2[...] = OMEGA / DG2[...]
    D3[...] = OMEGA / (restrict2(S2[...]) + center[3])
    SC[4:20, 16:48, :] = jnp.ones((16, 32, LANES), F32)
    finish(volume_moves)
    finish(weight_moves)
    weight_total = WS[...]
    for d in range(1, 8):
        weight_total += WB[d]
    IW[...] = 1.0 / weight_total

    def vcycle(n, slot, use):
        UA[4:20, 16:48, :] = D0[4:20, 16:48, :] * SC[4:20, 16:48, :]

        def own0(z):
            UB[pl.ds(z, 3), 8:56, :] = sweep(0, UA, SC, D0, z, 3, 8, 48)

        over(3, 18, 3, own0)
        restrict0(lambda z: residual(0, UB, SC, DG0, z, 4, 8, 48))
        VA[4:14, 8:32, :] = D1[4:14, 8:32, :] * S1C[4:14, 8:32, :]

        def own1(z):
            VC[pl.ds(z, 6), 8:32, :] = sweep(1, VA, S1C, D1, z, 6, 8, 24)

        over(3, 12, 6, own1)
        restrict1(lambda z: residual(1, VC, S1C, DG1, z, 8, 8, 24), slot)
        begin(gather(slot))
        begin_near(halo1(slot))

        @pl.when(n > 0)
        def _():
            finish_near(halo0(slot))

        source0 = S0.at[slot]

        def first0(z):
            U0a[pl.ds(z, 2), 8:56, :] = D0[pl.ds(z, 2), 8:56, :] * source0[pl.ds(z, 2), 8:56, :]

        over(1, 22, 2, first0)

        def pre0(z):
            U0b[pl.ds(z, 4), 8:56, :] = sweep(0, U0a, source0, D0, z, 4, 8, 48)

        over(2, 20, 4, pre0)
        summed1(slot)
        U1a[1:17, 8:32, :] = D1[1:17, 8:32, :] * S1[1:17, 8:32, :]

        def pre1(z):
            U1b[pl.ds(z, 7), 8:32, :] = sweep(1, U1a, S1, D1, z, 7, 8, 24)

        over(2, 14, 7, pre1)

        finish(gather(slot))
        gathered(slot)
        U2[1:5, 8:40, :] = D2[...] * S2[...]
        sweep2()
        mid, total = neighbours2()
        u3 = level3(restrict2(S2[...] - DG2[...] * mid + total))
        p = dot(u3, P3[...])
        for k in range(4):
            C2[k, pl.ds(0, 16, stride=2), :] = p[:, LANES * k : LANES * k + LANES]
            C2[k, pl.ds(1, 16, stride=2), :] = p[:, LANES * k : LANES * k + LANES]
        U2[1:5, 8:40, :] += C2[...]
        sweep2()
        sweep2()

        window = pl.ds(pl.multiple_of(8 * cy, 8), 24)
        own = U2[1 + cz, window, :][4:20]
        sides = jnp.where(upper_half, U2[cz, window, :][4:20], U2[2 + cz, window, :][4:20])
        wide = dot(jnp.concatenate([own, sides], axis=0), E1[...])
        for k in range(8):
            r, q = (0, k - 2) if 2 <= k < 6 else (16, (k - 2) % 4)
            C1[k, pl.ds(0, 16, stride=2), :] = wide[r : r + 16, LANES * q : LANES * q + LANES]
            C1[k, pl.ds(1, 16, stride=2), :] = wide[r : r + 16, LANES * q : LANES * q + LANES]
        for k in range(8):
            U1b[1 + 2 * k, 8:32, :] += C1[k, 4:28, :]
            U1b[2 + 2 * k, 8:32, :] += C1[k, 4:28, :]

        def post1a(z):
            U1a[pl.ds(z, 6), 8:32, :] = sweep(1, U1b, S1, D1, z, 6, 8, 24)

        over(3, 12, 6, post1a)

        def post1b(z):
            U1b[pl.ds(z, 5), 8:32, :] = sweep(1, U1a, S1, D1, z, 5, 8, 24)

        over(4, 10, 5, post1b)

        def widen0(i):
            wide = dot(flat(U1b[pl.ds(4 + i, 5), 8:32, :]), Px[...]).reshape(5, 24, LANES)
            C0[:, pl.ds(0, 24, stride=2), :] = wide
            C0[:, pl.ds(1, 24, stride=2), :] = wide
            for k in range(5):
                U0b[2 + 2 * (i + k), 8:56, :] += C0[k]
                U0b[3 + 2 * (i + k), 8:56, :] += C0[k]

        over(0, 10, 5, widen0)

        def post0a(z):
            U0a[pl.ds(z, 3), 8:56, :] = sweep(0, U0b, source0, D0, z, 3, 8, 48)

        over(3, 18, 3, post0a)

        def post0b(z):
            use(z, sweep(0, U0a, source0, D0, z, 4, 16, 32))

        over(4, 16, 4, post0b)

    def centroid():
        sibling = (member + 1 - 2 * mc, slab)
        swap = remote(LB.at[pl.ds(8 * (1 - mc), 8)], XB, x_send, x_recv, sibling)
        swap.start()
        swap.wait()
        HB[...] = LB[pl.ds(8 * mc, 8)] + XB[...]
        pieces = []
        for d in range(1, 4):
            to = lax.rem(mx + d, 4)
            pieces.append(
                remote(HB.at[pl.ds(2 * to, 2)], PB.at[d - 1], p_send.at[d - 1], p_recv.at[d - 1], (2 * to + mc, slab))
            )
        begin(pieces)
        finish(pieces)
        total = HB[pl.ds(2 * mx, 2)] + PB[0] + PB[1] + PB[2]
        inverse = jnp.broadcast_to(IW[...][None, None], (2, 4, 8, LANES)).reshape(2, 32, LANES)
        own = 8 * mc + 2 * mx
        CB[pl.ds(own, 2)] = jnp.exp(total * inverse)
        spread, passed = [], []
        for d in range(1, 4):
            to = lax.rem(mx + d, 4)
            spread.append(
                remote(CB.at[pl.ds(own, 2)], CB.at[pl.ds(own, 2)], c_send.at[d - 1], c_recv.at[d - 1], (2 * to + mc, slab))
            )
        for d in range(4):
            at = 8 * mc + 2 * lax.rem(mx - d + 4, 4)
            passed.append(remote(CB.at[pl.ds(at, 2)], CB.at[pl.ds(at, 2)], f_send.at[d], f_recv.at[d], sibling))
        begin(spread)
        passed[0].start()
        for d in range(1, 4):
            spread[d - 1].wait_recv()
            passed[d].start()
        for c in spread:
            c.wait_send()
        finish(passed)

    def half_step(n, _):
        slot = lax.rem(n, 2)

        def keep(z, h):
            MB[pl.ds(z - 4, 4)] = h

        vcycle(n, slot, keep)

        @pl.when(slot == 0)
        def _():
            def partner(z):
                p = VB[pl.ds(z - 4, 4)] / MB[pl.ds(z - 4, 4)]
                S0[1, pl.ds(z, 4), 16:48, :] = p
                SC[pl.ds(z, 4), 16:48, :] = p

            over(4, 16, 4, partner)

        @pl.when(slot == 1)
        def _():
            def marginal(z):
                m = S0[0, pl.ds(z, 4), 16:48, :] * MB[pl.ds(z - 4, 4)]
                MB[pl.ds(z - 4, 4)] = m
                LB[pl.ds(z - 4, 4)] = weight_ref[0] * jnp.log(m)

            over(4, 16, 4, marginal)
            centroid()

            def update(z):
                p = S0[0, pl.ds(z, 4), 16:48, :] * CB[pl.ds(z - 4, 4)] / MB[pl.ds(z - 4, 4)]
                S0[0, pl.ds(z, 4), 16:48, :] = p
                SC[pl.ds(z, 4), 16:48, :] = p

            over(4, 16, 4, update)

        @pl.when(n < 2 * ITERS - 1)
        def _():
            begin_near(halo0(1 - slot))

        return 0

    lax.fori_loop(0, 2 * ITERS, half_step, 0)

    moves = to_slabs(CB, 0, 0, cent_out, o_send.at[0], o_recv.at[0]) + to_slabs(
        S0.at[0], 4, 16, mult_out, o_send.at[1], o_recv.at[1]
    )
    begin(moves)
    cent_out[:, mine, :] = CB[pl.ds(4 * cy, 4)]
    mult_out[:, mine, :] = S0[0, pl.ds(4 + 4 * cy, 4), 16:48, :]
    finish(moves)


def body(nonnegative_volumes, reaction, diffusivity, member_weights):
    vmem, smem = pl.BlockSpec(memory_space=pltpu.VMEM), pl.BlockSpec(memory_space=pltpu.SMEM)
    field = jax.ShapeDtypeStruct((4, 128, 128), F32)

    def buffer(*shape):
        return pltpu.VMEM((*shape, LANES), F32)

    dma = pltpu.SemaphoreType.DMA
    scratch = [
        buffer(2, 24, 64), *[buffer(24, 64) for _ in range(7)], buffer(5, 48), buffer(10, 48),
        *[buffer(18, 40) for _ in range(8)], buffer(8, 32), buffer(8, 32), buffer(2, 2, 5, 24), buffer(2, 2, 10, 8), buffer(2, 4, 5, 8),
        buffer(2, 16, 2, 16), buffer(4, 32), buffer(4, 32), buffer(4, 32), buffer(6, 48), buffer(4, 32), buffer(4, 32), buffer(16),
        buffer(16, 32), buffer(16, 32), buffer(16, 32), buffer(8, 32), buffer(8, 32), buffer(3, 2, 32), buffer(16, 32),
        buffer(8), buffer(8, 8), buffer(8),
        buffer(128), buffer(512), buffer(512), pltpu.VMEM((128, 512), F32), pltpu.VMEM((128, 512), F32), buffer(128),
        dma((2, 8)), dma((2, 8)), dma((2, 8)), dma((2, 8)), dma((2, 16)), dma((2, 16)),
        dma((3,)), dma((3,)), dma((3,)), dma((3,)), dma((7,)), dma((7,)),
        dma, dma, dma((3,)), dma((3,)), dma((3,)), dma((3,)), dma((4,)), dma((4,)), dma((2, 3)), dma((2, 3)),
    ]
    centroid, multipliers = pl.pallas_call(
        kernel,
        out_shape=(field, field),
        in_specs=[vmem, vmem, smem, smem],
        out_specs=(vmem, vmem),
        scratch_shapes=scratch,
        compiler_params=pltpu.CompilerParams(collective_id=0, has_side_effects=True, vmem_limit_bytes=40 * 2**20),
    )(nonnegative_volumes[0], reaction, diffusivity, member_weights)
    return centroid, multipliers[None]


def solution(mesh):
    return jax.shard_map(
        body,
        mesh=mesh,
        in_specs=(P("member", "slab", None, None), P("slab", None, None), P(), P("member")),
        out_specs=(P("slab", None, None), P("member", "slab", None, None)),
        check_vma=False,
    )
```

```python
import jax
import jax.numpy as jnp
from jax import lax
from jax.experimental import pallas as pl
from jax.experimental.pallas import tpu as pltpu
from jax.sharding import PartitionSpec as P

ITERS = 3
COARSE_SWEEPS = 8
OMEGA = 0.8
LANES = 128
NZ, NY = 64, 128
F32, BF16 = jnp.float32, jnp.bfloat16
MESH = pl.DeviceIdType.MESH
FARTHEST = sorted(range(1, 16), key=lambda d: -min(d // 4, 4 - d // 4) - min(d % 4, 4 - d % 4))
DIRECTIONS = ((-1, 0), (1, 0), (0, -1), (0, 1), (-1, -1), (-1, 1), (1, -1), (1, 1))

GEOMETRY = (dict(own_z=4, own_y=16, nz=16, ny=32), dict(own_z=5, own_y=12, nz=8, ny=16))


def dot(a, b):
    high = a.astype(BF16)
    rest = a - high.astype(F32)
    middle = rest.astype(BF16)
    low = (rest - middle.astype(F32)).astype(BF16)

    def product(x):
        return jnp.dot(x, b, preferred_element_type=F32)

    return product(high) + (product(middle) + product(low))


def flat(a):
    return a.reshape(-1, LANES)


def lane_roll(a, shift):
    return pltpu.roll(flat(a), shift % LANES, 1).reshape(a.shape)


def kernel(
    vol_ref, reaction_ref, diff_ref, weight_ref, cent_out, mult_out,
    S0, SC, D0, DG0, UA, UB, U0a, U0b, C0, T0,
    S1, S1C, D1, DG1, VA, VC, U1a, U1b, C1, T1, P1, LZ, LY, LD, E0, LE, LQ,
    G, S2, D2, DG2, U2, T2, C2, D3,
    VB, MB, LB, XB, HB, PB, CB, WS, WB, IW,
    Rx, Rx1, R3, P3, E1, Px,
    h0_send, h0_recv, h1_send, h1_recv, g_send, g_recv,
    ra_send, ra_recv, va_send, va_recv, w_send, w_recv,
    x_send, x_recv, p_send, p_recv, c_send, c_recv, f_send, f_recv, o_send, o_recv,
):
    member, slab = lax.axis_index("member"), lax.axis_index("slab")
    cz, cy = slab // 4, lax.rem(slab, 4)
    mx, mc = member // 2, lax.rem(member, 2)

    def at_slab(dz, dy):
        return lax.rem(cz + dz + 4, 4) * 4 + lax.rem(cy + dy + 4, 4)

    def remote(src, dst, send, recv, to):
        return pltpu.make_async_remote_copy(
            src_ref=src, dst_ref=dst, send_sem=send, recv_sem=recv, device_id=to, device_id_type=MESH
        )

    for ref in (LZ, LY, LD, LE, LQ):
        ref[...] = jnp.zeros(ref.shape, F32)
    S0[...] = jnp.ones(S0.shape, F32)

    barrier = pltpu.get_barrier_semaphore()
    for d in FARTHEST:
        pl.semaphore_signal(barrier, inc=1, device_id=(member, at_slab(d // 4, d % 4)), device_id_type=MESH)
    for d in range(1, 8):
        pl.semaphore_signal(barrier, inc=1, device_id=(lax.rem(member + d, 8), slab), device_id_type=MESH)

    coupling = [[diff_ref[i] * (0.25**level) for i in range(3)] for level in range(4)]
    center = [2.0 * (c[0] + c[1] + c[2]) for c in coupling]

    lane = lax.broadcasted_iota(jnp.int32, (1, LANES), 1)
    one, zero = jnp.ones((1, LANES), F32), jnp.zeros((1, LANES), F32)

    def lane_mask(keep):
        return jnp.where(keep, one, zero)

    row_i = lax.broadcasted_iota(jnp.int32, (LANES, LANES), 0)
    col_i = lax.broadcasted_iota(jnp.int32, (LANES, LANES), 1)

    def half(a):
        return lax.shift_right_logical(a, 1)

    def matrix(keep, value=1.0):
        return jnp.where(keep, jnp.full((LANES, LANES), value, F32), jnp.zeros((LANES, LANES), F32)).astype(BF16)

    Rx[...] = matrix(half(row_i) == col_i, 0.125)
    Px[...] = matrix(row_i == half(col_i))
    for q in range(4):
        block = slice(LANES * q, LANES * q + LANES)
        Rx1[block, :] = matrix((row_i < 64) & (half(row_i) + 32 * q == col_i), 0.125)
        E1[:, block] = matrix((col_i < 64) & (row_i == half(col_i) + 32 * q))
        R3[block, :] = matrix(16 * (2 * q + lax.shift_right_logical(row_i, 6)) + half(row_i & 31) == col_i, 0.125)
        P3[:, block] = matrix(16 * (2 * q + lax.shift_right_logical(col_i, 6)) + half(col_i & 31) == row_i)

    left = [lane_mask(lane > 0) * coupling[0][2], None, lane_mask((lane & 31) > 0) * coupling[2][2], lane_mask((lane & 15) > 0) * coupling[3][2]]
    right = [lane_mask(lane < 127) * coupling[0][2], None, lane_mask((lane & 31) < 31) * coupling[2][2], lane_mask((lane & 15) < 15) * coupling[3][2]]
    WS[...] = jnp.full((8, LANES), weight_ref[0], F32)
    for ref in (SC, UA, UB, VA, VC, S1C, U0a, U0b, U1a, U1b, U2, T1):
        ref[...] = jnp.zeros(ref.shape, F32)
    pl.semaphore_wait(barrier, 22)

    def inner(dz, dy):
        return (cz + dz >= 0) & (cz + dz < 4) & (cy + dy >= 0) & (cy + dy < 4)

    def halo0(slot):
        copies = []
        for k, (dz, dy) in enumerate(DIRECTIONS):
            if dy == 0:
                zs, zd = (4, 20) if dz < 0 else (17, 1)
                src, dst = S0.at[slot, pl.ds(zs, 3), pl.ds(16, 32)], S0.at[slot, pl.ds(zd, 3), pl.ds(16, 32)]
            elif dz == 0:
                src, dst = E0.at[(dy + 1) // 2], LE.at[slot, k - 2]
            else:
                src, dst = E0.at[(dy + 1) // 2, pl.ds(0 if dz < 0 else 6, 2)], LQ.at[slot, k - 4]
            copies.append((
                dz, dy, remote(src, dst, h0_send.at[slot, k], h0_recv.at[slot, k], (member, at_slab(dz, dy)))
            ))
        return copies

    def begin_halo0(slot):
        for edge, row in ((0, 16), (1, 44)):
            for p in range(8):
                E0[edge, p, 0:4, :] = S0[slot, 4 + 2 * p, row : row + 4, :]
                E0[edge, p, 4:8, :] = S0[slot, 5 + 2 * p, row : row + 4, :]
        begin_near(halo0(slot))

    def finish_halo0(slot):
        finish_near(halo0(slot))
        for k, (dz, dy) in enumerate(DIRECTIONS):
            if dy == 0:
                continue
            row, z0, tiles = (48 if dy < 0 else 12), {-1: 20, 0: 4, 1: 0}[dz], 8 if dz == 0 else 2
            for p in range(tiles):
                tile = LE[slot, k - 2, p] if dz == 0 else LQ[slot, k - 4, p]
                S0[slot, z0 + 2 * p, row : row + 4, :] = tile[0:4]
                S0[slot, z0 + 2 * p + 1, row : row + 4, :] = tile[4:8]

    def landing1(k, slot):
        if k < 2:
            return LZ.at[slot, k]
        return LY.at[slot, k - 2] if k < 4 else LD.at[slot, k - 4]

    def halo1(slot):
        copies = []
        for k, (dz, dy) in enumerate(DIRECTIONS):
            z = {-1: pl.ds(0, 3), 0: pl.ds(0, 5), 1: pl.ds(2, 3)}[dz]
            y = {-1: pl.ds(0, 8), 0: pl.ds(0, 24), 1: pl.ds(16, 8)}[dy]
            copies.append((
                dz, dy,
                remote(
                    P1.at[z, y], landing1(k, slot),
                    h1_send.at[slot, k], h1_recv.at[slot, k], (member, at_slab(dz, dy)),
                ),
            ))
        return copies

    def begin_near(copies):
        for dz, dy, c in copies:
            pl.when(inner(dz, dy))(c.start)

    def begin_halo1(slot):
        for p in range(5):
            P1[p] = S1C[4 + 2 * p, 8:32, :] + lane_roll(S1C[5 + 2 * p, 8:32, :], 64)
        begin_near(halo1(slot))

    def finish_near(copies):
        for dz, dy, c in copies:
            pl.when(inner(-dz, -dy))(c.wait_recv)
        for dz, dy, c in copies:
            pl.when(inner(dz, dy))(c.wait_send)

    def gather(slot):
        return [
            remote(
                G.at[slot, slab], G.at[slot, slab],
                g_send.at[slot, d], g_recv.at[slot, d], (member, at_slab(d // 4, d % 4)),
            )
            for d in FARTHEST
        ]

    def begin(copies):
        for c in copies:
            c.start()

    def finish(copies):
        for c in copies:
            c.wait()

    def to_blocks(src, dst, dst_z, dst_y, send, recv):
        copies = []
        for d in range(1, 4):
            to = lax.rem(cy + d, 4)
            copies.append(
                remote(
                    src.at[:, pl.ds(pl.multiple_of(32 * to, 32), 32)],
                    dst.at[pl.ds(dst_z + 4 * cy, 4), pl.ds(dst_y, 32)],
                    send.at[d - 1], recv.at[d - 1], (member, cz * 4 + to),
                )
            )
        return copies

    def to_slabs(src, src_z, src_y, dst, send, recv):
        copies = []
        for d in range(1, 4):
            to = lax.rem(cy + d, 4)
            copies.append(
                remote(
                    src.at[pl.ds(src_z + 4 * to, 4), pl.ds(src_y, 32)],
                    dst.at[:, pl.ds(pl.multiple_of(32 * cy, 32), 32)],
                    send.at[d - 1], recv.at[d - 1], (member, cz * 4 + to),
                )
            )
        return copies

    reaction_moves = to_blocks(reaction_ref, S0.at[1], 4, 16, ra_send, ra_recv)
    volume_moves = to_blocks(vol_ref, VB, 0, 0, va_send, va_recv)
    begin(reaction_moves)
    weight_moves = [
        remote(WS, WB.at[d], w_send.at[d - 1], w_recv.at[d - 1], (lax.rem(member + d, 8), slab)) for d in range(1, 8)
    ]

    def neighbours(level, u, z, n, lo, rows):
        c = coupling[level]
        mid = u[pl.ds(z, n), lo : lo + rows, :]
        total = c[0] * (u[pl.ds(z - 1, n), lo : lo + rows, :] + u[pl.ds(z + 1, n), lo : lo + rows, :])
        total += c[1] * (u[pl.ds(z, n), lo - 1 : lo + rows - 1, :] + u[pl.ds(z, n), lo + 1 : lo + rows + 1, :])
        if level == 0:
            total += left[0] * lane_roll(mid, 1) + right[0] * lane_roll(mid, -1)
        else:
            total += c[2] * (lane_roll(mid, 1) + lane_roll(mid, -1))
        return mid, total

    def over(z0, count, step, body):
        for z in range(z0, z0 + count, step):
            body(z)

    def sweep(level, u, s, d, z, n, lo, rows):
        mid, total = neighbours(level, u, z, n, lo, rows)
        return (1.0 - OMEGA) * mid + d[pl.ds(z, n), lo : lo + rows, :] * (s[pl.ds(z, n), lo : lo + rows, :] + total)

    def residual(level, u, s, dg, z, n, lo, rows):
        mid, total = neighbours(level, u, z, n, lo, rows)
        return s[pl.ds(z, n), lo : lo + rows, :] - dg[pl.ds(z, n), lo : lo + rows, :] * mid + total

    def restrict0(fine):
        def body(z):
            a = fine(z)
            for k in range(2):
                T0[(z - 2) // 2 + k] = a[2 * k] + a[2 * k + 1]

        over(2, 20, 4, body)

        def rows(i):
            e = T0[pl.ds(i, 5), pl.ds(0, 24, stride=2), :] + T0[pl.ds(i, 5), pl.ds(1, 24, stride=2), :]
            S1C[pl.ds(4 + i, 5), 8:32, :] = dot(flat(e), Rx[...]).reshape(5, 24, LANES)

        over(0, 10, 5, rows)

    def restrict1(fine, slot):
        def body(z):
            a = fine(z)
            for k in range(4):
                T1[(z - 1) // 2 + k, 4:28, :] = a[2 * k] + a[2 * k + 1]

        over(1, 16, 8, body)
        e = T1[:, pl.ds(0, 16, stride=2), :] + T1[:, pl.ds(1, 16, stride=2), :]
        own = jnp.concatenate([e[2], e[3], e[4], e[5]], axis=1)
        sides = jnp.concatenate([e[6], e[7], e[0], e[1]], axis=1)
        m = dot(jnp.concatenate([own, sides], axis=0), Rx1[...]).reshape(2, 16, LANES)
        G[slot, slab, 0:8, :] = m[0, 4:12]
        G[slot, slab, 8:16, :] = m[1, 4:12]
        for row, part in ((16, m[0, 12:14]), (18, m[1, 12:14]), (20, m[1, 2:4]), (22, m[0, 2:4])):
            G[slot, slab, row : row + 2, :] = part

    upper_half, row8 = lane >= 64, lax.broadcasted_iota(jnp.int32, (8, LANES), 0)
    nothing = jnp.zeros((8, LANES), F32)

    def gathered(slot):
        def rows(c, j, g):
            below = G[slot, 4 * c + j - 1, 16:24, :] if j > 0 else nothing
            above = G[slot, 4 * c + j + 1, 16:24, :] if j < 3 else nothing
            if g:
                below = pltpu.roll(below, 6, 0) if j > 0 else nothing
                above = pltpu.roll(above, 2, 0) if j < 3 else nothing
            near = jnp.where(row8 < 2, below, jnp.where(row8 >= 6, above, nothing))
            return G[slot, 4 * c + j, 8 * g : 8 * g + 8, :] + near

        for j in range(4):
            side = [nothing] + [rows(c, j, 1) for c in range(4)] + [nothing]
            for c in range(4):
                S2[c, 8 * j : 8 * j + 8, :] = rows(c, j, 0) + jnp.where(upper_half, side[c + 2], side[c])

    def restrict2(a):
        T2[...] = a
        e = T2[:, pl.ds(0, 16, stride=2), :] + T2[:, pl.ds(1, 16, stride=2), :]
        return dot(jnp.concatenate([e[0], e[1], e[2], e[3]], axis=1), R3[...])

    first_chunk, last_chunk = lane < 32, lane >= 96
    plane2 = jnp.zeros((1, 32, LANES), F32)

    def neighbours2():
        c = coupling[2]
        mid = U2[1:5, 8:40, :]
        up, down = lane_roll(mid, 32), lane_roll(mid, -32)
        before = jnp.where(first_chunk, jnp.concatenate([plane2, up[:3]], axis=0), up)
        after = jnp.where(last_chunk, jnp.concatenate([down[1:], plane2], axis=0), down)
        total = c[0] * (before + after) + c[1] * (U2[1:5, 7:39, :] + U2[1:5, 9:41, :])
        total += left[2] * lane_roll(mid, 1) + right[2] * lane_roll(mid, -1)
        return mid, total

    def sweep2():
        mid, total = neighbours2()
        U2[1:5, 8:40, :] = (1.0 - OMEGA) * mid + D2[...] * (S2[...] + total)

    row16 = lax.broadcasted_iota(jnp.int32, (16, LANES), 0)
    zeros16, ones16 = jnp.zeros((16, LANES), F32), jnp.ones((16, LANES), F32)
    up3 = jnp.where(row16 > 0, ones16, zeros16) * coupling[3][1]
    down3 = jnp.where(row16 < 15, ones16, zeros16) * coupling[3][1]
    before3 = lane_mask(lane >= 16) * coupling[3][0]
    after3 = lane_mask(lane < 112) * coupling[3][0]

    def level3(s):
        d = D3[...]
        u = d * s
        for _ in range(COARSE_SWEEPS - 1):
            total = before3 * lane_roll(u, 16) + after3 * lane_roll(u, -16)
            total += up3 * pltpu.roll(u, 1, 0) + down3 * pltpu.roll(u, 15, 0)
            total += left[3] * lane_roll(u, 1) + right[3] * lane_roll(u, -1)
            u = (1.0 - OMEGA) * u + d * (s + total)
        return u

    def inside(level, z, n, lo, rows):
        g = GEOMETRY[level]
        zi = lax.broadcasted_iota(jnp.int32, (n, rows, LANES), 0) + (z - g["own_z"] + g["nz"] * cz)
        yi = lax.broadcasted_iota(jnp.int32, (n, rows, LANES), 1) + (lo - g["own_y"] + g["ny"] * cy)
        keep = (zi >= 0) & (zi < 4 * g["nz"]) & (yi >= 0) & (yi < 4 * g["ny"])
        if level:
            keep = keep & (lax.broadcasted_iota(jnp.int32, (n, rows, LANES), 2) < 64)
        return keep

    finish(reaction_moves)
    mine = pl.ds(pl.multiple_of(32 * cy, 32), 32)
    S0[1, pl.ds(4 + 4 * cy, 4), 16:48, :] = reaction_ref[:, mine, :]
    begin_halo0(1)
    SC[4:20, 16:48, :] = S0[1, 4:20, 16:48, :]
    restrict0(lambda z: SC[pl.ds(z, 4), 8:56, :])
    restrict1(lambda z: S1C[pl.ds(z, 8), 8:32, :], 1)
    begin(gather(1))
    begin_halo1(1)
    begin(volume_moves)
    begin(weight_moves)
    VB[pl.ds(4 * cy, 4)] = vol_ref[:, mine, :]

    def summed1(slot):
        finish_near(halo1(slot))
        S1[1:17, 8:32, :] = S1C[1:17, 8:32, :]
        for k, (dz, dy) in enumerate(DIRECTIONS):
            z0, tiles = {-1: (12, 3), 0: (4, 5), 1: (0, 3)}[dz]
            y = {-1: slice(24, 32), 0: slice(8, 32), 1: slice(8, 16)}[dy]
            for p in range(tiles):
                both = landing1(k, slot)[p]
                for z, part in ((z0 + 2 * p, both), (z0 + 2 * p + 1, lane_roll(both, 64))):
                    if 1 <= z < 17:
                        S1[z, y, :] += jnp.where(upper_half, jnp.zeros_like(part), part)

    finish_halo0(1)

    def diag0(z):
        diag = S0[1, pl.ds(z, 2), 8:56, :] + center[0]
        DG0[pl.ds(z, 2), 8:56, :] = diag
        D0[pl.ds(z, 2), 8:56, :] = jnp.where(inside(0, z, 2, 8, 48), OMEGA / diag, jnp.zeros((2, 48, LANES), F32))

    over(1, 22, 2, diag0)
    summed1(1)

    def diag1(z):
        diag = S1[pl.ds(z, 2), 8:32, :] + center[1]
        DG1[pl.ds(z, 2), 8:32, :] = diag
        D1[pl.ds(z, 2), 8:32, :] = jnp.where(inside(1, z, 2, 8, 24), OMEGA / diag, jnp.zeros((2, 24, LANES), F32))

    over(1, 16, 2, diag1)
    finish(gather(1))
    gathered(1)
    DG2[...] = S2[...] + center[2]
    D2[...] = OMEGA / DG2[...]
    D3[...] = OMEGA / (restrict2(S2[...]) + center[3])
    SC[4:20, 16:48, :] = jnp.ones((16, 32, LANES), F32)
    finish(volume_moves)
    finish(weight_moves)
    weight_total = WS[...]
    for d in range(1, 8):
        weight_total += WB[d]
    IW[...] = 1.0 / weight_total

    def vcycle(n, slot, use):
        UA[4:20, 16:48, :] = D0[4:20, 16:48, :] * SC[4:20, 16:48, :]

        def own0(z):
            UB[pl.ds(z, 3), 8:56, :] = sweep(0, UA, SC, D0, z, 3, 8, 48)

        over(3, 18, 3, own0)
        restrict0(lambda z: residual(0, UB, SC, DG0, z, 4, 8, 48))
        begin_halo1(slot)
        VA[4:14, 8:32, :] = D1[4:14, 8:32, :] * S1C[4:14, 8:32, :]

        def own1(z):
            VC[pl.ds(z, 6), 8:32, :] = sweep(1, VA, S1C, D1, z, 6, 8, 24)

        over(3, 12, 6, own1)
        restrict1(lambda z: residual(1, VC, S1C, DG1, z, 8, 8, 24), slot)
        begin(gather(slot))

        @pl.when(n > 0)
        def _():
            finish_halo0(slot)

        source0 = S0.at[slot]

        def first0(z):
            U0a[pl.ds(z, 2), 8:56, :] = D0[pl.ds(z, 2), 8:56, :] * source0[pl.ds(z, 2), 8:56, :]

        over(1, 22, 2, first0)

        def pre0(z):
            U0b[pl.ds(z, 4), 8:56, :] = sweep(0, U0a, source0, D0, z, 4, 8, 48)

        over(2, 20, 4, pre0)
        summed1(slot)
        U1a[1:17, 8:32, :] = D1[1:17, 8:32, :] * S1[1:17, 8:32, :]

        def pre1(z):
            U1b[pl.ds(z, 7), 8:32, :] = sweep(1, U1a, S1, D1, z, 7, 8, 24)

        over(2, 14, 7, pre1)

        finish(gather(slot))
        gathered(slot)
        U2[1:5, 8:40, :] = D2[...] * S2[...]
        sweep2()
        mid, total = neighbours2()
        u3 = level3(restrict2(S2[...] - DG2[...] * mid + total))
        p = dot(u3, P3[...])
        for k in range(4):
            C2[k, pl.ds(0, 16, stride=2), :] = p[:, LANES * k : LANES * k + LANES]
            C2[k, pl.ds(1, 16, stride=2), :] = p[:, LANES * k : LANES * k + LANES]
        U2[1:5, 8:40, :] += C2[...]
        sweep2()
        sweep2()

        window = pl.ds(pl.multiple_of(8 * cy, 8), 24)
        own = U2[1 + cz, window, :][4:20]
        sides = jnp.where(upper_half, U2[cz, window, :][4:20], U2[2 + cz, window, :][4:20])
        wide = dot(jnp.concatenate([own, sides], axis=0), E1[...])
        for k in range(8):
            r, q = (0, k - 2) if 2 <= k < 6 else (16, (k - 2) % 4)
            C1[k, pl.ds(0, 16, stride=2), :] = wide[r : r + 16, LANES * q : LANES * q + LANES]
            C1[k, pl.ds(1, 16, stride=2), :] = wide[r : r + 16, LANES * q : LANES * q + LANES]
        for k in range(8):
            U1b[1 + 2 * k, 8:32, :] += C1[k, 4:28, :]
            U1b[2 + 2 * k, 8:32, :] += C1[k, 4:28, :]

        def post1a(z):
            U1a[pl.ds(z, 6), 8:32, :] = sweep(1, U1b, S1, D1, z, 6, 8, 24)

        over(3, 12, 6, post1a)

        def post1b(z):
            U1b[pl.ds(z, 5), 8:32, :] = sweep(1, U1a, S1, D1, z, 5, 8, 24)

        over(4, 10, 5, post1b)

        def widen0(i):
            wide = dot(flat(U1b[pl.ds(4 + i, 5), 8:32, :]), Px[...]).reshape(5, 24, LANES)
            C0[:, pl.ds(0, 24, stride=2), :] = wide
            C0[:, pl.ds(1, 24, stride=2), :] = wide
            for k in range(5):
                U0b[2 + 2 * (i + k), 8:56, :] += C0[k]
                U0b[3 + 2 * (i + k), 8:56, :] += C0[k]

        over(0, 10, 5, widen0)

        def post0a(z):
            U0a[pl.ds(z, 3), 8:56, :] = sweep(0, U0b, source0, D0, z, 3, 8, 48)

        over(3, 18, 3, post0a)

        def post0b(z):
            use(z, sweep(0, U0a, source0, D0, z, 4, 16, 32))

        over(4, 16, 4, post0b)

    def centroid(last):
        sibling = (member + 1 - 2 * mc, slab)
        swap = remote(LB.at[pl.ds(8 * (1 - mc), 8)], XB, x_send, x_recv, sibling)

        def marginal(at):
            m = S0[0, pl.ds(4 + at, 4), 16:48, :] * MB[pl.ds(at, 4)]
            MB[pl.ds(at, 4)] = m
            LB[pl.ds(at, 4)] = weight_ref[0] * jnp.log(m)

        def update(at, planes):
            for k in range(0, planes, 2):
                z = pl.ds(at + k, 2)
                p = S0[0, pl.ds(4 + at + k, 2), 16:48, :] * CB[z] / MB[z]
                S0[0, pl.ds(4 + at + k, 2), 16:48, :] = p
                SC[pl.ds(4 + at + k, 2), 16:48, :] = p

        marginal(8 * (1 - mc))
        marginal(8 * (1 - mc) + 4)
        swap.start()
        marginal(8 * mc)
        marginal(8 * mc + 4)
        swap.wait()
        HB[...] = LB[pl.ds(8 * mc, 8)] + XB[...]
        pieces = []
        for d in range(1, 4):
            to = lax.rem(mx + d, 4)
            pieces.append(
                remote(HB.at[pl.ds(2 * to, 2)], PB.at[d - 1], p_send.at[d - 1], p_recv.at[d - 1], (2 * to + mc, slab))
            )
        begin(pieces)
        finish(pieces)
        total = HB[pl.ds(2 * mx, 2)] + PB[0] + PB[1] + PB[2]
        inverse = jnp.broadcast_to(IW[...][None, None], (2, 4, 8, LANES)).reshape(2, 32, LANES)
        own = 8 * mc + 2 * mx
        CB[pl.ds(own, 2)] = jnp.exp(total * inverse)
        spread, passed = [], []
        for d in range(1, 4):
            to = lax.rem(mx + d, 4)
            spread.append(
                remote(CB.at[pl.ds(own, 2)], CB.at[pl.ds(own, 2)], c_send.at[d - 1], c_recv.at[d - 1], (2 * to + mc, slab))
            )
        for d in range(4):
            at = 8 * mc + 2 * lax.rem(mx - d + 4, 4)
            passed.append(remote(CB.at[pl.ds(at, 2)], CB.at[pl.ds(at, 2)], f_send.at[d], f_recv.at[d], sibling))
        begin(spread)
        passed[0].start()
        update(own, 2)
        for d in range(1, 4):
            spread[d - 1].wait_recv()
            passed[d].start()
            update(8 * mc + 2 * lax.rem(mx - d + 4, 4), 2)
        for d in range(4):
            passed[d].wait_recv()
        pl.when(last)(lambda: begin(centroid_moves()))
        update(8 * (1 - mc), 8)
        for c in spread + passed:
            c.wait_send()

    def centroid_moves():
        copies = []
        for d in range(1, 4):
            to = lax.rem(cy + d, 4)
            copies.append(
                remote(
                    CB.at[pl.ds(4 * to + 2 * mc, 2)],
                    cent_out.at[pl.ds(2 * mc, 2), pl.ds(pl.multiple_of(32 * cy, 32), 32)],
                    o_send.at[0, d - 1], o_recv.at[0, d - 1], (member, cz * 4 + to),
                )
            )
        return copies

    def half_step(n, _):
        slot = lax.rem(n, 2)

        def keep(z, h):
            MB[pl.ds(z - 4, 4)] = h

        vcycle(n, slot, keep)

        @pl.when(slot == 0)
        def _():
            def partner(z):
                p = VB[pl.ds(z - 4, 4)] / MB[pl.ds(z - 4, 4)]
                S0[1, pl.ds(z, 4), 16:48, :] = p
                SC[pl.ds(z, 4), 16:48, :] = p

            over(4, 16, 4, partner)

        @pl.when(slot == 1)
        def _():
            centroid(n == 2 * ITERS - 1)

        @pl.when(n < 2 * ITERS - 1)
        def _():
            begin_halo0(1 - slot)

        return 0

    lax.fori_loop(0, 2 * ITERS, half_step, 0)

    moves = to_slabs(S0.at[0], 4, 16, mult_out, o_send.at[1], o_recv.at[1])
    begin(moves)
    mult_out[:, mine, :] = S0[0, pl.ds(4 + 4 * cy, 4), 16:48, :]
    cent_out[pl.ds(2 * mc, 2), mine, :] = CB[pl.ds(4 * cy + 2 * mc, 2)]
    finish(centroid_moves())
    half_out = cent_out.at[pl.ds(2 * mc, 2)]
    across = remote(half_out, half_out, x_send, x_recv, (member + 1 - 2 * mc, slab))
    across.start()
    finish(moves)
    across.wait()


def body(nonnegative_volumes, reaction, diffusivity, member_weights):
    vmem, smem = pl.BlockSpec(memory_space=pltpu.VMEM), pl.BlockSpec(memory_space=pltpu.SMEM)
    field = jax.ShapeDtypeStruct((4, 128, 128), F32)

    def buffer(*shape):
        return pltpu.VMEM((*shape, LANES), F32)

    dma = pltpu.SemaphoreType.DMA
    scratch = [
        buffer(2, 24, 64), *[buffer(24, 64) for _ in range(7)], buffer(5, 48), buffer(10, 48),
        *[buffer(18, 40) for _ in range(8)], buffer(8, 32), buffer(8, 32), buffer(5, 24),
        buffer(2, 2, 3, 24), buffer(2, 2, 5, 8), buffer(2, 4, 3, 8), buffer(2, 8, 8), buffer(2, 2, 8, 8), buffer(2, 4, 2, 8),
        buffer(2, 16, 24), buffer(4, 32), buffer(4, 32), buffer(4, 32), buffer(6, 48), buffer(4, 32), buffer(4, 32), buffer(16),
        buffer(16, 32), buffer(16, 32), buffer(16, 32), buffer(8, 32), buffer(8, 32), buffer(3, 2, 32), buffer(16, 32),
        buffer(8), buffer(8, 8), buffer(8),
        *[pltpu.VMEM(shape, BF16) for shape in ((128, 128), (512, 128), (512, 128), (128, 512), (128, 512), (128, 128))],
        dma((2, 8)), dma((2, 8)), dma((2, 8)), dma((2, 8)), dma((2, 16)), dma((2, 16)),
        dma((3,)), dma((3,)), dma((3,)), dma((3,)), dma((7,)), dma((7,)),
        dma, dma, dma((3,)), dma((3,)), dma((3,)), dma((3,)), dma((4,)), dma((4,)), dma((2, 3)), dma((2, 3)),
    ]
    centroid, multipliers = pl.pallas_call(
        kernel,
        out_shape=(field, field),
        in_specs=[vmem, vmem, smem, smem],
        out_specs=(vmem, vmem),
        scratch_shapes=scratch,
        compiler_params=pltpu.CompilerParams(collective_id=0, has_side_effects=True, vmem_limit_bytes=40 * 2**20),
    )(nonnegative_volumes[0], reaction, diffusivity, member_weights)
    return centroid, multipliers[None]


def solution(mesh):
    return jax.shard_map(
        body,
        mesh=mesh,
        in_specs=(P("member", "slab", None, None), P("slab", None, None), P(), P("member")),
        out_specs=(P("slab", None, None), P("member", "slab", None, None)),
        check_vma=False,
    )
```

```python
import jax
import jax.numpy as jnp
from jax import lax
from jax.experimental import pallas as pl
from jax.experimental.pallas import tpu as pltpu
from jax.sharding import PartitionSpec as P

ITERS = 3
COARSE_SWEEPS = 8
OMEGA = 0.8
LANES = 128
NZ, NY = 64, 128
F32, BF16 = jnp.float32, jnp.bfloat16
MESH = pl.DeviceIdType.MESH
FARTHEST = sorted(range(1, 16), key=lambda d: -min(d // 4, 4 - d // 4) - min(d % 4, 4 - d % 4))
DIRECTIONS = ((-1, 0), (1, 0), (0, -1), (0, 1), (-1, -1), (-1, 1), (1, -1), (1, 1))

GEOMETRY = (dict(own_z=4, own_y=16, nz=16, ny=32), dict(own_z=5, own_y=12, nz=8, ny=16))


def dot(a, b):
    high = a.astype(BF16)
    low = (a - high.astype(F32)).astype(BF16)
    return jnp.dot(high, b, preferred_element_type=F32) + jnp.dot(low, b, preferred_element_type=F32)


def flat(a):
    return a.reshape(-1, LANES)


def lane_roll(a, shift):
    return pltpu.roll(flat(a), shift % LANES, 1).reshape(a.shape)


def kernel(
    vol_ref, reaction_ref, diff_ref, weight_ref, cent_out, mult_out,
    S0, SC, D0, DG0, UA, UB, U0a, U0b, C0, T0,
    S1, S1C, D1, DG1, VA, VC, U1a, U1b, C1, T1, P1, LZ, LY, LD, E0, LE, LQ,
    G, S2, D2, DG2, U2, T2, C2, D3, K3,
    VB, MB, LB, XB, HB, PB, CB, WS, WB, IW,
    Rx, Rx1, R3, P3, E1, Px,
    h0_send, h0_recv, h1_send, h1_recv, g_send, g_recv,
    ra_send, ra_recv, va_send, va_recv, w_send, w_recv,
    l_sem, x_send, x_recv, p_send, p_recv, c_send, c_recv, f_send, f_recv, o_send, o_recv,
):
    member, slab = lax.axis_index("member"), lax.axis_index("slab")
    cz, cy = slab // 4, lax.rem(slab, 4)
    mx, mc = member // 2, lax.rem(member, 2)

    def at_slab(dz, dy):
        return lax.rem(cz + dz + 4, 4) * 4 + lax.rem(cy + dy + 4, 4)

    def remote(src, dst, send, recv, to):
        return pltpu.make_async_remote_copy(
            src_ref=src, dst_ref=dst, send_sem=send, recv_sem=recv, device_id=to, device_id_type=MESH
        )

    for ref in (LZ, LY, LD, LE, LQ):
        ref[...] = jnp.zeros(ref.shape, F32)
    S0[...] = jnp.ones(S0.shape, F32)
    mine = pl.ds(pl.multiple_of(32 * cy, 32), 32)
    own_reaction = pltpu.make_async_copy(reaction_ref.at[:, mine], S0.at[1, pl.ds(4 + 4 * cy, 4), pl.ds(16, 32)], l_sem.at[0])
    own_volume = pltpu.make_async_copy(vol_ref.at[:, mine], VB.at[pl.ds(4 * cy, 4)], l_sem.at[1])
    own_reaction.start()
    own_volume.start()

    barrier = pltpu.get_barrier_semaphore()
    for d in FARTHEST:
        pl.semaphore_signal(barrier, inc=1, device_id=(member, at_slab(d // 4, d % 4)), device_id_type=MESH)
    for d in range(1, 8):
        pl.semaphore_signal(barrier, inc=1, device_id=(lax.rem(member + d, 8), slab), device_id_type=MESH)

    coupling = [[diff_ref[i] * (0.25**level) for i in range(3)] for level in range(4)]
    center = [2.0 * (c[0] + c[1] + c[2]) for c in coupling]

    lane = lax.broadcasted_iota(jnp.int32, (1, LANES), 1)
    one, zero = jnp.ones((1, LANES), F32), jnp.zeros((1, LANES), F32)

    def lane_mask(keep):
        return jnp.where(keep, one, zero)

    row_i = lax.broadcasted_iota(jnp.int32, (LANES, LANES), 0)
    col_i = lax.broadcasted_iota(jnp.int32, (LANES, LANES), 1)

    def half(a):
        return lax.shift_right_logical(a, 1)

    def matrix(keep, value=1.0):
        return jnp.where(keep, jnp.full((LANES, LANES), value, F32), jnp.zeros((LANES, LANES), F32)).astype(BF16)

    Rx[...] = matrix(half(row_i) == col_i, 0.125)
    Px[...] = matrix(row_i == half(col_i))
    for q in range(4):
        block = slice(LANES * q, LANES * q + LANES)
        Rx1[block, :] = matrix((row_i < 64) & (half(row_i) + 32 * q == col_i), 0.125)
        E1[:, block] = matrix((col_i < 64) & (row_i == half(col_i) + 32 * q))
        R3[block, :] = matrix(16 * (2 * q + lax.shift_right_logical(row_i, 6)) + half(row_i & 31) == col_i, 0.125)
        P3[:, block] = matrix(16 * (2 * q + lax.shift_right_logical(col_i, 6)) + half(col_i & 31) == row_i)

    left = [lane_mask(lane > 0) * coupling[0][2], None, lane_mask((lane & 31) > 0) * coupling[2][2], lane_mask((lane & 15) > 0) * coupling[3][2]]
    right = [lane_mask(lane < 127) * coupling[0][2], None, lane_mask((lane & 31) < 31) * coupling[2][2], lane_mask((lane & 15) < 15) * coupling[3][2]]
    WS[...] = jnp.full((8, LANES), weight_ref[0], F32)
    for ref in (SC, UA, UB, VA, VC, S1C, U0a, U0b, U1a, U1b, U2, T1):
        ref[...] = jnp.zeros(ref.shape, F32)
    pl.semaphore_wait(barrier, 22)

    def inner(dz, dy):
        return (cz + dz >= 0) & (cz + dz < 4) & (cy + dy >= 0) & (cy + dy < 4)

    def halo0(slot):
        copies = []
        for k, (dz, dy) in enumerate(DIRECTIONS):
            if dy == 0:
                zs, zd = (4, 20) if dz < 0 else (17, 1)
                src, dst = S0.at[slot, pl.ds(zs, 3), pl.ds(16, 32)], S0.at[slot, pl.ds(zd, 3), pl.ds(16, 32)]
            elif dz == 0:
                src, dst = E0.at[(dy + 1) // 2], LE.at[slot, k - 2]
            else:
                src, dst = E0.at[(dy + 1) // 2, pl.ds(0 if dz < 0 else 6, 2)], LQ.at[slot, k - 4]
            copies.append((
                dz, dy, remote(src, dst, h0_send.at[slot, k], h0_recv.at[slot, k], (member, at_slab(dz, dy)))
            ))
        return copies

    def begin_halo0(slot):
        for edge, row in ((0, 16), (1, 44)):
            for p in range(8):
                E0[edge, p, 0:4, :] = S0[slot, 4 + 2 * p, row : row + 4, :]
                E0[edge, p, 4:8, :] = S0[slot, 5 + 2 * p, row : row + 4, :]
        begin_near(halo0(slot))

    def finish_halo0(slot):
        finish_near(halo0(slot))
        for k, (dz, dy) in enumerate(DIRECTIONS):
            if dy == 0:
                continue
            row, z0, tiles = (48 if dy < 0 else 12), {-1: 20, 0: 4, 1: 0}[dz], 8 if dz == 0 else 2
            for p in range(tiles):
                tile = LE[slot, k - 2, p] if dz == 0 else LQ[slot, k - 4, p]
                S0[slot, z0 + 2 * p, row : row + 4, :] = tile[0:4]
                S0[slot, z0 + 2 * p + 1, row : row + 4, :] = tile[4:8]

    def landing1(k, slot):
        if k < 2:
            return LZ.at[slot, k]
        return LY.at[slot, k - 2] if k < 4 else LD.at[slot, k - 4]

    def halo1(slot):
        copies = []
        for k, (dz, dy) in enumerate(DIRECTIONS):
            z = {-1: pl.ds(0, 3), 0: pl.ds(0, 5), 1: pl.ds(2, 3)}[dz]
            y = {-1: pl.ds(0, 8), 0: pl.ds(0, 24), 1: pl.ds(16, 8)}[dy]
            copies.append((
                dz, dy,
                remote(
                    P1.at[z, y], landing1(k, slot),
                    h1_send.at[slot, k], h1_recv.at[slot, k], (member, at_slab(dz, dy)),
                ),
            ))
        return copies

    def begin_near(copies):
        for dz, dy, c in copies:
            pl.when(inner(dz, dy))(c.start)

    def begin_halo1(slot):
        for p in range(5):
            P1[p] = S1C[4 + 2 * p, 8:32, :] + lane_roll(S1C[5 + 2 * p, 8:32, :], 64)
        begin_near(halo1(slot))

    def finish_near(copies):
        for dz, dy, c in copies:
            pl.when(inner(-dz, -dy))(c.wait_recv)
        for dz, dy, c in copies:
            pl.when(inner(dz, dy))(c.wait_send)

    def gather(slot):
        return [
            remote(
                G.at[slot, slab], G.at[slot, slab],
                g_send.at[slot, d], g_recv.at[slot, d], (member, at_slab(d // 4, d % 4)),
            )
            for d in FARTHEST
        ]

    def begin(copies):
        for c in copies:
            c.start()

    def finish(copies):
        for c in copies:
            c.wait()

    def to_blocks(src, dst, dst_z, dst_y, send, recv):
        copies = []
        for d in range(1, 4):
            to = lax.rem(cy + d, 4)
            copies.append(
                remote(
                    src.at[:, pl.ds(pl.multiple_of(32 * to, 32), 32)],
                    dst.at[pl.ds(dst_z + 4 * cy, 4), pl.ds(dst_y, 32)],
                    send.at[d - 1], recv.at[d - 1], (member, cz * 4 + to),
                )
            )
        return copies

    def to_slabs(src, src_z, src_y, dst, send, recv):
        copies = []
        for d in range(1, 4):
            to = lax.rem(cy + d, 4)
            copies.append(
                remote(
                    src.at[pl.ds(src_z + 4 * to, 4), pl.ds(src_y, 32)],
                    dst.at[:, pl.ds(pl.multiple_of(32 * cy, 32), 32)],
                    send.at[d - 1], recv.at[d - 1], (member, cz * 4 + to),
                )
            )
        return copies

    reaction_moves = to_blocks(reaction_ref, S0.at[1], 4, 16, ra_send, ra_recv)
    volume_moves = to_blocks(vol_ref, VB, 0, 0, va_send, va_recv)
    begin(reaction_moves)
    weight_moves = [
        remote(WS, WB.at[d], w_send.at[d - 1], w_recv.at[d - 1], (lax.rem(member + d, 8), slab)) for d in range(1, 8)
    ]

    def neighbours(level, u, z, n, lo, rows):
        c = coupling[level]
        mid = u[pl.ds(z, n), lo : lo + rows, :]
        total = c[0] * (u[pl.ds(z - 1, n), lo : lo + rows, :] + u[pl.ds(z + 1, n), lo : lo + rows, :])
        total += c[1] * (u[pl.ds(z, n), lo - 1 : lo + rows - 1, :] + u[pl.ds(z, n), lo + 1 : lo + rows + 1, :])
        if level == 0:
            total += left[0] * lane_roll(mid, 1) + right[0] * lane_roll(mid, -1)
        else:
            total += c[2] * (lane_roll(mid, 1) + lane_roll(mid, -1))
        return mid, total

    def over(z0, count, step, body):
        for z in range(z0, z0 + count, step):
            body(z)

    def sweep(level, u, s, d, z, n, lo, rows):
        mid, total = neighbours(level, u, z, n, lo, rows)
        return (1.0 - OMEGA) * mid + d[pl.ds(z, n), lo : lo + rows, :] * (s[pl.ds(z, n), lo : lo + rows, :] + total)

    def residual(level, u, s, dg, z, n, lo, rows):
        mid, total = neighbours(level, u, z, n, lo, rows)
        return s[pl.ds(z, n), lo : lo + rows, :] - dg[pl.ds(z, n), lo : lo + rows, :] * mid + total

    def restrict0(fine):
        def body(z):
            a = fine(z)
            for k in range(2):
                T0[(z - 2) // 2 + k] = a[2 * k] + a[2 * k + 1]

        over(2, 20, 4, body)

        def rows(i):
            e = T0[pl.ds(i, 5), pl.ds(0, 24, stride=2), :] + T0[pl.ds(i, 5), pl.ds(1, 24, stride=2), :]
            S1C[pl.ds(4 + i, 5), 8:32, :] = dot(flat(e), Rx[...]).reshape(5, 24, LANES)

        over(0, 10, 5, rows)

    def restrict1(fine, slot):
        def body(z):
            a = fine(z)
            for k in range(4):
                T1[(z - 1) // 2 + k, 4:28, :] = a[2 * k] + a[2 * k + 1]

        over(1, 16, 8, body)
        e = T1[:, pl.ds(0, 16, stride=2), :] + T1[:, pl.ds(1, 16, stride=2), :]
        own = jnp.concatenate([e[2], e[3], e[4], e[5]], axis=1)
        sides = jnp.concatenate([e[6], e[7], e[0], e[1]], axis=1)
        m = dot(jnp.concatenate([own, sides], axis=0), Rx1[...]).reshape(2, 16, LANES)
        G[slot, slab, 0:8, :] = m[0, 4:12]
        G[slot, slab, 8:16, :] = m[1, 4:12]
        for row, part in ((16, m[0, 12:14]), (18, m[1, 12:14]), (20, m[1, 2:4]), (22, m[0, 2:4])):
            G[slot, slab, row : row + 2, :] = part

    upper_half, row8 = lane >= 64, lax.broadcasted_iota(jnp.int32, (8, LANES), 0)
    nothing = jnp.zeros((8, LANES), F32)

    def gathered(slot):
        def rows(c, j, g):
            below = G[slot, 4 * c + j - 1, 16:24, :] if j > 0 else nothing
            above = G[slot, 4 * c + j + 1, 16:24, :] if j < 3 else nothing
            if g:
                below = pltpu.roll(below, 6, 0) if j > 0 else nothing
                above = pltpu.roll(above, 2, 0) if j < 3 else nothing
            near = jnp.where(row8 < 2, below, jnp.where(row8 >= 6, above, nothing))
            return G[slot, 4 * c + j, 8 * g : 8 * g + 8, :] + near

        for j in range(4):
            side = [nothing] + [rows(c, j, 1) for c in range(4)] + [nothing]
            for c in range(4):
                S2[c, 8 * j : 8 * j + 8, :] = rows(c, j, 0) + jnp.where(upper_half, side[c + 2], side[c])

    def restrict2(a):
        T2[...] = a
        e = T2[:, pl.ds(0, 16, stride=2), :] + T2[:, pl.ds(1, 16, stride=2), :]
        return dot(jnp.concatenate([e[0], e[1], e[2], e[3]], axis=1), R3[...])

    first_chunk, last_chunk = lane < 32, lane >= 96
    plane2 = jnp.zeros((1, 32, LANES), F32)

    def neighbours2():
        c = coupling[2]
        mid = U2[1:5, 8:40, :]
        up, down = lane_roll(mid, 32), lane_roll(mid, -32)
        before = jnp.where(first_chunk, jnp.concatenate([plane2, up[:3]], axis=0), up)
        after = jnp.where(last_chunk, jnp.concatenate([down[1:], plane2], axis=0), down)
        total = c[0] * (before + after) + c[1] * (U2[1:5, 7:39, :] + U2[1:5, 9:41, :])
        total += left[2] * lane_roll(mid, 1) + right[2] * lane_roll(mid, -1)
        return mid, total

    def sweep2():
        mid, total = neighbours2()
        U2[1:5, 8:40, :] = (1.0 - OMEGA) * mid + D2[...] * (S2[...] + total)

    row16 = lax.broadcasted_iota(jnp.int32, (16, LANES), 0)
    zeros16, ones16 = jnp.zeros((16, LANES), F32), jnp.ones((16, LANES), F32)
    up3 = jnp.where(row16 > 0, ones16, zeros16) * coupling[3][1]
    down3 = jnp.where(row16 < 15, ones16, zeros16) * coupling[3][1]
    before3 = lane_mask(lane >= 16) * coupling[3][0]
    after3 = lane_mask(lane < 112) * coupling[3][0]

    def coefficients3(d):
        for i, c in enumerate((before3, after3, up3, down3, left[3], right[3])):
            K3[i] = d * c
        D3[...] = d

    def level3(s):
        k = [K3[i] for i in range(6)]
        base = D3[...] * s
        u = base
        for _ in range(COARSE_SWEEPS - 1):
            z = k[0] * lane_roll(u, 16) + k[1] * lane_roll(u, -16)
            y = k[2] * pltpu.roll(u, 1, 0) + k[3] * pltpu.roll(u, 15, 0)
            x = k[4] * lane_roll(u, 1) + k[5] * lane_roll(u, -1)
            u = (base + (1.0 - OMEGA) * u + y) + (z + x)
        return u

    def inside(level, z, n, lo, rows):
        g = GEOMETRY[level]
        zi = lax.broadcasted_iota(jnp.int32, (n, rows, LANES), 0) + (z - g["own_z"] + g["nz"] * cz)
        yi = lax.broadcasted_iota(jnp.int32, (n, rows, LANES), 1) + (lo - g["own_y"] + g["ny"] * cy)
        keep = (zi >= 0) & (zi < 4 * g["nz"]) & (yi >= 0) & (yi < 4 * g["ny"])
        if level:
            keep = keep & (lax.broadcasted_iota(jnp.int32, (n, rows, LANES), 2) < 64)
        return keep

    finish(reaction_moves)
    own_reaction.wait()
    begin_halo0(1)
    SC[4:20, 16:48, :] = S0[1, 4:20, 16:48, :]
    restrict0(lambda z: SC[pl.ds(z, 4), 8:56, :])
    restrict1(lambda z: S1C[pl.ds(z, 8), 8:32, :], 1)
    begin(gather(1))
    begin_halo1(1)
    begin(volume_moves)
    begin(weight_moves)
    own_volume.wait()

    def summed1(slot):
        finish_near(halo1(slot))
        S1[1:17, 8:32, :] = S1C[1:17, 8:32, :]
        for k, (dz, dy) in enumerate(DIRECTIONS):
            z0, tiles = {-1: (12, 3), 0: (4, 5), 1: (0, 3)}[dz]
            y = {-1: slice(24, 32), 0: slice(8, 32), 1: slice(8, 16)}[dy]
            for p in range(tiles):
                both = landing1(k, slot)[p]
                for z, part in ((z0 + 2 * p, both), (z0 + 2 * p + 1, lane_roll(both, 64))):
                    if 1 <= z < 17:
                        S1[z, y, :] += jnp.where(upper_half, jnp.zeros_like(part), part)

    finish_halo0(1)

    def diag0(z):
        diag = S0[1, pl.ds(z, 2), 8:56, :] + center[0]
        DG0[pl.ds(z, 2), 8:56, :] = diag
        D0[pl.ds(z, 2), 8:56, :] = jnp.where(inside(0, z, 2, 8, 48), OMEGA / diag, jnp.zeros((2, 48, LANES), F32))

    over(1, 22, 2, diag0)
    summed1(1)

    def diag1(z):
        diag = S1[pl.ds(z, 2), 8:32, :] + center[1]
        DG1[pl.ds(z, 2), 8:32, :] = diag
        D1[pl.ds(z, 2), 8:32, :] = jnp.where(inside(1, z, 2, 8, 24), OMEGA / diag, jnp.zeros((2, 24, LANES), F32))

    over(1, 16, 2, diag1)
    finish(gather(1))
    gathered(1)
    DG2[...] = S2[...] + center[2]
    D2[...] = OMEGA / DG2[...]
    coefficients3(OMEGA / (restrict2(S2[...]) + center[3]))
    SC[4:20, 16:48, :] = jnp.ones((16, 32, LANES), F32)
    finish(volume_moves)
    finish(weight_moves)
    weight_total = WS[...]
    for d in range(1, 8):
        weight_total += WB[d]
    IW[...] = 1.0 / weight_total

    def vcycle(n, slot, use):
        UA[4:20, 16:48, :] = D0[4:20, 16:48, :] * SC[4:20, 16:48, :]

        def own0(z):
            UB[pl.ds(z, 3), 8:56, :] = sweep(0, UA, SC, D0, z, 3, 8, 48)

        over(3, 18, 3, own0)
        restrict0(lambda z: residual(0, UB, SC, DG0, z, 4, 8, 48))
        begin_halo1(slot)
        VA[4:14, 8:32, :] = D1[4:14, 8:32, :] * S1C[4:14, 8:32, :]

        def own1(z):
            VC[pl.ds(z, 6), 8:32, :] = sweep(1, VA, S1C, D1, z, 6, 8, 24)

        over(3, 12, 6, own1)
        restrict1(lambda z: residual(1, VC, S1C, DG1, z, 8, 8, 24), slot)
        begin(gather(slot))

        @pl.when(n > 0)
        def _():
            finish_halo0(slot)

        source0 = S0.at[slot]

        def first0(z):
            U0a[pl.ds(z, 2), 8:56, :] = D0[pl.ds(z, 2), 8:56, :] * source0[pl.ds(z, 2), 8:56, :]

        over(1, 22, 2, first0)

        def pre0(z):
            U0b[pl.ds(z, 4), 8:56, :] = sweep(0, U0a, source0, D0, z, 4, 8, 48)

        over(2, 20, 4, pre0)
        summed1(slot)
        U1a[1:17, 8:32, :] = D1[1:17, 8:32, :] * S1[1:17, 8:32, :]

        def pre1(z):
            U1b[pl.ds(z, 7), 8:32, :] = sweep(1, U1a, S1, D1, z, 7, 8, 24)

        over(2, 14, 7, pre1)

        finish(gather(slot))
        gathered(slot)
        U2[1:5, 8:40, :] = D2[...] * S2[...]
        sweep2()
        mid, total = neighbours2()
        u3 = level3(restrict2(S2[...] - DG2[...] * mid + total))
        p = dot(u3, P3[...])
        for k in range(4):
            C2[k, pl.ds(0, 16, stride=2), :] = p[:, LANES * k : LANES * k + LANES]
            C2[k, pl.ds(1, 16, stride=2), :] = p[:, LANES * k : LANES * k + LANES]
        U2[1:5, 8:40, :] += C2[...]
        sweep2()
        sweep2()

        window = pl.ds(pl.multiple_of(8 * cy, 8), 24)
        own = U2[1 + cz, window, :][4:20]
        sides = jnp.where(upper_half, U2[cz, window, :][4:20], U2[2 + cz, window, :][4:20])
        wide = dot(jnp.concatenate([own, sides], axis=0), E1[...])
        for k in range(8):
            r, q = (0, k - 2) if 2 <= k < 6 else (16, (k - 2) % 4)
            C1[k, pl.ds(0, 16, stride=2), :] = wide[r : r + 16, LANES * q : LANES * q + LANES]
            C1[k, pl.ds(1, 16, stride=2), :] = wide[r : r + 16, LANES * q : LANES * q + LANES]
        for k in range(8):
            U1b[1 + 2 * k, 8:32, :] += C1[k, 4:28, :]
            U1b[2 + 2 * k, 8:32, :] += C1[k, 4:28, :]

        def post1a(z):
            U1a[pl.ds(z, 6), 8:32, :] = sweep(1, U1b, S1, D1, z, 6, 8, 24)

        over(3, 12, 6, post1a)

        def post1b(z):
            U1b[pl.ds(z, 5), 8:32, :] = sweep(1, U1a, S1, D1, z, 5, 8, 24)

        over(4, 10, 5, post1b)

        def widen0(i):
            wide = dot(flat(U1b[pl.ds(4 + i, 5), 8:32, :]), Px[...]).reshape(5, 24, LANES)
            C0[:, pl.ds(0, 24, stride=2), :] = wide
            C0[:, pl.ds(1, 24, stride=2), :] = wide
            for k in range(5):
                U0b[2 + 2 * (i + k), 8:56, :] += C0[k]
                U0b[3 + 2 * (i + k), 8:56, :] += C0[k]

        over(0, 10, 5, widen0)

        def post0a(z):
            U0a[pl.ds(z, 3), 8:56, :] = sweep(0, U0b, source0, D0, z, 3, 8, 48)

        over(3, 18, 3, post0a)

        def post0b(z):
            use(z, sweep(0, U0a, source0, D0, z, 4, 16, 32))

        over(4, 16, 4, post0b)

    def centroid(last):
        sibling = (member + 1 - 2 * mc, slab)

        def marginal(at):
            m = S0[0, pl.ds(4 + at, 4), 16:48, :] * MB[pl.ds(at, 4)]
            MB[pl.ds(at, 4)] = m
            LB[pl.ds(at, 4)] = weight_ref[0] * jnp.log(m)

        def update(at):
            p = S0[0, 4 + at, 16:48, :] * CB[at] / MB[at]
            S0[0, 4 + at, 16:48, :] = p
            SC[4 + at, 16:48, :] = p

        def along_x(d):
            return (2 * lax.rem(mx + d, 4) + mc, slab)

        swaps, pieces, spread, passed = [], [], [], []
        for q in range(2):
            marginal(8 * q + 4 * (1 - mc))
            theirs, here = LB.at[pl.ds(8 * q + 4 * (1 - mc), 4)], XB.at[pl.ds(4 * q, 4)]
            swaps.append(remote(theirs, here, x_send.at[q], x_recv.at[q], sibling))
            swaps[q].start()
        for q in range(2):
            marginal(8 * q + 4 * mc)
        for q in range(2):
            swaps[q].wait_recv()
            HB[4 * q : 4 * q + 4] = LB[pl.ds(8 * q + 4 * mc, 4)] + XB[4 * q : 4 * q + 4]
            pieces.append([])
            for d in (2, 1, 3):
                part = HB.at[pl.ds(4 * q + lax.rem(mx + d, 4), 1)]
                pieces[q].append(remote(part, PB.at[q, d - 1], p_send.at[q, d - 1], p_recv.at[q, d - 1], along_x(d)))
            begin(pieces[q])
        inverse = jnp.broadcast_to(IW[...][None], (4, 8, LANES)).reshape(1, 32, LANES)
        for q in range(2):
            for c in pieces[q]:
                c.wait_recv()
            total = HB[pl.ds(4 * q + mx, 1)] + PB[q, 0] + PB[q, 1] + PB[q, 2]
            own = 8 * q + 4 * mc + mx
            CB[pl.ds(own, 1)] = jnp.exp(total * inverse)
            made = CB.at[pl.ds(own, 1)]
            spread.append([remote(made, made, c_send.at[q, d - 1], c_recv.at[q, d - 1], along_x(d)) for d in (2, 1, 3)])
            begin(spread[q])
            passed.append([])
            for d in (0, 1, 3, 2):
                at = CB.at[pl.ds(8 * q + 4 * mc + lax.rem(mx - d + 4, 4), 1)]
                passed[q].append((d, remote(at, at, f_send.at[q, d], f_recv.at[q, d], sibling)))
            passed[q][0][1].start()
            update(own)
        for q in range(2):
            for (d, c), arrived in zip(passed[q][1:], spread[q][1:] + spread[q][:1]):
                arrived.wait_recv()
                c.start()
                update(8 * q + 4 * mc + lax.rem(mx - d + 4, 4))
        for d in range(1, 4):
            to = lax.rem(cy + d, 4)
            pl.when(last & (lax.rem(to, 2) == mc))(multiplier_moves()[d - 1].start)
        for q in range(2):
            for d, c in passed[q]:
                c.wait_recv()
                update(8 * q + 4 * (1 - mc) + lax.rem(mx - d + 4, 4))
        for d in range(1, 4):
            to = lax.rem(cy + d, 4)
            pl.when(last & (lax.rem(to, 2) != mc))(multiplier_moves()[d - 1].start)
        pl.when(last)(lambda: begin(centroid_moves()))
        for q in range(2):
            for c in [swaps[q]] + pieces[q] + spread[q] + [f for _, f in passed[q]]:
                c.wait_send()

    def multiplier_moves():
        return to_slabs(S0.at[0], 4, 16, mult_out, o_send.at[1], o_recv.at[1])

    def centroid_moves():
        copies = []
        for d in range(1, 4):
            to = lax.rem(cy + d, 4)
            copies.append(
                remote(
                    CB.at[pl.ds(4 * to + 2 * mc, 2)],
                    cent_out.at[pl.ds(2 * mc, 2), pl.ds(pl.multiple_of(32 * cy, 32), 32)],
                    o_send.at[0, d - 1], o_recv.at[0, d - 1], (member, cz * 4 + to),
                )
            )
        return copies

    def half_step(n, _):
        slot = lax.rem(n, 2)

        def keep(z, h):
            MB[pl.ds(z - 4, 4)] = h

        vcycle(n, slot, keep)

        @pl.when(slot == 0)
        def _():
            def partner(z):
                p = VB[pl.ds(z - 4, 4)] / MB[pl.ds(z - 4, 4)]
                S0[1, pl.ds(z, 4), 16:48, :] = p
                SC[pl.ds(z, 4), 16:48, :] = p

            over(4, 16, 4, partner)

        @pl.when(slot == 1)
        def _():
            centroid(n == 2 * ITERS - 1)

        @pl.when(n < 2 * ITERS - 1)
        def _():
            begin_halo0(1 - slot)

        return 0

    lax.fori_loop(0, 2 * ITERS, half_step, 0)

    mult_out[:, mine, :] = S0[0, pl.ds(4 + 4 * cy, 4), 16:48, :]
    cent_out[pl.ds(2 * mc, 2), mine, :] = CB[pl.ds(4 * cy + 2 * mc, 2)]
    finish(centroid_moves())
    half_out = cent_out.at[pl.ds(2 * mc, 2)]
    across = remote(half_out, half_out, x_send.at[0], x_recv.at[0], (member + 1 - 2 * mc, slab))
    across.start()
    finish(multiplier_moves())
    across.wait()


def body(nonnegative_volumes, reaction, diffusivity, member_weights):
    vmem, smem = pl.BlockSpec(memory_space=pltpu.VMEM), pl.BlockSpec(memory_space=pltpu.SMEM)
    hbm = pl.BlockSpec(memory_space=pl.ANY)
    field = jax.ShapeDtypeStruct((4, 128, 128), F32)

    def buffer(*shape):
        return pltpu.VMEM((*shape, LANES), F32)

    dma = pltpu.SemaphoreType.DMA
    scratch = [
        buffer(2, 24, 64), *[buffer(24, 64) for _ in range(7)], buffer(5, 48), buffer(10, 48),
        *[buffer(18, 40) for _ in range(8)], buffer(8, 32), buffer(8, 32), buffer(5, 24),
        buffer(2, 2, 3, 24), buffer(2, 2, 5, 8), buffer(2, 4, 3, 8), buffer(2, 8, 8), buffer(2, 2, 8, 8), buffer(2, 4, 2, 8),
        buffer(2, 16, 24), buffer(4, 32), buffer(4, 32), buffer(4, 32), buffer(6, 48), buffer(4, 32), buffer(4, 32), buffer(16), buffer(6, 16),
        buffer(16, 32), buffer(16, 32), buffer(16, 32), buffer(8, 32), buffer(8, 32), buffer(2, 3, 1, 32), buffer(16, 32),
        buffer(8), buffer(8, 8), buffer(8),
        *[pltpu.VMEM(shape, BF16) for shape in ((128, 128), (512, 128), (512, 128), (128, 512), (128, 512), (128, 128))],
        dma((2, 8)), dma((2, 8)), dma((2, 8)), dma((2, 8)), dma((2, 16)), dma((2, 16)),
        dma((3,)), dma((3,)), dma((3,)), dma((3,)), dma((7,)), dma((7,)),
        dma((2,)), dma((2,)), dma((2,)), *[dma((2, 3)) for _ in range(4)], dma((2, 4)), dma((2, 4)), dma((2, 3)), dma((2, 3)),
    ]
    centroid, multipliers = pl.pallas_call(
        kernel,
        out_shape=(field, field),
        in_specs=[hbm, hbm, smem, smem],
        out_specs=(vmem, vmem),
        scratch_shapes=scratch,
        compiler_params=pltpu.CompilerParams(collective_id=0, has_side_effects=True, vmem_limit_bytes=40 * 2**20),
    )(nonnegative_volumes[0], reaction, diffusivity, member_weights)
    return centroid, multipliers[None]


def solution(mesh):
    return jax.shard_map(
        body,
        mesh=mesh,
        in_specs=(P("member", "slab", None, None), P("slab", None, None), P(), P("member")),
        out_specs=(P("slab", None, None), P("member", "slab", None, None)),
        check_vma=False,
    )
```

```python
import jax
import jax.numpy as jnp
from jax import lax
from jax.experimental import pallas as pl
from jax.experimental.pallas import tpu as pltpu
from jax.sharding import PartitionSpec as P

ITERS = 3
COARSE_SWEEPS = 8
OMEGA = 0.8
LANES = 128
NZ, NY = 64, 128
F32, BF16 = jnp.float32, jnp.bfloat16
MESH = pl.DeviceIdType.MESH
FARTHEST = sorted(range(1, 16), key=lambda d: -min(d // 4, 4 - d // 4) - min(d % 4, 4 - d % 4))
DIRECTIONS = ((-1, 0), (1, 0), (0, -1), (0, 1), (-1, -1), (-1, 1), (1, -1), (1, 1))

GEOMETRY = (dict(own_z=4, own_y=16, nz=16, ny=32), dict(own_z=5, own_y=12, nz=8, ny=16))


def dot(a, b):
    high = a.astype(BF16)
    low = (a - high.astype(F32)).astype(BF16)
    return jnp.dot(high, b, preferred_element_type=F32) + jnp.dot(low, b, preferred_element_type=F32)


def flat(a):
    return a.reshape(-1, LANES)


def lane_roll(a, shift):
    return pltpu.roll(flat(a), shift % LANES, 1).reshape(a.shape)


def kernel(
    vol_ref, reaction_ref, diff_ref, weight_ref, cent_out, mult_out,
    S0, SC, D0, DG0, UA, UB, U0a, U0b, C0, T0,
    S1, S1C, D1, DG1, VA, VC, U1a, U1b, C1, T1, P1, LZ, LY, LD, E0, LE, LQ,
    G, S2, D2, DG2, U2, T2, C2, D3, K3,
    VB, MB, LB, XB, HB, PB, CB, WS, WB, IW,
    Rx, Rx1, R3, P3, E1, Px,
    h0_send, h0_recv, h1_send, h1_recv, g_send, g_recv,
    ra_send, ra_recv, va_send, va_recv, w_send, w_recv,
    l_sem, x_send, x_recv, p_send, p_recv, c_send, c_recv, f_send, f_recv, o_send, o_recv, e_send, e_recv, k_send, k_recv,
):
    member, slab = lax.axis_index("member"), lax.axis_index("slab")
    cz, cy = slab // 4, lax.rem(slab, 4)
    mx, mc = member // 2, lax.rem(member, 2)

    def at_slab(dz, dy):
        return lax.rem(cz + dz + 4, 4) * 4 + lax.rem(cy + dy + 4, 4)

    def remote(src, dst, send, recv, to):
        return pltpu.make_async_remote_copy(
            src_ref=src, dst_ref=dst, send_sem=send, recv_sem=recv, device_id=to, device_id_type=MESH
        )

    for ref in (LZ, LY, LD, LE, LQ):
        ref[...] = jnp.zeros(ref.shape, F32)
    S0[...] = jnp.ones(S0.shape, F32)
    mine = pl.ds(pl.multiple_of(32 * cy, 32), 32)
    own_reaction = pltpu.make_async_copy(reaction_ref.at[:, mine], S0.at[1, pl.ds(4 + 4 * cy, 4), pl.ds(16, 32)], l_sem.at[0])
    own_volume = pltpu.make_async_copy(vol_ref.at[:, mine], VB.at[pl.ds(4 * cy, 4)], l_sem.at[1])
    own_reaction.start()
    own_volume.start()

    barrier = pltpu.get_barrier_semaphore()
    for d in FARTHEST:
        pl.semaphore_signal(barrier, inc=1, device_id=(member, at_slab(d // 4, d % 4)), device_id_type=MESH)
    for d in range(1, 8):
        pl.semaphore_signal(barrier, inc=1, device_id=(lax.rem(member + d, 8), slab), device_id_type=MESH)

    coupling = [[diff_ref[i] * (0.25**level) for i in range(3)] for level in range(4)]
    center = [2.0 * (c[0] + c[1] + c[2]) for c in coupling]

    lane = lax.broadcasted_iota(jnp.int32, (1, LANES), 1)
    one, zero = jnp.ones((1, LANES), F32), jnp.zeros((1, LANES), F32)

    def lane_mask(keep):
        return jnp.where(keep, one, zero)

    row_i = lax.broadcasted_iota(jnp.int32, (LANES, LANES), 0)
    col_i = lax.broadcasted_iota(jnp.int32, (LANES, LANES), 1)

    def half(a):
        return lax.shift_right_logical(a, 1)

    def matrix(keep, value=1.0):
        return jnp.where(keep, jnp.full((LANES, LANES), value, F32), jnp.zeros((LANES, LANES), F32)).astype(BF16)

    Rx[...] = matrix(half(row_i) == col_i, 0.125)
    Px[...] = matrix(row_i == half(col_i))
    for q in range(4):
        block = slice(LANES * q, LANES * q + LANES)
        Rx1[block, :] = matrix((row_i < 64) & (half(row_i) + 32 * q == col_i), 0.125)
        E1[:, block] = matrix((col_i < 64) & (row_i == half(col_i) + 32 * q))
        R3[block, :] = matrix(16 * (2 * q + lax.shift_right_logical(row_i, 6)) + half(row_i & 31) == col_i, 0.125)
        P3[:, block] = matrix(16 * (2 * q + lax.shift_right_logical(col_i, 6)) + half(col_i & 31) == row_i)

    left = [lane_mask(lane > 0) * coupling[0][2], None, lane_mask((lane & 31) > 0) * coupling[2][2], lane_mask((lane & 15) > 0) * coupling[3][2]]
    right = [lane_mask(lane < 127) * coupling[0][2], None, lane_mask((lane & 31) < 31) * coupling[2][2], lane_mask((lane & 15) < 15) * coupling[3][2]]
    WS[...] = jnp.full((8, LANES), weight_ref[0], F32)
    for ref in (SC, UA, UB, VA, VC, S1C, U0a, U0b, U1a, U1b, U2, T1):
        ref[...] = jnp.zeros(ref.shape, F32)
    pl.semaphore_wait(barrier, 22)

    def inner(dz, dy):
        return (cz + dz >= 0) & (cz + dz < 4) & (cy + dy >= 0) & (cy + dy < 4)

    def halo0(slot):
        copies = []
        for k, (dz, dy) in enumerate(DIRECTIONS):
            if dy == 0:
                zs, zd = (4, 20) if dz < 0 else (17, 1)
                src, dst = S0.at[slot, pl.ds(zs, 3), pl.ds(16, 32)], S0.at[slot, pl.ds(zd, 3), pl.ds(16, 32)]
            elif dz == 0:
                src, dst = E0.at[(dy + 1) // 2], LE.at[slot, k - 2]
            else:
                src, dst = E0.at[(dy + 1) // 2, pl.ds(0 if dz < 0 else 7, 1)], LQ.at[slot, k - 4]
            copies.append((
                dz, dy, remote(src, dst, h0_send.at[slot, k], h0_recv.at[slot, k], (member, at_slab(dz, dy)))
            ))
        return copies

    def begin_halo0(slot):
        for edge, row in ((0, 16), (1, 44)):
            for p in range(8):
                E0[edge, p, 0:4, :] = S0[slot, 4 + 2 * p, row : row + 4, :]
                E0[edge, p, 4:8, :] = S0[slot, 5 + 2 * p, row : row + 4, :]
        begin_near(halo0(slot))

    def finish_halo0(slot):
        finish_near(halo0(slot))
        for k, (dz, dy) in enumerate(DIRECTIONS):
            if dy == 0:
                continue
            row, z0, tiles = (48 if dy < 0 else 12), {-1: 20, 0: 4, 1: 2}[dz], 8 if dz == 0 else 1
            for p in range(tiles):
                tile = LE[slot, k - 2, p] if dz == 0 else LQ[slot, k - 4, p]
                S0[slot, z0 + 2 * p, row : row + 4, :] = tile[0:4]
                S0[slot, z0 + 2 * p + 1, row : row + 4, :] = tile[4:8]

    def landing1(k, slot):
        if k < 2:
            return LZ.at[slot, k]
        return LY.at[slot, k - 2] if k < 4 else LD.at[slot, k - 4]

    def halo1(slot):
        copies = []
        for k, (dz, dy) in enumerate(DIRECTIONS):
            z = {-1: pl.ds(0, 3), 0: pl.ds(0, 5), 1: pl.ds(2, 3)}[dz]
            y = {-1: pl.ds(0, 8), 0: pl.ds(0, 24), 1: pl.ds(16, 8)}[dy]
            copies.append((
                dz, dy,
                remote(
                    P1.at[z, y], landing1(k, slot),
                    h1_send.at[slot, k], h1_recv.at[slot, k], (member, at_slab(dz, dy)),
                ),
            ))
        return copies

    def begin_near(copies):
        for dz, dy, c in copies:
            pl.when(inner(dz, dy))(c.start)

    def begin_halo1(slot):
        for p in range(5):
            P1[p] = S1C[4 + 2 * p, 8:32, :] + lane_roll(S1C[5 + 2 * p, 8:32, :], 64)
        begin_near(halo1(slot))

    def finish_near(copies):
        for dz, dy, c in copies:
            pl.when(inner(-dz, -dy))(c.wait_recv)
        for dz, dy, c in copies:
            pl.when(inner(dz, dy))(c.wait_send)

    def gather(slot):
        return [
            remote(
                G.at[slot, slab], G.at[slot, slab],
                g_send.at[slot], g_recv.at[slot], (member, at_slab(d // 4, d % 4)),
            )
            for d in FARTHEST
        ]

    def finish_gather(slot):
        all_of_them = G.at[slot, 0:15]
        pltpu.make_async_copy(all_of_them, all_of_them, g_recv.at[slot]).wait()

    def finish_gather_sends(slot):
        all_of_them = G.at[slot, 0:15]
        pltpu.make_async_copy(all_of_them, all_of_them, g_send.at[slot]).wait()

    def begin(copies):
        for c in copies:
            c.start()

    def finish(copies):
        for c in copies:
            c.wait()

    def to_blocks(src, dst, dst_z, dst_y, send, recv):
        copies = []
        for d in range(1, 4):
            to = lax.rem(cy + d, 4)
            copies.append(
                remote(
                    src.at[:, pl.ds(pl.multiple_of(32 * to, 32), 32)],
                    dst.at[pl.ds(dst_z + 4 * cy, 4), pl.ds(dst_y, 32)],
                    send.at[d - 1], recv.at[d - 1], (member, cz * 4 + to),
                )
            )
        return copies

    def to_slabs(src, src_z, src_y, dst, send, recv):
        copies = []
        for d in range(1, 4):
            to = lax.rem(cy + d, 4)
            copies.append(
                remote(
                    src.at[pl.ds(src_z + 4 * to, 4), pl.ds(src_y, 32)],
                    dst.at[:, pl.ds(pl.multiple_of(32 * cy, 32), 32)],
                    send.at[d - 1], recv.at[d - 1], (member, cz * 4 + to),
                )
            )
        return copies

    reaction_moves = to_blocks(reaction_ref, S0.at[1], 4, 16, ra_send, ra_recv)
    volume_moves = to_blocks(vol_ref, VB, 0, 0, va_send, va_recv)
    begin(reaction_moves)
    weight_moves = [
        remote(WS, WB.at[d], w_send.at[d - 1], w_recv.at[d - 1], (lax.rem(member + d, 8), slab)) for d in range(1, 8)
    ]

    def neighbours(level, u, z, n, lo, rows):
        c = coupling[level]
        mid = u[pl.ds(z, n), lo : lo + rows, :]
        total = c[0] * (u[pl.ds(z - 1, n), lo : lo + rows, :] + u[pl.ds(z + 1, n), lo : lo + rows, :])
        total += c[1] * (u[pl.ds(z, n), lo - 1 : lo + rows - 1, :] + u[pl.ds(z, n), lo + 1 : lo + rows + 1, :])
        if level == 0:
            total += left[0] * lane_roll(mid, 1) + right[0] * lane_roll(mid, -1)
        else:
            total += c[2] * (lane_roll(mid, 1) + lane_roll(mid, -1))
        return mid, total

    def over(z0, count, step, body):
        for z in range(z0, z0 + count, step):
            body(z)

    def sweep(level, u, s, d, z, n, lo, rows):
        mid, total = neighbours(level, u, z, n, lo, rows)
        return (1.0 - OMEGA) * mid + d[pl.ds(z, n), lo : lo + rows, :] * (s[pl.ds(z, n), lo : lo + rows, :] + total)

    def residual(level, u, s, dg, z, n, lo, rows):
        mid, total = neighbours(level, u, z, n, lo, rows)
        return s[pl.ds(z, n), lo : lo + rows, :] - dg[pl.ds(z, n), lo : lo + rows, :] * mid + total

    def restrict0(fine):
        def body(z):
            a = fine(z)
            for k in range(2):
                T0[(z - 2) // 2 + k] = a[2 * k] + a[2 * k + 1]

        over(2, 20, 4, body)

        def rows(i):
            e = T0[pl.ds(i, 5), pl.ds(0, 24, stride=2), :] + T0[pl.ds(i, 5), pl.ds(1, 24, stride=2), :]
            S1C[pl.ds(4 + i, 5), 8:32, :] = dot(flat(e), Rx[...]).reshape(5, 24, LANES)

        over(0, 10, 5, rows)

    def restrict1(fine, slot):
        def body(z):
            a = fine(z)
            for k in range(4):
                T1[(z - 1) // 2 + k, 4:28, :] = a[2 * k] + a[2 * k + 1]

        over(1, 16, 8, body)
        e = T1[:, pl.ds(0, 16, stride=2), :] + T1[:, pl.ds(1, 16, stride=2), :]
        own = jnp.concatenate([e[2], e[3], e[4], e[5]], axis=1)
        sides = jnp.concatenate([e[6], e[7], e[0], e[1]], axis=1)
        m = dot(jnp.concatenate([own, sides], axis=0), Rx1[...]).reshape(2, 16, LANES)
        G[slot, slab, 0:8, :] = m[0, 4:12]
        G[slot, slab, 8:16, :] = m[1, 4:12]
        for row, part in ((16, m[0, 12:14]), (18, m[1, 12:14]), (20, m[1, 2:4]), (22, m[0, 2:4])):
            G[slot, slab, row : row + 2, :] = part

    upper_half, row8 = lane >= 64, lax.broadcasted_iota(jnp.int32, (8, LANES), 0)
    nothing = jnp.zeros((8, LANES), F32)

    def gathered(slot):
        def rows(c, j, g):
            below = G[slot, 4 * c + j - 1, 16:24, :] if j > 0 else nothing
            above = G[slot, 4 * c + j + 1, 16:24, :] if j < 3 else nothing
            if g:
                below = pltpu.roll(below, 6, 0) if j > 0 else nothing
                above = pltpu.roll(above, 2, 0) if j < 3 else nothing
            near = jnp.where(row8 < 2, below, jnp.where(row8 >= 6, above, nothing))
            return G[slot, 4 * c + j, 8 * g : 8 * g + 8, :] + near

        for j in range(4):
            side = [nothing] + [rows(c, j, 1) for c in range(4)] + [nothing]
            for c in range(4):
                S2[c, 8 * j : 8 * j + 8, :] = rows(c, j, 0) + jnp.where(upper_half, side[c + 2], side[c])

    def restrict2(a):
        T2[...] = a
        e = T2[:, pl.ds(0, 16, stride=2), :] + T2[:, pl.ds(1, 16, stride=2), :]
        return dot(jnp.concatenate([e[0], e[1], e[2], e[3]], axis=1), R3[...])

    first_chunk, last_chunk = lane < 32, lane >= 96
    plane2 = jnp.zeros((1, 32, LANES), F32)

    def neighbours2():
        c = coupling[2]
        mid = U2[1:5, 8:40, :]
        up, down = lane_roll(mid, 32), lane_roll(mid, -32)
        before = jnp.where(first_chunk, jnp.concatenate([plane2, up[:3]], axis=0), up)
        after = jnp.where(last_chunk, jnp.concatenate([down[1:], plane2], axis=0), down)
        total = c[0] * (before + after) + c[1] * (U2[1:5, 7:39, :] + U2[1:5, 9:41, :])
        total += left[2] * lane_roll(mid, 1) + right[2] * lane_roll(mid, -1)
        return mid, total

    def sweep2():
        mid, total = neighbours2()
        U2[1:5, 8:40, :] = (1.0 - OMEGA) * mid + D2[...] * (S2[...] + total)

    row16 = lax.broadcasted_iota(jnp.int32, (16, LANES), 0)
    zeros16, ones16 = jnp.zeros((16, LANES), F32), jnp.ones((16, LANES), F32)
    up3 = jnp.where(row16 > 0, ones16, zeros16) * coupling[3][1]
    down3 = jnp.where(row16 < 15, ones16, zeros16) * coupling[3][1]
    before3 = lane_mask(lane >= 16) * coupling[3][0]
    after3 = lane_mask(lane < 112) * coupling[3][0]

    def coefficients3(d):
        for i, c in enumerate((before3, after3, up3, down3, left[3], right[3])):
            K3[i] = d * c
        D3[...] = d

    def level3(s):
        k = [K3[i] for i in range(6)]
        base = D3[...] * s
        u = base
        for _ in range(COARSE_SWEEPS - 1):
            z = k[0] * lane_roll(u, 16) + k[1] * lane_roll(u, -16)
            y = k[2] * pltpu.roll(u, 1, 0) + k[3] * pltpu.roll(u, 15, 0)
            x = k[4] * lane_roll(u, 1) + k[5] * lane_roll(u, -1)
            u = (base + (1.0 - OMEGA) * u + y) + (z + x)
        return u

    def inside(level, z, n, lo, rows):
        g = GEOMETRY[level]
        zi = lax.broadcasted_iota(jnp.int32, (n, rows, LANES), 0) + (z - g["own_z"] + g["nz"] * cz)
        yi = lax.broadcasted_iota(jnp.int32, (n, rows, LANES), 1) + (lo - g["own_y"] + g["ny"] * cy)
        keep = (zi >= 0) & (zi < 4 * g["nz"]) & (yi >= 0) & (yi < 4 * g["ny"])
        if level:
            keep = keep & (lax.broadcasted_iota(jnp.int32, (n, rows, LANES), 2) < 64)
        return keep

    finish(reaction_moves)
    own_reaction.wait()
    begin_halo0(1)
    SC[4:20, 16:48, :] = S0[1, 4:20, 16:48, :]
    restrict0(lambda z: SC[pl.ds(z, 4), 8:56, :])
    restrict1(lambda z: S1C[pl.ds(z, 8), 8:32, :], 1)
    begin(gather(1))
    begin_halo1(1)
    begin(volume_moves)
    begin(weight_moves)
    own_volume.wait()

    def summed1(slot):
        finish_near(halo1(slot))
        S1[1:17, 8:32, :] = S1C[1:17, 8:32, :]
        for k, (dz, dy) in enumerate(DIRECTIONS):
            z0, tiles = {-1: (12, 3), 0: (4, 5), 1: (0, 3)}[dz]
            y = {-1: slice(24, 32), 0: slice(8, 32), 1: slice(8, 16)}[dy]
            for p in range(tiles):
                both = landing1(k, slot)[p]
                for z, part in ((z0 + 2 * p, both), (z0 + 2 * p + 1, lane_roll(both, 64))):
                    if 1 <= z < 17:
                        S1[z, y, :] += jnp.where(upper_half, jnp.zeros_like(part), part)

    finish_halo0(1)

    def diag0(z):
        diag = S0[1, pl.ds(z, 2), 8:56, :] + center[0]
        DG0[pl.ds(z, 2), 8:56, :] = diag
        D0[pl.ds(z, 2), 8:56, :] = jnp.where(inside(0, z, 2, 8, 48), OMEGA / diag, jnp.zeros((2, 48, LANES), F32))

    over(1, 22, 2, diag0)
    summed1(1)

    def diag1(z):
        diag = S1[pl.ds(z, 2), 8:32, :] + center[1]
        DG1[pl.ds(z, 2), 8:32, :] = diag
        D1[pl.ds(z, 2), 8:32, :] = jnp.where(inside(1, z, 2, 8, 24), OMEGA / diag, jnp.zeros((2, 24, LANES), F32))

    over(1, 16, 2, diag1)
    finish_gather(1)
    finish_gather_sends(1)
    gathered(1)
    DG2[...] = S2[...] + center[2]
    D2[...] = OMEGA / DG2[...]
    coefficients3(OMEGA / (restrict2(S2[...]) + center[3]))
    SC[4:20, 16:48, :] = jnp.ones((16, 32, LANES), F32)
    finish(volume_moves)
    finish(weight_moves)
    weight_total = WS[...]
    for d in range(1, 8):
        weight_total += WB[d]
    IW[...] = 1.0 / weight_total

    def vcycle(n, slot, use):
        UA[4:20, 16:48, :] = D0[4:20, 16:48, :] * SC[4:20, 16:48, :]

        def own0(z):
            UB[pl.ds(z, 3), 8:56, :] = sweep(0, UA, SC, D0, z, 3, 8, 48)

        over(3, 18, 3, own0)
        restrict0(lambda z: residual(0, UB, SC, DG0, z, 4, 8, 48))
        begin_halo1(slot)
        VA[4:14, 8:32, :] = D1[4:14, 8:32, :] * S1C[4:14, 8:32, :]

        def own1(z):
            VC[pl.ds(z, 6), 8:32, :] = sweep(1, VA, S1C, D1, z, 6, 8, 24)

        over(3, 12, 6, own1)
        restrict1(lambda z: residual(1, VC, S1C, DG1, z, 8, 8, 24), slot)
        begin(gather(slot))

        @pl.when(n > 0)
        def _():
            finish_halo0(slot)

        source0 = S0.at[slot]

        def first0(z):
            U0a[pl.ds(z, 2), 8:56, :] = D0[pl.ds(z, 2), 8:56, :] * source0[pl.ds(z, 2), 8:56, :]

        over(1, 22, 2, first0)

        def pre0(z):
            U0b[pl.ds(z, 4), 8:56, :] = sweep(0, U0a, source0, D0, z, 4, 8, 48)

        over(2, 20, 4, pre0)
        summed1(slot)
        U1a[1:17, 8:32, :] = D1[1:17, 8:32, :] * S1[1:17, 8:32, :]

        def pre1(z):
            U1b[pl.ds(z, 7), 8:32, :] = sweep(1, U1a, S1, D1, z, 7, 8, 24)

        over(2, 14, 7, pre1)

        finish_gather(slot)
        gathered(slot)
        U2[1:5, 8:40, :] = D2[...] * S2[...]
        sweep2()
        mid, total = neighbours2()
        u3 = level3(restrict2(S2[...] - DG2[...] * mid + total))
        p = dot(u3, P3[...])
        for k in range(4):
            C2[k, pl.ds(0, 16, stride=2), :] = p[:, LANES * k : LANES * k + LANES]
            C2[k, pl.ds(1, 16, stride=2), :] = p[:, LANES * k : LANES * k + LANES]
        U2[1:5, 8:40, :] += C2[...]
        sweep2()
        sweep2()

        finish_gather_sends(slot)

        window = pl.ds(pl.multiple_of(8 * cy, 8), 24)
        own = U2[1 + cz, window, :][4:20]
        sides = jnp.where(upper_half, U2[cz, window, :][4:20], U2[2 + cz, window, :][4:20])
        wide = dot(jnp.concatenate([own, sides], axis=0), E1[...])
        for k in range(8):
            r, q = (0, k - 2) if 2 <= k < 6 else (16, (k - 2) % 4)
            C1[k, pl.ds(0, 16, stride=2), :] = wide[r : r + 16, LANES * q : LANES * q + LANES]
            C1[k, pl.ds(1, 16, stride=2), :] = wide[r : r + 16, LANES * q : LANES * q + LANES]
        for k in range(8):
            U1b[1 + 2 * k, 8:32, :] += C1[k, 4:28, :]
            U1b[2 + 2 * k, 8:32, :] += C1[k, 4:28, :]

        def post1a(z):
            U1a[pl.ds(z, 6), 8:32, :] = sweep(1, U1b, S1, D1, z, 6, 8, 24)

        over(3, 12, 6, post1a)

        def post1b(z):
            U1b[pl.ds(z, 5), 8:32, :] = sweep(1, U1a, S1, D1, z, 5, 8, 24)

        over(4, 10, 5, post1b)

        def widen0(i):
            wide = dot(flat(U1b[pl.ds(4 + i, 5), 8:32, :]), Px[...]).reshape(5, 24, LANES)
            C0[:, pl.ds(0, 24, stride=2), :] = wide
            C0[:, pl.ds(1, 24, stride=2), :] = wide
            for k in range(5):
                U0b[2 + 2 * (i + k), 8:56, :] += C0[k]
                U0b[3 + 2 * (i + k), 8:56, :] += C0[k]

        over(0, 10, 5, widen0)

        def post0a(z):
            U0a[pl.ds(z, 3), 8:56, :] = sweep(0, U0b, source0, D0, z, 3, 8, 48)

        over(3, 18, 3, post0a)

        def post0b(z):
            use(z, sweep(0, U0a, source0, D0, z, 4, 16, 32))

        over(4, 16, 4, post0b)

    def centroid(last):
        sibling = (member + 1 - 2 * mc, slab)

        def marginal(at):
            m = S0[0, pl.ds(4 + at, 4), 16:48, :] * MB[pl.ds(at, 4)]
            MB[pl.ds(at, 4)] = m
            LB[pl.ds(at, 4)] = weight_ref[0] * jnp.log(m)

        def update(at):
            p = S0[0, 4 + at, 16:48, :] * CB[at] / MB[at]
            S0[0, 4 + at, 16:48, :] = p
            SC[4 + at, 16:48, :] = p

        def along_x(d):
            return (2 * lax.rem(mx + d, 4) + mc, slab)

        swaps, pieces, spread, passed = [], [], [], []
        for q in range(2):
            marginal(8 * q + 4 * (1 - mc))
            theirs, here = LB.at[pl.ds(8 * q + 4 * (1 - mc), 4)], XB.at[pl.ds(4 * q, 4)]
            swaps.append(remote(theirs, here, x_send.at[q], x_recv.at[q], sibling))
            swaps[q].start()
        for q in range(2):
            marginal(8 * q + 4 * mc)

        @pl.when(last)
        def _():
            for z in range(0, 16, 4):
                VB[z : z + 4] = S0[0, 4 + z : 8 + z, 16:48, :] / MB[z : z + 4]

        for q in range(2):
            swaps[q].wait_recv()
            HB[4 * q : 4 * q + 4] = LB[pl.ds(8 * q + 4 * mc, 4)] + XB[4 * q : 4 * q + 4]
            pieces.append([])
            for d in (2, 1, 3):
                part = HB.at[pl.ds(4 * q + lax.rem(mx + d, 4), 1)]
                pieces[q].append(remote(part, PB.at[q, d - 1], p_send.at[q, d - 1], p_recv.at[q, d - 1], along_x(d)))
            begin(pieces[q])

        @pl.when(last)
        def _():
            begin(multiplier_moves())
            mult_out[:, mine, :] = VB[pl.ds(4 * cy, 4)]

        inverse = jnp.broadcast_to(IW[...][None], (4, 8, LANES)).reshape(1, 32, LANES)
        for q in range(2):
            for c in pieces[q]:
                c.wait_recv()
            total = HB[pl.ds(4 * q + mx, 1)] + PB[q, 0] + PB[q, 1] + PB[q, 2]
            own = 8 * q + 4 * mc + mx
            CB[pl.ds(own, 1)] = jnp.exp(total * inverse)
            made = CB.at[pl.ds(own, 1)]
            spread.append([remote(made, made, c_send.at[q, d - 1], c_recv.at[q, d - 1], along_x(d)) for d in (2, 1, 3)])
            passed.append([])
            for d in (0, 1, 3, 2):
                at = CB.at[pl.ds(8 * q + 4 * mc + lax.rem(mx - d + 4, 4), 1)]
                passed[q].append((d, remote(at, at, f_send.at[q, d], f_recv.at[q, d], sibling)))

            @pl.when(jnp.logical_not(last))
            def _():
                begin(spread[q])
                passed[q][0][1].start()
                update(own)

            @pl.when(last)
            def _():
                begin_slabs(q, own)

        @pl.when(jnp.logical_not(last))
        def _():
            for q in range(2):
                for (d, c), arrived in zip(passed[q][1:], spread[q][1:] + spread[q][:1]):
                    arrived.wait_recv()
                    c.start()
                    update(8 * q + 4 * mc + lax.rem(mx - d + 4, 4))
            for q in range(2):
                for d, c in passed[q]:
                    c.wait_recv()
                    update(8 * q + 4 * (1 - mc) + lax.rem(mx - d + 4, 4))
            for q in range(2):
                for c in spread[q] + [f for _, f in passed[q]]:
                    c.wait_send()

        @pl.when(last)
        def _():
            finish_slabs()

        for q in range(2):
            for c in [swaps[q]] + pieces[q]:
                c.wait_send()

    def slab_pieces(q, own):
        made, place = CB.at[pl.ds(own, 1)], cent_out.at[pl.ds(mx, 1), mine]
        return [
            remote(made, place, e_send.at[q, d], e_recv.at[d, cy], (2 * lax.rem(mx + d, 4) + mc, cz * 4 + 2 * q + mc))
            for d in range(4)
        ]

    def begin_slabs(q, own):
        home, copies = cy == 2 * q + mc, slab_pieces(q, own)
        for d in (2, 1, 3):
            copies[d].start()
        pl.when(jnp.logical_not(home))(copies[0].start)

        @pl.when(home)
        def _():
            cent_out[pl.ds(mx, 1), mine, :] = CB[pl.ds(own, 1)]

    def finish_slabs():
        receiver = lax.rem(cy, 2) == mc
        sibling = (member + 1 - 2 * mc, slab)

        def piece(d, e):
            return cent_out.at[pl.ds(lax.rem(mx - d + 4, 4), 1), pl.ds(32 * e, 32)]

        def passing(d, e):
            return remote(piece(d, e), piece(d, e), k_send.at[d, e], k_recv.at[d, e], sibling)

        order = [(d, e) for d in (0, 1, 3, 2) for e in range(4)]

        @pl.when(receiver)
        def _():
            for d, e in order:
                arrival = remote(piece(d, e), piece(d, e), e_send.at[0, d], e_recv.at[d, e], sibling)
                if d == 0:
                    pl.when(cy != e)(arrival.wait_recv)
                else:
                    arrival.wait_recv()
                passing(d, e).start()
            for d, e in order:
                passing(d, e).wait_send()

        @pl.when(jnp.logical_not(receiver))
        def _():
            for d, e in order:
                passing(d, e).wait_recv()

        for q in range(2):
            copies = slab_pieces(q, 8 * q + 4 * mc + mx)
            for d in (1, 2, 3):
                copies[d].wait_send()
            pl.when(cy != 2 * q + mc)(copies[0].wait_send)
        finish(multiplier_moves())

    def multiplier_moves():
        return to_slabs(VB, 0, 0, mult_out, o_send, o_recv)

    def half_step(n, _):
        slot = lax.rem(n, 2)

        def keep(z, h):
            MB[pl.ds(z - 4, 4)] = h

        vcycle(n, slot, keep)

        @pl.when(slot == 0)
        def _():
            def partner(z):
                p = VB[pl.ds(z - 4, 4)] / MB[pl.ds(z - 4, 4)]
                S0[1, pl.ds(z, 4), 16:48, :] = p
                SC[pl.ds(z, 4), 16:48, :] = p

            over(4, 16, 4, partner)

        @pl.when(slot == 1)
        def _():
            centroid(n == 2 * ITERS - 1)

        @pl.when(n < 2 * ITERS - 1)
        def _():
            begin_halo0(1 - slot)

        return 0

    lax.fori_loop(0, 2 * ITERS, half_step, 0)

    mult_out[...] = mult_out[...] * cent_out[...]


def body(nonnegative_volumes, reaction, diffusivity, member_weights):
    vmem, smem = pl.BlockSpec(memory_space=pltpu.VMEM), pl.BlockSpec(memory_space=pltpu.SMEM)
    hbm = pl.BlockSpec(memory_space=pl.ANY)
    field = jax.ShapeDtypeStruct((4, 128, 128), F32)

    def buffer(*shape):
        return pltpu.VMEM((*shape, LANES), F32)

    dma = pltpu.SemaphoreType.DMA
    scratch = [
        buffer(2, 24, 64), *[buffer(24, 64) for _ in range(7)], buffer(5, 48), buffer(10, 48),
        *[buffer(18, 40) for _ in range(8)], buffer(8, 32), buffer(8, 32), buffer(5, 24),
        buffer(2, 2, 3, 24), buffer(2, 2, 5, 8), buffer(2, 4, 3, 8), buffer(2, 8, 8), buffer(2, 2, 8, 8), buffer(2, 4, 1, 8),
        buffer(2, 16, 24), buffer(4, 32), buffer(4, 32), buffer(4, 32), buffer(6, 48), buffer(4, 32), buffer(4, 32), buffer(16), buffer(6, 16),
        buffer(16, 32), buffer(16, 32), buffer(16, 32), buffer(8, 32), buffer(8, 32), buffer(2, 3, 1, 32), buffer(16, 32),
        buffer(8), buffer(8, 8), buffer(8),
        *[pltpu.VMEM(shape, BF16) for shape in ((128, 128), (512, 128), (512, 128), (128, 512), (128, 512), (128, 128))],
        dma((2, 8)), dma((2, 8)), dma((2, 8)), dma((2, 8)), dma((2,)), dma((2,)),
        dma((3,)), dma((3,)), dma((3,)), dma((3,)), dma((7,)), dma((7,)),
        dma((2,)), dma((2,)), dma((2,)), *[dma((2, 3)) for _ in range(4)], dma((2, 4)), dma((2, 4)), dma((3,)), dma((3,)),
        dma((2, 4)), dma((4, 4)), dma((4, 4)), dma((4, 4)),
    ]
    centroid, multipliers = pl.pallas_call(
        kernel,
        out_shape=(field, field),
        in_specs=[hbm, hbm, smem, smem],
        out_specs=(vmem, vmem),
        scratch_shapes=scratch,
        compiler_params=pltpu.CompilerParams(collective_id=0, has_side_effects=True, vmem_limit_bytes=40 * 2**20),
    )(nonnegative_volumes[0], reaction, diffusivity, member_weights)
    return centroid, multipliers[None]


def solution(mesh):
    return jax.shard_map(
        body,
        mesh=mesh,
        in_specs=(P("member", "slab", None, None), P("slab", None, None), P(), P("member")),
        out_specs=(P("slab", None, None), P("member", "slab", None, None)),
        check_vma=False,
    )
```

```python
import jax
import jax.numpy as jnp
from jax import lax
from jax.experimental import pallas as pl
from jax.experimental.pallas import tpu as pltpu
from jax.sharding import PartitionSpec as P

ITERS = 3
COARSE_SWEEPS = 8
OMEGA = 0.8
LANES = 128
NZ, NY = 64, 128
F32, BF16 = jnp.float32, jnp.bfloat16
MESH = pl.DeviceIdType.MESH
FARTHEST = sorted(range(1, 16), key=lambda d: -min(d // 4, 4 - d // 4) - min(d % 4, 4 - d % 4))
DIRECTIONS = ((-1, 0), (1, 0), (0, -1), (0, 1), (-1, -1), (-1, 1), (1, -1), (1, 1))

GEOMETRY = (dict(own_z=4, own_y=16, nz=16, ny=32), dict(own_z=5, own_y=12, nz=8, ny=16))


def dot(a, b):
    high = a.astype(BF16)
    low = (a - high.astype(F32)).astype(BF16)
    return jnp.dot(high, b, preferred_element_type=F32) + jnp.dot(low, b, preferred_element_type=F32)


def flat(a):
    return a.reshape(-1, LANES)


def lane_roll(a, shift):
    return pltpu.roll(flat(a), shift % LANES, 1).reshape(a.shape)


def kernel(
    vol_ref, reaction_ref, diff_ref, weight_ref, cent_out, mult_out,
    S0, SC, D0, DG0, UA, UB, U0a, U0b, C0, T0,
    S1, S1C, D1, DG1, VA, VC, U1a, U1b, C1, T1, P1, LZ, LY, LD, E0, LE, LQ,
    G, S2, D2, DG2, U2, T2, C2, D3, K3,
    RS, RT, RG, VB, QB, MB, LB, XB, HB, PB, CB, WS, WB, IW,
    Rx, Rx1, R3, P3, E1, Px,
    h0_send, h0_recv, h1_send, h1_recv, g_send, g_recv,
    ra_send, ra_recv, va_send, va_recv, w_send, w_recv,
    l_sem, rg_sem, x_send, x_recv, p_send, p_recv, c_send, c_recv, f_send, f_recv, o_send, o_recv, e_send, e_recv, k_send, k_recv,
):
    member, slab = lax.axis_index("member"), lax.axis_index("slab")
    cz, cy = slab // 4, lax.rem(slab, 4)
    mx, mc = member // 2, lax.rem(member, 2)

    def at_slab(dz, dy):
        return lax.rem(cz + dz + 4, 4) * 4 + lax.rem(cy + dy + 4, 4)

    def remote(src, dst, send, recv, to):
        return pltpu.make_async_remote_copy(
            src_ref=src, dst_ref=dst, send_sem=send, recv_sem=recv, device_id=to, device_id_type=MESH
        )

    for ref in (LZ, LY, LD, LE, LQ):
        ref[...] = jnp.zeros(ref.shape, F32)
    S0[...] = jnp.ones(S0.shape, F32)
    mine = pl.ds(pl.multiple_of(32 * cy, 32), 32)
    own_reaction = pltpu.make_async_copy(reaction_ref.at[:, mine], S0.at[1, pl.ds(4 + 4 * cy, 4), pl.ds(16, 32)], l_sem.at[0])
    own_volume = pltpu.make_async_copy(vol_ref.at[:, mine], VB.at[pl.ds(4 * cy, 4)], l_sem.at[1])
    own_reaction.start()
    own_volume.start()
    slab_reaction = pltpu.make_async_copy(reaction_ref, RS, l_sem.at[2])
    slab_reaction.start()

    barrier = pltpu.get_barrier_semaphore()
    for d in FARTHEST:
        pl.semaphore_signal(barrier, inc=1, device_id=(member, at_slab(d // 4, d % 4)), device_id_type=MESH)
    for d in range(1, 8):
        pl.semaphore_signal(barrier, inc=1, device_id=(lax.rem(member + d, 8), slab), device_id_type=MESH)

    coupling = [[diff_ref[i] * (0.25**level) for i in range(3)] for level in range(4)]
    center = [2.0 * (c[0] + c[1] + c[2]) for c in coupling]

    lane = lax.broadcasted_iota(jnp.int32, (1, LANES), 1)
    one, zero = jnp.ones((1, LANES), F32), jnp.zeros((1, LANES), F32)

    def lane_mask(keep):
        return jnp.where(keep, one, zero)

    row_i = lax.broadcasted_iota(jnp.int32, (LANES, LANES), 0)
    col_i = lax.broadcasted_iota(jnp.int32, (LANES, LANES), 1)

    def half(a):
        return lax.shift_right_logical(a, 1)

    def matrix(keep, value=1.0):
        return jnp.where(keep, jnp.full((LANES, LANES), value, F32), jnp.zeros((LANES, LANES), F32)).astype(BF16)

    Rx[...] = matrix(half(row_i) == col_i, 0.125)
    Px[...] = matrix(row_i == half(col_i))
    for q in range(4):
        block = slice(LANES * q, LANES * q + LANES)
        Rx1[block, :] = matrix((row_i < 64) & (half(row_i) + 32 * q == col_i), 0.125)
        E1[:, block] = matrix((col_i < 64) & (row_i == half(col_i) + 32 * q))
        R3[block, :] = matrix(16 * (2 * q + lax.shift_right_logical(row_i, 6)) + half(row_i & 31) == col_i, 0.125)
        P3[:, block] = matrix(16 * (2 * q + lax.shift_right_logical(col_i, 6)) + half(col_i & 31) == row_i)

    left = [lane_mask(lane > 0) * coupling[0][2], None, lane_mask((lane & 31) > 0) * coupling[2][2], lane_mask((lane & 15) > 0) * coupling[3][2]]
    right = [lane_mask(lane < 127) * coupling[0][2], None, lane_mask((lane & 31) < 31) * coupling[2][2], lane_mask((lane & 15) < 15) * coupling[3][2]]
    WS[...] = jnp.full((8, LANES), weight_ref[0], F32)
    for ref in (SC, UA, UB, VA, VC, S1C, U0a, U0b, U1a, U1b, U2, T1):
        ref[...] = jnp.zeros(ref.shape, F32)

    slab_reaction.wait()
    RT[0] = RS[0] + RS[1]
    RT[1] = RS[2] + RS[3]
    level1 = dot(flat(RT[:, pl.ds(0, 64, stride=2), :] + RT[:, pl.ds(1, 64, stride=2), :]), Rx[...])
    RT[0, 0:64, :] = level1[0:64] + level1[64:128]
    level2 = RT[0, pl.ds(0, 32, stride=2), :] + RT[0, pl.ds(1, 32, stride=2), :]
    groups = jnp.concatenate([level2[8 * k : 8 * k + 8] for k in range(4)], axis=1)
    RG[slab] = dot(jnp.concatenate([groups, groups], axis=0), Rx1[...])[0:8]
    pl.semaphore_wait(barrier, 22)

    def inner(dz, dy):
        return (cz + dz >= 0) & (cz + dz < 4) & (cy + dy >= 0) & (cy + dy < 4)

    def halo0(slot):
        copies = []
        for k, (dz, dy) in enumerate(DIRECTIONS):
            if dy == 0:
                zs, zd = (4, 20) if dz < 0 else (17, 1)
                src, dst = S0.at[slot, pl.ds(zs, 3), pl.ds(16, 32)], S0.at[slot, pl.ds(zd, 3), pl.ds(16, 32)]
            elif dz == 0:
                src, dst = E0.at[(dy + 1) // 2], LE.at[slot, k - 2]
            else:
                src, dst = E0.at[(dy + 1) // 2, pl.ds(0 if dz < 0 else 7, 1)], LQ.at[slot, k - 4]
            copies.append((
                dz, dy, remote(src, dst, h0_send.at[slot, k], h0_recv.at[slot, k], (member, at_slab(dz, dy)))
            ))
        return copies

    def begin_halo0(slot):
        for edge, row in ((0, 16), (1, 44)):
            for p in range(8):
                E0[edge, p, 0:4, :] = S0[slot, 4 + 2 * p, row : row + 4, :]
                E0[edge, p, 4:8, :] = S0[slot, 5 + 2 * p, row : row + 4, :]
        begin_near(halo0(slot))

    def finish_halo0(slot):
        finish_near(halo0(slot))
        for k, (dz, dy) in enumerate(DIRECTIONS):
            if dy == 0:
                continue
            row, z0, tiles = (48 if dy < 0 else 12), {-1: 20, 0: 4, 1: 2}[dz], 8 if dz == 0 else 1
            for p in range(tiles):
                tile = LE[slot, k - 2, p] if dz == 0 else LQ[slot, k - 4, p]
                S0[slot, z0 + 2 * p, row : row + 4, :] = tile[0:4]
                S0[slot, z0 + 2 * p + 1, row : row + 4, :] = tile[4:8]

    def landing1(k, slot):
        if k < 2:
            return LZ.at[slot, k]
        return LY.at[slot, k - 2] if k < 4 else LD.at[slot, k - 4]

    def halo1(slot):
        copies = []
        for k, (dz, dy) in enumerate(DIRECTIONS):
            z = {-1: pl.ds(0, 3), 0: pl.ds(0, 5), 1: pl.ds(2, 3)}[dz]
            y = {-1: pl.ds(0, 8), 0: pl.ds(0, 24), 1: pl.ds(16, 8)}[dy]
            copies.append((
                dz, dy,
                remote(
                    P1.at[z, y], landing1(k, slot),
                    h1_send.at[slot, k], h1_recv.at[slot, k], (member, at_slab(dz, dy)),
                ),
            ))
        return copies

    def begin_near(copies):
        for dz, dy, c in copies:
            pl.when(inner(dz, dy))(c.start)

    def begin_halo1(slot):
        for p in range(5):
            P1[p] = S1C[4 + 2 * p, 8:32, :] + lane_roll(S1C[5 + 2 * p, 8:32, :], 64)
        begin_near(halo1(slot))

    def finish_near(copies):
        for dz, dy, c in copies:
            pl.when(inner(-dz, -dy))(c.wait_recv)
        for dz, dy, c in copies:
            pl.when(inner(dz, dy))(c.wait_send)

    def gather(slot):
        return [
            remote(
                G.at[slot, slab], G.at[slot, slab],
                g_send.at[slot], g_recv.at[slot], (member, at_slab(d // 4, d % 4)),
            )
            for d in FARTHEST
        ]

    def finish_gather(slot):
        all_of_them = G.at[slot, 0:15]
        pltpu.make_async_copy(all_of_them, all_of_them, g_recv.at[slot]).wait()

    def finish_gather_sends(slot):
        all_of_them = G.at[slot, 0:15]
        pltpu.make_async_copy(all_of_them, all_of_them, g_send.at[slot]).wait()

    def begin(copies):
        for c in copies:
            c.start()

    def finish(copies):
        for c in copies:
            c.wait()

    def to_blocks(src, dst, dst_z, dst_y, send, recv):
        copies = []
        for d in range(1, 4):
            to = lax.rem(cy + d, 4)
            copies.append(
                remote(
                    src.at[:, pl.ds(pl.multiple_of(32 * to, 32), 32)],
                    dst.at[pl.ds(dst_z + 4 * cy, 4), pl.ds(dst_y, 32)],
                    send.at[d - 1], recv.at[d - 1], (member, cz * 4 + to),
                )
            )
        return copies

    def to_slabs(src, src_z, src_y, dst, send, recv):
        copies = []
        for d in range(1, 4):
            to = lax.rem(cy + d, 4)
            copies.append(
                remote(
                    src.at[pl.ds(src_z + 4 * to, 4), pl.ds(src_y, 32)],
                    dst.at[:, pl.ds(pl.multiple_of(32 * cy, 32), 32)],
                    send.at[d - 1], recv.at[d - 1], (member, cz * 4 + to),
                )
            )
        return copies

    reaction_moves = to_blocks(reaction_ref, S0.at[1], 4, 16, ra_send, ra_recv)
    volume_moves = to_blocks(vol_ref, VB, 0, 0, va_send, va_recv)
    begin(reaction_moves)
    begin([
        remote(RG.at[slab], RG.at[slab], rg_sem.at[0], rg_sem.at[1], (member, at_slab(d // 4, d % 4))) for d in FARTHEST
    ])
    weight_moves = [
        remote(WS, WB.at[d], w_send.at[d - 1], w_recv.at[d - 1], (lax.rem(member + d, 8), slab)) for d in range(1, 8)
    ]

    def neighbours(level, u, z, n, lo, rows):
        c = coupling[level]
        mid = u[pl.ds(z, n), lo : lo + rows, :]
        total = c[0] * (u[pl.ds(z - 1, n), lo : lo + rows, :] + u[pl.ds(z + 1, n), lo : lo + rows, :])
        total += c[1] * (u[pl.ds(z, n), lo - 1 : lo + rows - 1, :] + u[pl.ds(z, n), lo + 1 : lo + rows + 1, :])
        if level == 0:
            total += left[0] * lane_roll(mid, 1) + right[0] * lane_roll(mid, -1)
        else:
            total += c[2] * (lane_roll(mid, 1) + lane_roll(mid, -1))
        return mid, total

    def over(z0, count, step, body):
        for z in range(z0, z0 + count, step):
            body(z)

    def sweep(level, u, s, d, z, n, lo, rows):
        mid, total = neighbours(level, u, z, n, lo, rows)
        return (1.0 - OMEGA) * mid + d[pl.ds(z, n), lo : lo + rows, :] * (s[pl.ds(z, n), lo : lo + rows, :] + total)

    def residual(level, u, s, dg, z, n, lo, rows):
        mid, total = neighbours(level, u, z, n, lo, rows)
        return s[pl.ds(z, n), lo : lo + rows, :] - dg[pl.ds(z, n), lo : lo + rows, :] * mid + total

    def restrict0(fine):
        def body(z):
            a = fine(z)
            for k in range(2):
                T0[(z - 2) // 2 + k] = a[2 * k] + a[2 * k + 1]

        over(2, 20, 4, body)

        def rows(i):
            e = T0[pl.ds(i, 5), pl.ds(0, 24, stride=2), :] + T0[pl.ds(i, 5), pl.ds(1, 24, stride=2), :]
            S1C[pl.ds(4 + i, 5), 8:32, :] = dot(flat(e), Rx[...]).reshape(5, 24, LANES)

        over(0, 10, 5, rows)

    def restrict1(fine, slot):
        def body(z):
            a = fine(z)
            for k in range(4):
                T1[(z - 1) // 2 + k, 4:28, :] = a[2 * k] + a[2 * k + 1]

        over(1, 16, 8, body)
        e = T1[:, pl.ds(0, 16, stride=2), :] + T1[:, pl.ds(1, 16, stride=2), :]
        own = jnp.concatenate([e[2], e[3], e[4], e[5]], axis=1)
        sides = jnp.concatenate([e[6], e[7], e[0], e[1]], axis=1)
        m = dot(jnp.concatenate([own, sides], axis=0), Rx1[...]).reshape(2, 16, LANES)
        G[slot, slab, 0:8, :] = m[0, 4:12]
        G[slot, slab, 8:16, :] = m[1, 4:12]
        for row, part in ((16, m[0, 12:14]), (18, m[1, 12:14]), (20, m[1, 2:4]), (22, m[0, 2:4])):
            G[slot, slab, row : row + 2, :] = part

    upper_half, row8 = lane >= 64, lax.broadcasted_iota(jnp.int32, (8, LANES), 0)
    nothing = jnp.zeros((8, LANES), F32)

    def gathered(slot):
        def rows(c, j, g):
            below = G[slot, 4 * c + j - 1, 16:24, :] if j > 0 else nothing
            above = G[slot, 4 * c + j + 1, 16:24, :] if j < 3 else nothing
            if g:
                below = pltpu.roll(below, 6, 0) if j > 0 else nothing
                above = pltpu.roll(above, 2, 0) if j < 3 else nothing
            near = jnp.where(row8 < 2, below, jnp.where(row8 >= 6, above, nothing))
            return G[slot, 4 * c + j, 8 * g : 8 * g + 8, :] + near

        for j in range(4):
            side = [nothing] + [rows(c, j, 1) for c in range(4)] + [nothing]
            for c in range(4):
                S2[c, 8 * j : 8 * j + 8, :] = rows(c, j, 0) + jnp.where(upper_half, side[c + 2], side[c])

    def restrict2(a):
        T2[...] = a
        e = T2[:, pl.ds(0, 16, stride=2), :] + T2[:, pl.ds(1, 16, stride=2), :]
        return dot(jnp.concatenate([e[0], e[1], e[2], e[3]], axis=1), R3[...])

    first_chunk, last_chunk = lane < 32, lane >= 96
    plane2 = jnp.zeros((1, 32, LANES), F32)

    def neighbours2():
        c = coupling[2]
        mid = U2[1:5, 8:40, :]
        up, down = lane_roll(mid, 32), lane_roll(mid, -32)
        before = jnp.where(first_chunk, jnp.concatenate([plane2, up[:3]], axis=0), up)
        after = jnp.where(last_chunk, jnp.concatenate([down[1:], plane2], axis=0), down)
        total = c[0] * (before + after) + c[1] * (U2[1:5, 7:39, :] + U2[1:5, 9:41, :])
        total += left[2] * lane_roll(mid, 1) + right[2] * lane_roll(mid, -1)
        return mid, total

    def sweep2():
        mid, total = neighbours2()
        U2[1:5, 8:40, :] = (1.0 - OMEGA) * mid + D2[...] * (S2[...] + total)

    row16 = lax.broadcasted_iota(jnp.int32, (16, LANES), 0)
    zeros16, ones16 = jnp.zeros((16, LANES), F32), jnp.ones((16, LANES), F32)
    up3 = jnp.where(row16 > 0, ones16, zeros16) * coupling[3][1]
    down3 = jnp.where(row16 < 15, ones16, zeros16) * coupling[3][1]
    before3 = lane_mask(lane >= 16) * coupling[3][0]
    after3 = lane_mask(lane < 112) * coupling[3][0]

    def coefficients3(d):
        for i, c in enumerate((before3, after3, up3, down3, left[3], right[3])):
            K3[i] = d * c
        D3[...] = d

    def level3(s):
        k = [K3[i] for i in range(6)]
        base = D3[...] * s
        u = base
        for _ in range(COARSE_SWEEPS - 1):
            z = k[0] * lane_roll(u, 16) + k[1] * lane_roll(u, -16)
            y = k[2] * pltpu.roll(u, 1, 0) + k[3] * pltpu.roll(u, 15, 0)
            x = k[4] * lane_roll(u, 1) + k[5] * lane_roll(u, -1)
            u = (base + (1.0 - OMEGA) * u + y) + (z + x)
        return u

    def inside(level, z, n, lo, rows):
        g = GEOMETRY[level]
        zi = lax.broadcasted_iota(jnp.int32, (n, rows, LANES), 0) + (z - g["own_z"] + g["nz"] * cz)
        yi = lax.broadcasted_iota(jnp.int32, (n, rows, LANES), 1) + (lo - g["own_y"] + g["ny"] * cy)
        keep = (zi >= 0) & (zi < 4 * g["nz"]) & (yi >= 0) & (yi < 4 * g["ny"])
        if level:
            keep = keep & (lax.broadcasted_iota(jnp.int32, (n, rows, LANES), 2) < 64)
        return keep

    finish(reaction_moves)
    own_reaction.wait()
    begin_halo0(1)
    SC[4:20, 16:48, :] = S0[1, 4:20, 16:48, :]
    restrict0(lambda z: SC[pl.ds(z, 4), 8:56, :])
    begin_halo1(1)
    begin(volume_moves)
    begin(weight_moves)
    own_volume.wait()

    def summed1(slot):
        finish_near(halo1(slot))
        S1[1:17, 8:32, :] = S1C[1:17, 8:32, :]
        for k, (dz, dy) in enumerate(DIRECTIONS):
            z0, tiles = {-1: (12, 3), 0: (4, 5), 1: (0, 3)}[dz]
            y = {-1: slice(24, 32), 0: slice(8, 32), 1: slice(8, 16)}[dy]
            for p in range(tiles):
                both = landing1(k, slot)[p]
                for z, part in ((z0 + 2 * p, both), (z0 + 2 * p + 1, lane_roll(both, 64))):
                    if 1 <= z < 17:
                        S1[z, y, :] += jnp.where(upper_half, jnp.zeros_like(part), part)

    finish_halo0(1)

    def diag0(z):
        diag = S0[1, pl.ds(z, 2), 8:56, :] + center[0]
        DG0[pl.ds(z, 2), 8:56, :] = diag
        D0[pl.ds(z, 2), 8:56, :] = jnp.where(inside(0, z, 2, 8, 48), OMEGA / diag, jnp.zeros((2, 48, LANES), F32))

    over(1, 22, 2, diag0)
    summed1(1)

    def diag1(z):
        diag = S1[pl.ds(z, 2), 8:32, :] + center[1]
        DG1[pl.ds(z, 2), 8:32, :] = diag
        D1[pl.ds(z, 2), 8:32, :] = jnp.where(inside(1, z, 2, 8, 24), OMEGA / diag, jnp.zeros((2, 24, LANES), F32))

    over(1, 16, 2, diag1)
    tiles = RG.at[0:15]
    pltpu.make_async_copy(tiles, tiles, rg_sem.at[1]).wait()
    pltpu.make_async_copy(tiles, tiles, rg_sem.at[0]).wait()
    for c in range(4):
        for k in range(4):
            rows = jnp.zeros((8, LANES), F32)
            for j in range(4):
                rows = jnp.where((lane >= 32 * j) & (lane < 32 * j + 32), lane_roll(RG[4 * c + j], 32 * (j - k)), rows)
            S2[c, 8 * k : 8 * k + 8, :] = rows
    DG2[...] = S2[...] + center[2]
    D2[...] = OMEGA / DG2[...]
    coefficients3(OMEGA / (restrict2(S2[...]) + center[3]))
    SC[4:20, 16:48, :] = jnp.ones((16, 32, LANES), F32)
    finish(volume_moves)
    finish(weight_moves)
    weight_total = WS[...]
    for d in range(1, 8):
        weight_total += WB[d]
    IW[...] = 1.0 / weight_total

    def vcycle(n, slot):
        UA[4:20, 16:48, :] = D0[4:20, 16:48, :] * SC[4:20, 16:48, :]

        def own0(z):
            UB[pl.ds(z, 3), 8:56, :] = sweep(0, UA, SC, D0, z, 3, 8, 48)

        over(3, 18, 3, own0)
        restrict0(lambda z: residual(0, UB, SC, DG0, z, 4, 8, 48))
        begin_halo1(slot)
        VA[4:14, 8:32, :] = D1[4:14, 8:32, :] * S1C[4:14, 8:32, :]

        def own1(z):
            VC[pl.ds(z, 6), 8:32, :] = sweep(1, VA, S1C, D1, z, 6, 8, 24)

        over(3, 12, 6, own1)
        restrict1(lambda z: residual(1, VC, S1C, DG1, z, 8, 8, 24), slot)
        begin(gather(slot))

        @pl.when(n > 0)
        def _():
            finish_halo0(slot)

        source0 = S0.at[slot]

        def first0(z):
            U0a[pl.ds(z, 2), 8:56, :] = D0[pl.ds(z, 2), 8:56, :] * source0[pl.ds(z, 2), 8:56, :]

        over(1, 22, 2, first0)

        def pre0(z):
            U0b[pl.ds(z, 4), 8:56, :] = sweep(0, U0a, source0, D0, z, 4, 8, 48)

        over(2, 20, 4, pre0)
        summed1(slot)
        U1a[1:17, 8:32, :] = D1[1:17, 8:32, :] * S1[1:17, 8:32, :]

        def pre1(z):
            U1b[pl.ds(z, 7), 8:32, :] = sweep(1, U1a, S1, D1, z, 7, 8, 24)

        over(2, 14, 7, pre1)

        finish_gather(slot)
        gathered(slot)
        U2[1:5, 8:40, :] = D2[...] * S2[...]
        sweep2()
        mid, total = neighbours2()
        u3 = level3(restrict2(S2[...] - DG2[...] * mid + total))
        p = dot(u3, P3[...])
        for k in range(4):
            C2[k, pl.ds(0, 16, stride=2), :] = p[:, LANES * k : LANES * k + LANES]
            C2[k, pl.ds(1, 16, stride=2), :] = p[:, LANES * k : LANES * k + LANES]
        U2[1:5, 8:40, :] += C2[...]
        sweep2()
        sweep2()

        finish_gather_sends(slot)

        window = pl.ds(pl.multiple_of(8 * cy, 8), 24)
        own = U2[1 + cz, window, :][4:20]
        sides = jnp.where(upper_half, U2[cz, window, :][4:20], U2[2 + cz, window, :][4:20])
        wide = dot(jnp.concatenate([own, sides], axis=0), E1[...])
        for k in range(8):
            r, q = (0, k - 2) if 2 <= k < 6 else (16, (k - 2) % 4)
            C1[k, pl.ds(0, 16, stride=2), :] = wide[r : r + 16, LANES * q : LANES * q + LANES]
            C1[k, pl.ds(1, 16, stride=2), :] = wide[r : r + 16, LANES * q : LANES * q + LANES]
        for k in range(8):
            U1b[1 + 2 * k, 8:32, :] += C1[k, 4:28, :]
            U1b[2 + 2 * k, 8:32, :] += C1[k, 4:28, :]

        def post1a(z):
            U1a[pl.ds(z, 6), 8:32, :] = sweep(1, U1b, S1, D1, z, 6, 8, 24)

        over(3, 12, 6, post1a)

        def post1b(z):
            U1b[pl.ds(z, 5), 8:32, :] = sweep(1, U1a, S1, D1, z, 5, 8, 24)

        over(4, 10, 5, post1b)

        def widen0(i):
            wide = dot(flat(U1b[pl.ds(4 + i, 5), 8:32, :]), Px[...]).reshape(5, 24, LANES)
            C0[:, pl.ds(0, 24, stride=2), :] = wide
            C0[:, pl.ds(1, 24, stride=2), :] = wide
            for k in range(5):
                U0b[2 + 2 * (i + k), 8:56, :] += C0[k]
                U0b[3 + 2 * (i + k), 8:56, :] += C0[k]

        over(0, 10, 5, widen0)

        def post0a(z):
            U0a[pl.ds(z, 3), 8:56, :] = sweep(0, U0b, source0, D0, z, 3, 8, 48)

        over(3, 18, 3, post0a)

        def post0b(z):
            return sweep(0, U0a, source0, D0, z, 4, 16, 32)

        @pl.when(slot == 0)
        def _():
            for z in range(4, 20, 4):
                p = VB[z - 4 : z] / post0b(z)
                S0[1, z : z + 4, 16:48, :] = p
                SC[z : z + 4, 16:48, :] = p

        @pl.when(slot == 1)
        def _():
            for z in range(4, 20, 4):
                MB[z - 4 : z] = post0b(z)

    def centroid(last):
        sibling = (member + 1 - 2 * mc, slab)

        def marginal(at):
            m = S0[0, pl.ds(4 + at, 4), 16:48, :] * MB[pl.ds(at, 4)]
            MB[pl.ds(at, 4)] = m
            LB[pl.ds(at, 4)] = weight_ref[0] * jnp.log(m)

        def update(at):
            p = QB[at] * CB[at]
            S0[0, 4 + at, 16:48, :] = p
            SC[4 + at, 16:48, :] = p

        def along_x(d):
            return (2 * lax.rem(mx + d, 4) + mc, slab)

        swaps, pieces, spread, passed = [], [], [], []
        for q in range(2):
            marginal(8 * q + 4 * (1 - mc))
            theirs, here = LB.at[pl.ds(8 * q + 4 * (1 - mc), 4)], XB.at[pl.ds(4 * q, 4)]
            swaps.append(remote(theirs, here, x_send.at[q], x_recv.at[q], sibling))
            swaps[q].start()
        for q in range(2):
            marginal(8 * q + 4 * mc)

        for q in range(2):
            swaps[q].wait_recv()
            HB[4 * q : 4 * q + 4] = LB[pl.ds(8 * q + 4 * mc, 4)] + XB[4 * q : 4 * q + 4]
            pieces.append([])
            for d in (2, 1, 3):
                part = HB.at[pl.ds(4 * q + lax.rem(mx + d, 4), 1)]
                pieces[q].append(remote(part, PB.at[q, d - 1], p_send.at[q, d - 1], p_recv.at[q, d - 1], along_x(d)))
            begin(pieces[q])

        for z in range(0, 16, 4):
            QB[z : z + 4] = S0[0, 4 + z : 8 + z, 16:48, :] / MB[z : z + 4]

        @pl.when(last)
        def _():
            begin(multiplier_moves())
            mult_out[:, mine, :] = QB[pl.ds(4 * cy, 4)]

        inverse = jnp.broadcast_to(IW[...][None], (4, 8, LANES)).reshape(1, 32, LANES)
        for q in range(2):
            for c in pieces[q]:
                c.wait_recv()
            total = HB[pl.ds(4 * q + mx, 1)] + PB[q, 0] + PB[q, 1] + PB[q, 2]
            own = 8 * q + 4 * mc + mx
            CB[pl.ds(own, 1)] = jnp.exp(total * inverse)
            made = CB.at[pl.ds(own, 1)]
            spread.append([remote(made, made, c_send.at[q, d - 1], c_recv.at[q, d - 1], along_x(d)) for d in (2, 1, 3)])
            passed.append([])
            for d in (0, 1, 3, 2):
                at = CB.at[pl.ds(8 * q + 4 * mc + lax.rem(mx - d + 4, 4), 1)]
                passed[q].append((d, remote(at, at, f_send.at[q, d], f_recv.at[q, d], sibling)))

            @pl.when(jnp.logical_not(last))
            def _():
                begin(spread[q])
                passed[q][0][1].start()
                update(own)

            @pl.when(last)
            def _():
                begin_slabs(q, own)

        @pl.when(jnp.logical_not(last))
        def _():
            for q in range(2):
                for (d, c), arrived in zip(passed[q][1:], spread[q][1:] + spread[q][:1]):
                    arrived.wait_recv()
                    c.start()
                    update(8 * q + 4 * mc + lax.rem(mx - d + 4, 4))
            for q in range(2):
                for d, c in passed[q]:
                    c.wait_recv()
                    update(8 * q + 4 * (1 - mc) + lax.rem(mx - d + 4, 4))
            for q in range(2):
                for c in spread[q] + [f for _, f in passed[q]]:
                    c.wait_send()

        @pl.when(last)
        def _():
            finish_slabs()

        for q in range(2):
            for c in [swaps[q]] + pieces[q]:
                c.wait_send()

    def slab_pieces(q, own):
        made, place = CB.at[pl.ds(own, 1)], cent_out.at[pl.ds(mx, 1), mine]
        return [
            remote(made, place, e_send.at[q, d], e_recv.at[d, cy], (2 * lax.rem(mx + d, 4) + mc, cz * 4 + 2 * q + mc))
            for d in range(4)
        ]

    def begin_slabs(q, own):
        home, copies = cy == 2 * q + mc, slab_pieces(q, own)
        for d in (2, 1, 3):
            copies[d].start()
        pl.when(jnp.logical_not(home))(copies[0].start)

        @pl.when(home)
        def _():
            cent_out[pl.ds(mx, 1), mine, :] = CB[pl.ds(own, 1)]

    def finish_slabs():
        receiver = lax.rem(cy, 2) == mc
        sibling = (member + 1 - 2 * mc, slab)

        def piece(d, e):
            return cent_out.at[pl.ds(lax.rem(mx - d + 4, 4), 1), pl.ds(32 * e, 32)]

        def passing(d, e):
            return remote(piece(d, e), piece(d, e), k_send.at[d, e], k_recv.at[d, e], sibling)

        order = [(d, e) for d in (0, 1, 3, 2) for e in range(4)]

        @pl.when(receiver)
        def _():
            for d, e in order:
                arrival = remote(piece(d, e), piece(d, e), e_send.at[0, d], e_recv.at[d, e], sibling)
                if d == 0:
                    pl.when(cy != e)(arrival.wait_recv)
                else:
                    arrival.wait_recv()
                passing(d, e).start()
            for d, e in order:
                passing(d, e).wait_send()

        @pl.when(jnp.logical_not(receiver))
        def _():
            for d, e in order:
                passing(d, e).wait_recv()

        for q in range(2):
            copies = slab_pieces(q, 8 * q + 4 * mc + mx)
            for d in (1, 2, 3):
                copies[d].wait_send()
            pl.when(cy != 2 * q + mc)(copies[0].wait_send)
        finish(multiplier_moves())

    def multiplier_moves():
        return to_slabs(QB, 0, 0, mult_out, o_send, o_recv)

    def half_step(n, _):
        slot = lax.rem(n, 2)

        vcycle(n, slot)

        @pl.when(slot == 1)
        def _():
            centroid(n == 2 * ITERS - 1)

        @pl.when(n < 2 * ITERS - 1)
        def _():
            begin_halo0(1 - slot)

        return 0

    lax.fori_loop(0, 2 * ITERS, half_step, 0)

    mult_out[...] = mult_out[...] * cent_out[...]


def body(nonnegative_volumes, reaction, diffusivity, member_weights):
    vmem, smem = pl.BlockSpec(memory_space=pltpu.VMEM), pl.BlockSpec(memory_space=pltpu.SMEM)
    hbm = pl.BlockSpec(memory_space=pl.ANY)
    field = jax.ShapeDtypeStruct((4, 128, 128), F32)

    def buffer(*shape):
        return pltpu.VMEM((*shape, LANES), F32)

    dma = pltpu.SemaphoreType.DMA
    scratch = [
        buffer(2, 24, 64), *[buffer(24, 64) for _ in range(7)], buffer(5, 48), buffer(10, 48),
        *[buffer(18, 40) for _ in range(8)], buffer(8, 32), buffer(8, 32), buffer(5, 24),
        buffer(2, 2, 3, 24), buffer(2, 2, 5, 8), buffer(2, 4, 3, 8), buffer(2, 8, 8), buffer(2, 2, 8, 8), buffer(2, 4, 1, 8),
        buffer(2, 16, 24), buffer(4, 32), buffer(4, 32), buffer(4, 32), buffer(6, 48), buffer(4, 32), buffer(4, 32), buffer(16), buffer(6, 16),
        buffer(4, 128), buffer(2, 128), buffer(16, 8),
        buffer(16, 32), buffer(16, 32), buffer(16, 32), buffer(16, 32), buffer(8, 32), buffer(8, 32), buffer(2, 3, 1, 32), buffer(16, 32),
        buffer(8), buffer(8, 8), buffer(8),
        *[pltpu.VMEM(shape, BF16) for shape in ((128, 128), (512, 128), (512, 128), (128, 512), (128, 512), (128, 128))],
        dma((2, 8)), dma((2, 8)), dma((2, 8)), dma((2, 8)), dma((2,)), dma((2,)),
        dma((3,)), dma((3,)), dma((3,)), dma((3,)), dma((7,)), dma((7,)),
        dma((3,)), dma((2,)), dma((2,)), dma((2,)), *[dma((2, 3)) for _ in range(4)], dma((2, 4)), dma((2, 4)), dma((3,)), dma((3,)),
        dma((2, 4)), dma((4, 4)), dma((4, 4)), dma((4, 4)),
    ]
    centroid, multipliers = pl.pallas_call(
        kernel,
        out_shape=(field, field),
        in_specs=[hbm, hbm, smem, smem],
        out_specs=(vmem, vmem),
        scratch_shapes=scratch,
        compiler_params=pltpu.CompilerParams(collective_id=0, has_side_effects=True, vmem_limit_bytes=40 * 2**20),
    )(nonnegative_volumes[0], reaction, diffusivity, member_weights)
    return centroid, multipliers[None]


def solution(mesh):
    return jax.shard_map(
        body,
        mesh=mesh,
        in_specs=(P("member", "slab", None, None), P("slab", None, None), P(), P("member")),
        out_specs=(P("slab", None, None), P("member", "slab", None, None)),
        check_vma=False,
    )
```

```python
import jax
import jax.numpy as jnp
from jax import lax
from jax.experimental import pallas as pl
from jax.experimental.pallas import tpu as pltpu
from jax.sharding import PartitionSpec as P

ITERS = 3
COARSE_SWEEPS = 8
OMEGA = 0.8
LANES = 128
NZ, NY = 64, 128
F32, BF16 = jnp.float32, jnp.bfloat16
MESH = pl.DeviceIdType.MESH
FARTHEST = sorted(range(1, 16), key=lambda d: -min(d // 4, 4 - d // 4) - min(d % 4, 4 - d % 4))
DIRECTIONS = ((-1, 0), (1, 0), (0, -1), (0, 1), (-1, -1), (-1, 1), (1, -1), (1, 1))

GEOMETRY = (dict(own_z=4, own_y=16, nz=16, ny=32), dict(own_z=5, own_y=12, nz=8, ny=16))


def dot(a, b):
    high = a.astype(BF16)
    low = (a - high.astype(F32)).astype(BF16)
    return jnp.dot(high, b, preferred_element_type=F32) + jnp.dot(low, b, preferred_element_type=F32)


def flat(a):
    return a.reshape(-1, LANES)


def lane_roll(a, shift):
    return pltpu.roll(flat(a), shift % LANES, 1).reshape(a.shape)


def kernel(
    vol_ref, reaction_ref, diff_ref, weight_ref, cent_out, mult_out,
    S0, SC, D0, DG0, UA, UB, U0a, U0b, C0, T0,
    S1, S1C, D1, DG1, VA, VC, U1a, U1b, C1, T1, P1, LZ, LY, LD, E0, LE, LQ,
    G, S2, D2, DG2, U2, T2, C2, D3, K3,
    RS, RT, RG, VB, QB, MB, LB, XB, HB, PB, CB, WS, WB, IW,
    Rx, Rx1, R3, P3, E1, Px,
    h0_send, h0_recv, h1_send, h1_recv, g_send, g_recv,
    ra_send, ra_recv, va_send, va_recv, w_send, w_recv,
    l_sem, rg_sem, x_send, x_recv, p_send, p_recv, c_send, c_recv, f_send, f_recv, o_send, o_recv, e_send, e_recv, k_send, k_recv,
):
    member, slab = lax.axis_index("member"), lax.axis_index("slab")
    cz, cy = slab // 4, lax.rem(slab, 4)
    mx, mc = member // 2, lax.rem(member, 2)

    def at_slab(dz, dy):
        return lax.rem(cz + dz + 4, 4) * 4 + lax.rem(cy + dy + 4, 4)

    def remote(src, dst, send, recv, to):
        return pltpu.make_async_remote_copy(
            src_ref=src, dst_ref=dst, send_sem=send, recv_sem=recv, device_id=to, device_id_type=MESH
        )

    for ref in (LZ, LY, LD, LE, LQ):
        ref[...] = jnp.zeros(ref.shape, F32)
    S0[...] = jnp.ones(S0.shape, F32)
    mine = pl.ds(pl.multiple_of(32 * cy, 32), 32)
    own_reaction = pltpu.make_async_copy(reaction_ref.at[:, mine], S0.at[1, pl.ds(4 + 4 * cy, 4), pl.ds(16, 32)], l_sem.at[0])
    own_volume = pltpu.make_async_copy(vol_ref.at[:, mine], VB.at[pl.ds(4 * cy, 4)], l_sem.at[1])
    own_reaction.start()
    own_volume.start()
    slab_reaction = pltpu.make_async_copy(reaction_ref, RS, l_sem.at[2])
    slab_reaction.start()

    barrier = pltpu.get_barrier_semaphore()
    for d in FARTHEST:
        pl.semaphore_signal(barrier, inc=1, device_id=(member, at_slab(d // 4, d % 4)), device_id_type=MESH)
    for d in range(1, 8):
        pl.semaphore_signal(barrier, inc=1, device_id=(lax.rem(member + d, 8), slab), device_id_type=MESH)

    coupling = [[diff_ref[i] * (0.25**level) for i in range(3)] for level in range(4)]
    center = [2.0 * (c[0] + c[1] + c[2]) for c in coupling]

    lane = lax.broadcasted_iota(jnp.int32, (1, LANES), 1)
    one, zero = jnp.ones((1, LANES), F32), jnp.zeros((1, LANES), F32)

    def lane_mask(keep):
        return jnp.where(keep, one, zero)

    row_i = lax.broadcasted_iota(jnp.int32, (LANES, LANES), 0)
    col_i = lax.broadcasted_iota(jnp.int32, (LANES, LANES), 1)

    def half(a):
        return lax.shift_right_logical(a, 1)

    def matrix(keep, value=1.0):
        return jnp.where(keep, jnp.full((LANES, LANES), value, F32), jnp.zeros((LANES, LANES), F32)).astype(BF16)

    Rx[...] = matrix(half(row_i) == col_i, 0.125)
    Px[...] = matrix(row_i == half(col_i))
    for q in range(4):
        block = slice(LANES * q, LANES * q + LANES)
        Rx1[block, :] = matrix((row_i < 64) & (half(row_i) + 32 * q == col_i), 0.125)
        E1[:, block] = matrix((col_i < 64) & (row_i == half(col_i) + 32 * q))
        R3[block, :] = matrix(16 * (2 * q + lax.shift_right_logical(row_i, 6)) + half(row_i & 31) == col_i, 0.125)
        P3[:, block] = matrix(16 * (2 * q + lax.shift_right_logical(col_i, 6)) + half(col_i & 31) == row_i)

    left = [lane_mask(lane > 0) * coupling[0][2], None, lane_mask((lane & 31) > 0) * coupling[2][2], lane_mask((lane & 15) > 0) * coupling[3][2]]
    right = [lane_mask(lane < 127) * coupling[0][2], None, lane_mask((lane & 31) < 31) * coupling[2][2], lane_mask((lane & 15) < 15) * coupling[3][2]]
    WS[...] = jnp.full((8, LANES), weight_ref[0], F32)
    for ref in (SC, UA, UB, VA, VC, S1C, U0a, U0b, U1a, U1b, U2, T1):
        ref[...] = jnp.zeros(ref.shape, F32)

    slab_reaction.wait()
    RT[0] = RS[0] + RS[1]
    RT[1] = RS[2] + RS[3]
    level1 = dot(flat(RT[:, pl.ds(0, 64, stride=2), :] + RT[:, pl.ds(1, 64, stride=2), :]), Rx[...])
    RT[0, 0:64, :] = level1[0:64] + level1[64:128]
    level2 = RT[0, pl.ds(0, 32, stride=2), :] + RT[0, pl.ds(1, 32, stride=2), :]
    groups = jnp.concatenate([level2[8 * k : 8 * k + 8] for k in range(4)], axis=1)
    RG[slab] = dot(jnp.concatenate([groups, groups], axis=0), Rx1[...])[0:8]
    pl.semaphore_wait(barrier, 22)

    def inner(dz, dy):
        return (cz + dz >= 0) & (cz + dz < 4) & (cy + dy >= 0) & (cy + dy < 4)

    def halo0(slot):
        copies = []
        for k, (dz, dy) in enumerate(DIRECTIONS):
            if dy == 0:
                zs, zd = (4, 20) if dz < 0 else (17, 1)
                src, dst = S0.at[slot, pl.ds(zs, 3), pl.ds(16, 32)], S0.at[slot, pl.ds(zd, 3), pl.ds(16, 32)]
            elif dz == 0:
                src, dst = E0.at[(dy + 1) // 2], LE.at[slot, k - 2]
            else:
                src, dst = E0.at[(dy + 1) // 2, pl.ds(0 if dz < 0 else 7, 1)], LQ.at[slot, k - 4]
            copies.append((
                dz, dy, remote(src, dst, h0_send.at[slot, k], h0_recv.at[slot, k], (member, at_slab(dz, dy)))
            ))
        return copies

    def begin_halo0(slot):
        begin_near(halo0(slot)[:2])
        for edge, row in ((0, 16), (1, 44)):
            for p in range(8):
                E0[edge, p, 0:4, :] = S0[slot, 4 + 2 * p, row : row + 4, :]
                E0[edge, p, 4:8, :] = S0[slot, 5 + 2 * p, row : row + 4, :]
        begin_near(halo0(slot)[2:])

    def finish_halo0(slot):
        finish_near(halo0(slot))
        for k, (dz, dy) in enumerate(DIRECTIONS):
            if dy == 0:
                continue
            row, z0, tiles = (48 if dy < 0 else 12), {-1: 20, 0: 4, 1: 2}[dz], 8 if dz == 0 else 1
            for p in range(tiles):
                tile = LE[slot, k - 2, p] if dz == 0 else LQ[slot, k - 4, p]
                S0[slot, z0 + 2 * p, row : row + 4, :] = tile[0:4]
                S0[slot, z0 + 2 * p + 1, row : row + 4, :] = tile[4:8]

    def landing1(k, slot):
        if k < 2:
            return LZ.at[slot, k]
        return LY.at[slot, k - 2] if k < 4 else LD.at[slot, k - 4]

    def halo1(slot):
        copies = []
        for k, (dz, dy) in enumerate(DIRECTIONS):
            z = {-1: pl.ds(0, 3), 0: pl.ds(0, 5), 1: pl.ds(2, 3)}[dz]
            y = {-1: pl.ds(0, 8), 0: pl.ds(0, 24), 1: pl.ds(16, 8)}[dy]
            copies.append((
                dz, dy,
                remote(
                    P1.at[z, y], landing1(k, slot),
                    h1_send.at[slot, k], h1_recv.at[slot, k], (member, at_slab(dz, dy)),
                ),
            ))
        return copies

    def begin_near(copies):
        for dz, dy, c in copies:
            pl.when(inner(dz, dy))(c.start)

    def begin_halo1(slot):
        for p in range(5):
            P1[p] = S1C[4 + 2 * p, 8:32, :] + lane_roll(S1C[5 + 2 * p, 8:32, :], 64)
        begin_near(halo1(slot))

    def finish_near(copies):
        for dz, dy, c in copies:
            pl.when(inner(-dz, -dy))(c.wait_recv)
        for dz, dy, c in copies:
            pl.when(inner(dz, dy))(c.wait_send)

    def gather(slot):
        return [
            remote(
                G.at[slot, slab], G.at[slot, slab],
                g_send.at[slot], g_recv.at[slot], (member, at_slab(d // 4, d % 4)),
            )
            for d in FARTHEST
        ]

    def finish_gather(slot):
        all_of_them = G.at[slot, 0:15]
        pltpu.make_async_copy(all_of_them, all_of_them, g_recv.at[slot]).wait()

    def finish_gather_sends(slot):
        all_of_them = G.at[slot, 0:15]
        pltpu.make_async_copy(all_of_them, all_of_them, g_send.at[slot]).wait()

    def begin(copies):
        for c in copies:
            c.start()

    def finish(copies):
        for c in copies:
            c.wait()

    def to_blocks(src, dst, dst_z, dst_y, send, recv):
        copies = []
        for d in range(1, 4):
            to = lax.rem(cy + d, 4)
            copies.append(
                remote(
                    src.at[:, pl.ds(pl.multiple_of(32 * to, 32), 32)],
                    dst.at[pl.ds(dst_z + 4 * cy, 4), pl.ds(dst_y, 32)],
                    send.at[d - 1], recv.at[d - 1], (member, cz * 4 + to),
                )
            )
        return copies

    def to_slabs(src, src_z, src_y, dst, send, recv):
        copies = []
        for d in range(1, 4):
            to = lax.rem(cy + d, 4)
            copies.append(
                remote(
                    src.at[pl.ds(src_z + 4 * to, 4), pl.ds(src_y, 32)],
                    dst.at[:, pl.ds(pl.multiple_of(32 * cy, 32), 32)],
                    send.at[d - 1], recv.at[d - 1], (member, cz * 4 + to),
                )
            )
        return copies

    reaction_moves = to_blocks(reaction_ref, S0.at[1], 4, 16, ra_send, ra_recv)
    volume_moves = to_blocks(vol_ref, VB, 0, 0, va_send, va_recv)
    begin(reaction_moves)
    begin([
        remote(RG.at[slab], RG.at[slab], rg_sem.at[0], rg_sem.at[1], (member, at_slab(d // 4, d % 4))) for d in FARTHEST
    ])
    weight_moves = [
        remote(WS, WB.at[d], w_send.at[d - 1], w_recv.at[d - 1], (lax.rem(member + d, 8), slab)) for d in range(1, 8)
    ]

    def neighbours(level, u, z, n, lo, rows):
        c = coupling[level]
        mid = u[pl.ds(z, n), lo : lo + rows, :]
        total = c[0] * (u[pl.ds(z - 1, n), lo : lo + rows, :] + u[pl.ds(z + 1, n), lo : lo + rows, :])
        total += c[1] * (u[pl.ds(z, n), lo - 1 : lo + rows - 1, :] + u[pl.ds(z, n), lo + 1 : lo + rows + 1, :])
        if level == 0:
            total += left[0] * lane_roll(mid, 1) + right[0] * lane_roll(mid, -1)
        else:
            total += c[2] * (lane_roll(mid, 1) + lane_roll(mid, -1))
        return mid, total

    def over(z0, count, step, body):
        for z in range(z0, z0 + count, step):
            body(z)

    def sweep(level, u, s, d, z, n, lo, rows):
        mid, total = neighbours(level, u, z, n, lo, rows)
        return (1.0 - OMEGA) * mid + d[pl.ds(z, n), lo : lo + rows, :] * (s[pl.ds(z, n), lo : lo + rows, :] + total)

    def residual(level, u, s, dg, z, n, lo, rows):
        mid, total = neighbours(level, u, z, n, lo, rows)
        return s[pl.ds(z, n), lo : lo + rows, :] - dg[pl.ds(z, n), lo : lo + rows, :] * mid + total

    def restrict0(fine):
        def body(z):
            a = fine(z)
            for k in range(2):
                T0[(z - 2) // 2 + k] = a[2 * k] + a[2 * k + 1]

        over(2, 20, 4, body)

        def rows(i):
            e = T0[pl.ds(i, 5), pl.ds(0, 24, stride=2), :] + T0[pl.ds(i, 5), pl.ds(1, 24, stride=2), :]
            S1C[pl.ds(4 + i, 5), 8:32, :] = dot(flat(e), Rx[...]).reshape(5, 24, LANES)

        over(0, 10, 5, rows)

    def restrict1(fine, slot):
        def body(z):
            a = fine(z)
            for k in range(4):
                T1[(z - 1) // 2 + k, 4:28, :] = a[2 * k] + a[2 * k + 1]

        over(1, 16, 8, body)
        e = T1[:, pl.ds(0, 16, stride=2), :] + T1[:, pl.ds(1, 16, stride=2), :]
        own = jnp.concatenate([e[2], e[3], e[4], e[5]], axis=1)
        sides = jnp.concatenate([e[6], e[7], e[0], e[1]], axis=1)
        m = dot(jnp.concatenate([own, sides], axis=0), Rx1[...]).reshape(2, 16, LANES)
        G[slot, slab, 0:8, :] = m[0, 4:12]
        G[slot, slab, 8:16, :] = m[1, 4:12]
        for row, part in ((16, m[0, 12:14]), (18, m[1, 12:14]), (20, m[1, 2:4]), (22, m[0, 2:4])):
            G[slot, slab, row : row + 2, :] = part

    upper_half, row8 = lane >= 64, lax.broadcasted_iota(jnp.int32, (8, LANES), 0)
    nothing = jnp.zeros((8, LANES), F32)

    def gathered(slot):
        def rows(c, j, g):
            below = G[slot, 4 * c + j - 1, 16:24, :] if j > 0 else nothing
            above = G[slot, 4 * c + j + 1, 16:24, :] if j < 3 else nothing
            if g:
                below = pltpu.roll(below, 6, 0) if j > 0 else nothing
                above = pltpu.roll(above, 2, 0) if j < 3 else nothing
            near = jnp.where(row8 < 2, below, jnp.where(row8 >= 6, above, nothing))
            return G[slot, 4 * c + j, 8 * g : 8 * g + 8, :] + near

        for j in range(4):
            side = [nothing] + [rows(c, j, 1) for c in range(4)] + [nothing]
            for c in range(4):
                S2[c, 8 * j : 8 * j + 8, :] = rows(c, j, 0) + jnp.where(upper_half, side[c + 2], side[c])

    def restrict2(a):
        T2[...] = a
        e = T2[:, pl.ds(0, 16, stride=2), :] + T2[:, pl.ds(1, 16, stride=2), :]
        return dot(jnp.concatenate([e[0], e[1], e[2], e[3]], axis=1), R3[...])

    first_chunk, last_chunk = lane < 32, lane >= 96
    plane2 = jnp.zeros((1, 32, LANES), F32)

    def neighbours2():
        c = coupling[2]
        mid = U2[1:5, 8:40, :]
        up, down = lane_roll(mid, 32), lane_roll(mid, -32)
        before = jnp.where(first_chunk, jnp.concatenate([plane2, up[:3]], axis=0), up)
        after = jnp.where(last_chunk, jnp.concatenate([down[1:], plane2], axis=0), down)
        total = c[0] * (before + after) + c[1] * (U2[1:5, 7:39, :] + U2[1:5, 9:41, :])
        total += left[2] * lane_roll(mid, 1) + right[2] * lane_roll(mid, -1)
        return mid, total

    def sweep2():
        mid, total = neighbours2()
        U2[1:5, 8:40, :] = (1.0 - OMEGA) * mid + D2[...] * (S2[...] + total)

    row16 = lax.broadcasted_iota(jnp.int32, (16, LANES), 0)
    zeros16, ones16 = jnp.zeros((16, LANES), F32), jnp.ones((16, LANES), F32)
    up3 = jnp.where(row16 > 0, ones16, zeros16) * coupling[3][1]
    down3 = jnp.where(row16 < 15, ones16, zeros16) * coupling[3][1]
    before3 = lane_mask(lane >= 16) * coupling[3][0]
    after3 = lane_mask(lane < 112) * coupling[3][0]

    def coefficients3(d):
        for i, c in enumerate((before3, after3, up3, down3, left[3], right[3])):
            K3[i] = d * c
        D3[...] = d

    def level3(s):
        k = [K3[i] for i in range(6)]
        base = D3[...] * s
        u = base
        for _ in range(COARSE_SWEEPS - 1):
            z = k[0] * lane_roll(u, 16) + k[1] * lane_roll(u, -16)
            y = k[2] * pltpu.roll(u, 1, 0) + k[3] * pltpu.roll(u, 15, 0)
            x = k[4] * lane_roll(u, 1) + k[5] * lane_roll(u, -1)
            u = (base + (1.0 - OMEGA) * u + y) + (z + x)
        return u

    def inside(level, z, n, lo, rows):
        g = GEOMETRY[level]
        zi = lax.broadcasted_iota(jnp.int32, (n, rows, LANES), 0) + (z - g["own_z"] + g["nz"] * cz)
        yi = lax.broadcasted_iota(jnp.int32, (n, rows, LANES), 1) + (lo - g["own_y"] + g["ny"] * cy)
        keep = (zi >= 0) & (zi < 4 * g["nz"]) & (yi >= 0) & (yi < 4 * g["ny"])
        if level:
            keep = keep & (lax.broadcasted_iota(jnp.int32, (n, rows, LANES), 2) < 64)
        return keep

    finish(reaction_moves)
    own_reaction.wait()
    begin_halo0(1)
    SC[4:20, 16:48, :] = S0[1, 4:20, 16:48, :]
    restrict0(lambda z: SC[pl.ds(z, 4), 8:56, :])
    begin_halo1(1)
    begin(volume_moves)
    begin(weight_moves)
    own_volume.wait()

    def summed1(slot):
        finish_near(halo1(slot))
        S1[1:17, 8:32, :] = S1C[1:17, 8:32, :]
        for k, (dz, dy) in enumerate(DIRECTIONS):
            z0, tiles = {-1: (12, 3), 0: (4, 5), 1: (0, 3)}[dz]
            y = {-1: slice(24, 32), 0: slice(8, 32), 1: slice(8, 16)}[dy]
            for p in range(tiles):
                both = landing1(k, slot)[p]
                for z, part in ((z0 + 2 * p, both), (z0 + 2 * p + 1, lane_roll(both, 64))):
                    if 1 <= z < 17:
                        S1[z, y, :] += jnp.where(upper_half, jnp.zeros_like(part), part)

    finish_halo0(1)

    def diag0(z):
        diag = S0[1, pl.ds(z, 2), 8:56, :] + center[0]
        DG0[pl.ds(z, 2), 8:56, :] = diag
        D0[pl.ds(z, 2), 8:56, :] = jnp.where(inside(0, z, 2, 8, 48), OMEGA / diag, jnp.zeros((2, 48, LANES), F32))

    over(1, 22, 2, diag0)
    summed1(1)

    def diag1(z):
        diag = S1[pl.ds(z, 2), 8:32, :] + center[1]
        DG1[pl.ds(z, 2), 8:32, :] = diag
        D1[pl.ds(z, 2), 8:32, :] = jnp.where(inside(1, z, 2, 8, 24), OMEGA / diag, jnp.zeros((2, 24, LANES), F32))

    over(1, 16, 2, diag1)
    tiles = RG.at[0:15]
    pltpu.make_async_copy(tiles, tiles, rg_sem.at[1]).wait()
    pltpu.make_async_copy(tiles, tiles, rg_sem.at[0]).wait()
    for c in range(4):
        for k in range(4):
            rows = jnp.zeros((8, LANES), F32)
            for j in range(4):
                rows = jnp.where((lane >= 32 * j) & (lane < 32 * j + 32), lane_roll(RG[4 * c + j], 32 * (j - k)), rows)
            S2[c, 8 * k : 8 * k + 8, :] = rows
    DG2[...] = S2[...] + center[2]
    D2[...] = OMEGA / DG2[...]
    coefficients3(OMEGA / (restrict2(S2[...]) + center[3]))
    SC[4:20, 16:48, :] = jnp.ones((16, 32, LANES), F32)
    finish(volume_moves)
    finish(weight_moves)
    weight_total = WS[...]
    for d in range(1, 8):
        weight_total += WB[d]
    IW[...] = 1.0 / weight_total

    def vcycle(n, slot):
        UA[4:20, 16:48, :] = D0[4:20, 16:48, :] * SC[4:20, 16:48, :]

        def own0(z):
            UB[pl.ds(z, 3), 8:56, :] = sweep(0, UA, SC, D0, z, 3, 8, 48)

        over(3, 18, 3, own0)
        restrict0(lambda z: residual(0, UB, SC, DG0, z, 4, 8, 48))
        begin_halo1(slot)
        VA[4:14, 8:32, :] = D1[4:14, 8:32, :] * S1C[4:14, 8:32, :]

        def own1(z):
            VC[pl.ds(z, 6), 8:32, :] = sweep(1, VA, S1C, D1, z, 6, 8, 24)

        over(3, 12, 6, own1)
        restrict1(lambda z: residual(1, VC, S1C, DG1, z, 8, 8, 24), slot)
        begin(gather(slot))

        @pl.when(n > 0)
        def _():
            finish_halo0(slot)

        source0 = S0.at[slot]

        def first0(z):
            U0a[pl.ds(z, 2), 8:56, :] = D0[pl.ds(z, 2), 8:56, :] * source0[pl.ds(z, 2), 8:56, :]

        over(1, 22, 2, first0)

        def pre0(z):
            U0b[pl.ds(z, 4), 8:56, :] = sweep(0, U0a, source0, D0, z, 4, 8, 48)

        over(2, 20, 4, pre0)
        summed1(slot)
        U1a[1:17, 8:32, :] = D1[1:17, 8:32, :] * S1[1:17, 8:32, :]

        def pre1(z):
            U1b[pl.ds(z, 7), 8:32, :] = sweep(1, U1a, S1, D1, z, 7, 8, 24)

        over(2, 14, 7, pre1)

        finish_gather(slot)
        gathered(slot)
        U2[1:5, 8:40, :] = D2[...] * S2[...]
        sweep2()
        mid, total = neighbours2()
        u3 = level3(restrict2(S2[...] - DG2[...] * mid + total))
        p = dot(u3, P3[...])
        for k in range(4):
            C2[k, pl.ds(0, 16, stride=2), :] = p[:, LANES * k : LANES * k + LANES]
            C2[k, pl.ds(1, 16, stride=2), :] = p[:, LANES * k : LANES * k + LANES]
        U2[1:5, 8:40, :] += C2[...]
        sweep2()
        sweep2()

        finish_gather_sends(slot)

        window = pl.ds(pl.multiple_of(8 * cy, 8), 24)
        own = U2[1 + cz, window, :][4:20]
        sides = jnp.where(upper_half, U2[cz, window, :][4:20], U2[2 + cz, window, :][4:20])
        wide = dot(jnp.concatenate([own, sides], axis=0), E1[...])
        for k in range(8):
            r, q = (0, k - 2) if 2 <= k < 6 else (16, (k - 2) % 4)
            C1[k, pl.ds(0, 16, stride=2), :] = wide[r : r + 16, LANES * q : LANES * q + LANES]
            C1[k, pl.ds(1, 16, stride=2), :] = wide[r : r + 16, LANES * q : LANES * q + LANES]
        for k in range(8):
            U1b[1 + 2 * k, 8:32, :] += C1[k, 4:28, :]
            U1b[2 + 2 * k, 8:32, :] += C1[k, 4:28, :]

        def post1a(z):
            U1a[pl.ds(z, 6), 8:32, :] = sweep(1, U1b, S1, D1, z, 6, 8, 24)

        over(3, 12, 6, post1a)

        def post1b(z):
            U1b[pl.ds(z, 5), 8:32, :] = sweep(1, U1a, S1, D1, z, 5, 8, 24)

        over(4, 10, 5, post1b)

        def widen0(i):
            wide = dot(flat(U1b[pl.ds(4 + i, 5), 8:32, :]), Px[...]).reshape(5, 24, LANES)
            C0[:, pl.ds(0, 24, stride=2), :] = wide
            C0[:, pl.ds(1, 24, stride=2), :] = wide
            for k in range(5):
                U0b[2 + 2 * (i + k), 8:56, :] += C0[k]
                U0b[3 + 2 * (i + k), 8:56, :] += C0[k]

        over(0, 10, 5, widen0)

        def post0a(z):
            U0a[pl.ds(z, 3), 8:56, :] = sweep(0, U0b, source0, D0, z, 3, 8, 48)

        over(3, 18, 3, post0a)

        def post0b(z):
            return sweep(0, U0a, source0, D0, z, 4, 16, 32)

        @pl.when(slot == 0)
        def _():
            for z in range(4, 20, 4):
                p = VB[z - 4 : z] / post0b(z)
                S0[1, z : z + 4, 16:48, :] = p
                SC[z : z + 4, 16:48, :] = p

        @pl.when(slot == 1)
        def _():
            for z in range(4, 20, 4):
                MB[z - 4 : z] = post0b(z)

    def centroid(last):
        sibling = (member + 1 - 2 * mc, slab)

        def marginal(at):
            m = S0[0, pl.ds(4 + at, 4), 16:48, :] * MB[pl.ds(at, 4)]
            MB[pl.ds(at, 4)] = m
            LB[pl.ds(at, 4)] = weight_ref[0] * jnp.log(m)

        def update(at):
            p = QB[at] * CB[at]
            S0[0, 4 + at, 16:48, :] = p
            SC[4 + at, 16:48, :] = p

        def along_x(d):
            return (2 * lax.rem(mx + d, 4) + mc, slab)

        swaps, pieces, spread, passed = [], [], [], []
        for q in range(2):
            marginal(8 * q + 4 * (1 - mc))
            theirs, here = LB.at[pl.ds(8 * q + 4 * (1 - mc), 4)], XB.at[pl.ds(4 * q, 4)]
            swaps.append(remote(theirs, here, x_send.at[q], x_recv.at[q], sibling))
            swaps[q].start()
        for q in range(2):
            marginal(8 * q + 4 * mc)

        for q in range(2):
            swaps[q].wait_recv()
            HB[4 * q : 4 * q + 4] = LB[pl.ds(8 * q + 4 * mc, 4)] + XB[4 * q : 4 * q + 4]
            pieces.append([])
            for d in (2, 1, 3):
                part = HB.at[pl.ds(4 * q + lax.rem(mx + d, 4), 1)]
                pieces[q].append(remote(part, PB.at[q, d - 1], p_send.at[q, d - 1], p_recv.at[q, d - 1], along_x(d)))
            begin(pieces[q])

        for z in range(0, 16, 4):
            QB[z : z + 4] = S0[0, 4 + z : 8 + z, 16:48, :] / MB[z : z + 4]

        @pl.when(last)
        def _():
            begin(multiplier_moves())
            mult_out[:, mine, :] = QB[pl.ds(4 * cy, 4)]

        inverse = jnp.broadcast_to(IW[...][None], (4, 8, LANES)).reshape(1, 32, LANES)
        for q in range(2):
            for c in pieces[q]:
                c.wait_recv()
            total = HB[pl.ds(4 * q + mx, 1)] + PB[q, 0] + PB[q, 1] + PB[q, 2]
            own = 8 * q + 4 * mc + mx
            CB[pl.ds(own, 1)] = jnp.exp(total * inverse)
            made = CB.at[pl.ds(own, 1)]
            spread.append([remote(made, made, c_send.at[q, d - 1], c_recv.at[q, d - 1], along_x(d)) for d in (2, 1, 3)])
            passed.append([])
            for d in (0, 1, 3, 2):
                at = CB.at[pl.ds(8 * q + 4 * mc + lax.rem(mx - d + 4, 4), 1)]
                passed[q].append((d, remote(at, at, f_send.at[q, d], f_recv.at[q, d], sibling)))

            @pl.when(jnp.logical_not(last))
            def _():
                begin(spread[q])
                passed[q][0][1].start()
                update(own)

            @pl.when(last)
            def _():
                begin_slabs(q, own)

        @pl.when(jnp.logical_not(last))
        def _():
            for q in range(2):
                for (d, c), arrived in zip(passed[q][1:], spread[q][1:] + spread[q][:1]):
                    arrived.wait_recv()
                    c.start()
                    update(8 * q + 4 * mc + lax.rem(mx - d + 4, 4))
            for q in range(2):
                for d, c in passed[q]:
                    c.wait_recv()
                    update(8 * q + 4 * (1 - mc) + lax.rem(mx - d + 4, 4))
            for q in range(2):
                for c in spread[q] + [f for _, f in passed[q]]:
                    c.wait_send()

        @pl.when(last)
        def _():
            finish_slabs()

        for q in range(2):
            for c in [swaps[q]] + pieces[q]:
                c.wait_send()

    def slab_pieces(q, own):
        made, place = CB.at[pl.ds(own, 1)], cent_out.at[pl.ds(mx, 1), mine]
        return [
            remote(made, place, e_send.at[q, d], e_recv.at[d, cy], (2 * lax.rem(mx + d, 4) + mc, cz * 4 + 2 * q + mc))
            for d in range(4)
        ]

    def begin_slabs(q, own):
        home, copies = cy == 2 * q + mc, slab_pieces(q, own)
        for d in (2, 1, 3):
            copies[d].start()
        pl.when(jnp.logical_not(home))(copies[0].start)

        @pl.when(home)
        def _():
            cent_out[pl.ds(mx, 1), mine, :] = CB[pl.ds(own, 1)]

    def finish_slabs():
        receiver = lax.rem(cy, 2) == mc
        sibling = (member + 1 - 2 * mc, slab)

        def piece(d, e):
            return cent_out.at[pl.ds(lax.rem(mx - d + 4, 4), 1), pl.ds(32 * e, 32)]

        def passing(d, e):
            return remote(piece(d, e), piece(d, e), k_send.at[d, e], k_recv.at[d, e], sibling)

        order = [(d, e) for d in (0, 1, 3, 2) for e in range(4)]

        @pl.when(receiver)
        def _():
            for d, e in order:
                arrival = remote(piece(d, e), piece(d, e), e_send.at[0, d], e_recv.at[d, e], sibling)
                if d == 0:
                    pl.when(cy != e)(arrival.wait_recv)
                else:
                    arrival.wait_recv()
                passing(d, e).start()
            for d, e in order:
                passing(d, e).wait_send()

        @pl.when(jnp.logical_not(receiver))
        def _():
            for d, e in order:
                passing(d, e).wait_recv()

        for q in range(2):
            copies = slab_pieces(q, 8 * q + 4 * mc + mx)
            for d in (1, 2, 3):
                copies[d].wait_send()
            pl.when(cy != 2 * q + mc)(copies[0].wait_send)
        finish(multiplier_moves())

    def multiplier_moves():
        return to_slabs(QB, 0, 0, mult_out, o_send, o_recv)

    def half_step(n, slot):
        vcycle(n, slot)

        @pl.when(slot == 1)
        def _():
            centroid(n == 2 * ITERS - 1)

        @pl.when(n < 2 * ITERS - 1)
        def _():
            begin_halo0(1 - slot)


    def iteration(i, _):
        half_step(2 * i, 0)
        half_step(2 * i + 1, 1)
        return 0

    lax.fori_loop(0, ITERS, iteration, 0)

    mult_out[...] = mult_out[...] * cent_out[...]


def body(nonnegative_volumes, reaction, diffusivity, member_weights):
    vmem, smem = pl.BlockSpec(memory_space=pltpu.VMEM), pl.BlockSpec(memory_space=pltpu.SMEM)
    hbm = pl.BlockSpec(memory_space=pl.ANY)
    field = jax.ShapeDtypeStruct((4, 128, 128), F32)

    def buffer(*shape):
        return pltpu.VMEM((*shape, LANES), F32)

    dma = pltpu.SemaphoreType.DMA
    scratch = [
        buffer(2, 24, 64), *[buffer(24, 64) for _ in range(7)], buffer(5, 48), buffer(10, 48),
        *[buffer(18, 40) for _ in range(8)], buffer(8, 32), buffer(8, 32), buffer(5, 24),
        buffer(2, 2, 3, 24), buffer(2, 2, 5, 8), buffer(2, 4, 3, 8), buffer(2, 8, 8), buffer(2, 2, 8, 8), buffer(2, 4, 1, 8),
        buffer(2, 16, 24), buffer(4, 32), buffer(4, 32), buffer(4, 32), buffer(6, 48), buffer(4, 32), buffer(4, 32), buffer(16), buffer(6, 16),
        buffer(4, 128), buffer(2, 128), buffer(16, 8),
        buffer(16, 32), buffer(16, 32), buffer(16, 32), buffer(16, 32), buffer(8, 32), buffer(8, 32), buffer(2, 3, 1, 32), buffer(16, 32),
        buffer(8), buffer(8, 8), buffer(8),
        *[pltpu.VMEM(shape, BF16) for shape in ((128, 128), (512, 128), (512, 128), (128, 512), (128, 512), (128, 128))],
        dma((2, 8)), dma((2, 8)), dma((2, 8)), dma((2, 8)), dma((2,)), dma((2,)),
        dma((3,)), dma((3,)), dma((3,)), dma((3,)), dma((7,)), dma((7,)),
        dma((3,)), dma((2,)), dma((2,)), dma((2,)), *[dma((2, 3)) for _ in range(4)], dma((2, 4)), dma((2, 4)), dma((3,)), dma((3,)),
        dma((2, 4)), dma((4, 4)), dma((4, 4)), dma((4, 4)),
    ]
    centroid, multipliers = pl.pallas_call(
        kernel,
        out_shape=(field, field),
        in_specs=[hbm, hbm, smem, smem],
        out_specs=(vmem, vmem),
        scratch_shapes=scratch,
        compiler_params=pltpu.CompilerParams(collective_id=0, has_side_effects=True, vmem_limit_bytes=40 * 2**20),
    )(nonnegative_volumes[0], reaction, diffusivity, member_weights)
    return centroid, multipliers[None]


def solution(mesh):
    return jax.shard_map(
        body,
        mesh=mesh,
        in_specs=(P("member", "slab", None, None), P("slab", None, None), P(), P("member")),
        out_specs=(P("slab", None, None), P("member", "slab", None, None)),
        check_vma=False,
    )
```

```python
import jax
import jax.numpy as jnp
from jax import lax
from jax.experimental import pallas as pl
from jax.experimental.pallas import tpu as pltpu
from jax.sharding import PartitionSpec as P

ITERS = 3
COARSE_SWEEPS = 8
OMEGA = 0.8
LANES = 128
NZ, NY = 64, 128
F32, BF16 = jnp.float32, jnp.bfloat16
MESH = pl.DeviceIdType.MESH
FARTHEST = sorted(range(1, 16), key=lambda d: -min(d // 4, 4 - d // 4) - min(d % 4, 4 - d % 4))
DIRECTIONS = ((-1, 0), (1, 0), (0, -1), (0, 1), (-1, -1), (-1, 1), (1, -1), (1, 1))

GEOMETRY = (dict(own_z=4, own_y=16, nz=16, ny=32), dict(own_z=5, own_y=12, nz=8, ny=16))


def dot(a, b):
    high = a.astype(BF16)
    low = (a - high.astype(F32)).astype(BF16)
    return jnp.dot(high, b, preferred_element_type=F32) + jnp.dot(low, b, preferred_element_type=F32)


def flat(a):
    return a.reshape(-1, LANES)


def lane_roll(a, shift):
    return pltpu.roll(flat(a), shift % LANES, 1).reshape(a.shape)


def kernel(
    vol_ref, reaction_ref, diff_ref, weight_ref, cent_out, mult_out,
    S0, SC, D0, DG0, UA, UB, U0a, U0b, C0, T0,
    S1, S1C, D1, DG1, VA, VC, U1a, U1b, C1, T1, P1, LZ, LY, LD, E0, LE, LQ,
    G, S2, D2, DG2, U2, T2, C2, D3, K3,
    RS, RT, RG, VB, QB, MB, LB, XB, HB, PB, CB, WS, WB, IW,
    Rx, Rx1, R3, P3, E1, Px,
    h0_send, h0_recv, h1_send, h1_recv, g_send, g_recv,
    ra_send, ra_recv, va_send, va_recv, w_send, w_recv,
    l_sem, rg_sem, x_send, x_recv, p_send, p_recv, c_send, c_recv, f_send, f_recv, o_send, o_recv, e_send, e_recv, k_send, k_recv,
):
    member, slab = lax.axis_index("member"), lax.axis_index("slab")
    cz, cy = slab // 4, lax.rem(slab, 4)
    mx, mc = member // 2, lax.rem(member, 2)

    def at_slab(dz, dy):
        return lax.rem(cz + dz + 4, 4) * 4 + lax.rem(cy + dy + 4, 4)

    def remote(src, dst, send, recv, to):
        return pltpu.make_async_remote_copy(
            src_ref=src, dst_ref=dst, send_sem=send, recv_sem=recv, device_id=to, device_id_type=MESH
        )

    for ref in (LZ, LY, LD, LE, LQ):
        ref[...] = jnp.zeros(ref.shape, F32)
    S0[...] = jnp.ones(S0.shape, F32)
    mine = pl.ds(pl.multiple_of(32 * cy, 32), 32)
    own_reaction = pltpu.make_async_copy(reaction_ref.at[:, mine], S0.at[1, pl.ds(4 + 4 * cy, 4), pl.ds(16, 32)], l_sem.at[0])
    own_volume = pltpu.make_async_copy(vol_ref.at[:, mine], VB.at[pl.ds(4 * cy, 4)], l_sem.at[1])
    own_reaction.start()
    own_volume.start()
    slab_reaction = pltpu.make_async_copy(reaction_ref, RS, l_sem.at[2])
    slab_reaction.start()

    barrier = pltpu.get_barrier_semaphore()
    for d in FARTHEST:
        pl.semaphore_signal(barrier, inc=1, device_id=(member, at_slab(d // 4, d % 4)), device_id_type=MESH)
    for d in range(1, 8):
        pl.semaphore_signal(barrier, inc=1, device_id=(lax.rem(member + d, 8), slab), device_id_type=MESH)

    coupling = [[diff_ref[i] * (0.25**level) for i in range(3)] for level in range(4)]
    center = [2.0 * (c[0] + c[1] + c[2]) for c in coupling]

    lane = lax.broadcasted_iota(jnp.int32, (1, LANES), 1)
    one, zero = jnp.ones((1, LANES), F32), jnp.zeros((1, LANES), F32)

    def lane_mask(keep):
        return jnp.where(keep, one, zero)

    row_i = lax.broadcasted_iota(jnp.int32, (LANES, LANES), 0)
    col_i = lax.broadcasted_iota(jnp.int32, (LANES, LANES), 1)

    def half(a):
        return lax.shift_right_logical(a, 1)

    def matrix(keep, value=1.0):
        return jnp.where(keep, jnp.full((LANES, LANES), value, F32), jnp.zeros((LANES, LANES), F32)).astype(BF16)

    Rx[...] = matrix(half(row_i) == col_i, 0.125)
    Px[...] = matrix(row_i == half(col_i))
    for q in range(4):
        block = slice(LANES * q, LANES * q + LANES)
        Rx1[block, :] = matrix((row_i < 64) & (half(row_i) + 32 * q == col_i), 0.125)
        E1[:, block] = matrix((col_i < 64) & (row_i == half(col_i) + 32 * q))
        R3[block, :] = matrix(16 * (2 * q + lax.shift_right_logical(row_i, 6)) + half(row_i & 31) == col_i, 0.125)
        P3[:, block] = matrix(16 * (2 * q + lax.shift_right_logical(col_i, 6)) + half(col_i & 31) == row_i)

    left = [lane_mask(lane > 0) * coupling[0][2], None, lane_mask((lane & 31) > 0) * coupling[2][2], lane_mask((lane & 15) > 0) * coupling[3][2]]
    right = [lane_mask(lane < 127) * coupling[0][2], None, lane_mask((lane & 31) < 31) * coupling[2][2], lane_mask((lane & 15) < 15) * coupling[3][2]]
    WS[...] = jnp.full((8, LANES), weight_ref[0], F32)
    for ref in (SC, UA, UB, VA, VC, S1C, U0a, U0b, U1a, U1b, U2, T1):
        ref[...] = jnp.zeros(ref.shape, F32)

    slab_reaction.wait()
    RT[0] = RS[0] + RS[1]
    RT[1] = RS[2] + RS[3]
    level1 = dot(flat(RT[:, pl.ds(0, 64, stride=2), :] + RT[:, pl.ds(1, 64, stride=2), :]), Rx[...])
    RT[0, 0:64, :] = level1[0:64] + level1[64:128]
    level2 = RT[0, pl.ds(0, 32, stride=2), :] + RT[0, pl.ds(1, 32, stride=2), :]
    groups = jnp.concatenate([level2[8 * k : 8 * k + 8] for k in range(4)], axis=1)
    RG[slab] = dot(jnp.concatenate([groups, groups], axis=0), Rx1[...])[0:8]
    pl.semaphore_wait(barrier, 22)

    def inner(dz, dy):
        return (cz + dz >= 0) & (cz + dz < 4) & (cy + dy >= 0) & (cy + dy < 4)

    def halo0(slot):
        copies = []
        for k, (dz, dy) in enumerate(DIRECTIONS):
            if dy == 0:
                zs, zd = (4, 20) if dz < 0 else (17, 1)
                src, dst = S0.at[slot, pl.ds(zs, 3), pl.ds(16, 32)], S0.at[slot, pl.ds(zd, 3), pl.ds(16, 32)]
            elif dz == 0:
                src, dst = E0.at[(dy + 1) // 2], LE.at[slot, k - 2]
            else:
                src, dst = E0.at[(dy + 1) // 2, pl.ds(0 if dz < 0 else 7, 1)], LQ.at[slot, k - 4]
            copies.append((
                dz, dy, remote(src, dst, h0_send.at[slot, k], h0_recv.at[slot, k], (member, at_slab(dz, dy)))
            ))
        return copies

    def begin_halo0(slot):
        begin_near(halo0(slot)[:2])
        for edge, row in ((0, 16), (1, 44)):
            for p in range(8):
                E0[edge, p, 0:4, :] = S0[slot, 4 + 2 * p, row : row + 4, :]
                E0[edge, p, 4:8, :] = S0[slot, 5 + 2 * p, row : row + 4, :]
        begin_near(halo0(slot)[2:])

    def finish_halo0(slot):
        finish_near(halo0(slot))
        for k, (dz, dy) in enumerate(DIRECTIONS):
            if dy == 0:
                continue
            row, z0, tiles = (48 if dy < 0 else 12), {-1: 20, 0: 4, 1: 2}[dz], 8 if dz == 0 else 1
            for p in range(tiles):
                tile = LE[slot, k - 2, p] if dz == 0 else LQ[slot, k - 4, p]
                S0[slot, z0 + 2 * p, row : row + 4, :] = tile[0:4]
                S0[slot, z0 + 2 * p + 1, row : row + 4, :] = tile[4:8]

    def landing1(k, slot):
        if k < 2:
            return LZ.at[slot, k]
        return LY.at[slot, k - 2] if k < 4 else LD.at[slot, k - 4]

    def halo1(slot):
        copies = []
        for k, (dz, dy) in enumerate(DIRECTIONS):
            z = {-1: pl.ds(0, 3), 0: pl.ds(0, 5), 1: pl.ds(2, 3)}[dz]
            y = {-1: pl.ds(0, 8), 0: pl.ds(0, 24), 1: pl.ds(16, 8)}[dy]
            copies.append((
                dz, dy,
                remote(
                    P1.at[z, y], landing1(k, slot),
                    h1_send.at[slot, k], h1_recv.at[slot, k], (member, at_slab(dz, dy)),
                ),
            ))
        return copies

    def begin_near(copies):
        for dz, dy, c in copies:
            pl.when(inner(dz, dy))(c.start)

    def begin_halo1(slot):
        for p in range(5):
            P1[p] = S1C[4 + 2 * p, 8:32, :] + lane_roll(S1C[5 + 2 * p, 8:32, :], 64)
        begin_near(halo1(slot))

    def finish_near(copies):
        for dz, dy, c in copies:
            pl.when(inner(-dz, -dy))(c.wait_recv)
        for dz, dy, c in copies:
            pl.when(inner(dz, dy))(c.wait_send)

    def gather(slot):
        return [
            remote(
                G.at[slot, slab], G.at[slot, slab],
                g_send.at[slot], g_recv.at[slot], (member, at_slab(d // 4, d % 4)),
            )
            for d in FARTHEST
        ]

    def finish_gather(slot):
        all_of_them = G.at[slot, 0:15]
        pltpu.make_async_copy(all_of_them, all_of_them, g_recv.at[slot]).wait()

    def finish_gather_sends(slot):
        all_of_them = G.at[slot, 0:15]
        pltpu.make_async_copy(all_of_them, all_of_them, g_send.at[slot]).wait()

    def begin(copies):
        for c in copies:
            c.start()

    def finish(copies):
        for c in copies:
            c.wait()

    def to_blocks(src, dst, dst_z, dst_y, send, recv):
        copies = []
        for d in range(1, 4):
            to = lax.rem(cy + d, 4)
            copies.append(
                remote(
                    src.at[:, pl.ds(pl.multiple_of(32 * to, 32), 32)],
                    dst.at[pl.ds(dst_z + 4 * cy, 4), pl.ds(dst_y, 32)],
                    send.at[d - 1], recv.at[d - 1], (member, cz * 4 + to),
                )
            )
        return copies

    def to_slabs(src, src_z, src_y, dst, send, recv):
        copies = []
        for d in range(1, 4):
            to = lax.rem(cy + d, 4)
            copies.append(
                remote(
                    src.at[pl.ds(src_z + 4 * to, 4), pl.ds(src_y, 32)],
                    dst.at[:, pl.ds(pl.multiple_of(32 * cy, 32), 32)],
                    send.at[d - 1], recv.at[d - 1], (member, cz * 4 + to),
                )
            )
        return copies

    reaction_moves = to_blocks(reaction_ref, S0.at[1], 4, 16, ra_send, ra_recv)
    volume_moves = to_blocks(vol_ref, VB, 0, 0, va_send, va_recv)
    begin(reaction_moves)
    begin([
        remote(RG.at[slab], RG.at[slab], rg_sem.at[0], rg_sem.at[1], (member, at_slab(d // 4, d % 4))) for d in FARTHEST
    ])
    weight_moves = [
        remote(WS, WB.at[d], w_send.at[d - 1], w_recv.at[d - 1], (lax.rem(member + d, 8), slab)) for d in range(1, 8)
    ]

    def neighbours(level, u, z, n, lo, rows):
        c = coupling[level]
        mid = u[pl.ds(z, n), lo : lo + rows, :]
        total = c[0] * (u[pl.ds(z - 1, n), lo : lo + rows, :] + u[pl.ds(z + 1, n), lo : lo + rows, :])
        total += c[1] * (u[pl.ds(z, n), lo - 1 : lo + rows - 1, :] + u[pl.ds(z, n), lo + 1 : lo + rows + 1, :])
        if level == 0:
            total += left[0] * lane_roll(mid, 1) + right[0] * lane_roll(mid, -1)
        else:
            total += c[2] * (lane_roll(mid, 1) + lane_roll(mid, -1))
        return mid, total

    def over(z0, count, step, body):
        for z in range(z0, z0 + count, step):
            body(z)

    def sweep(level, u, s, d, z, n, lo, rows):
        mid, total = neighbours(level, u, z, n, lo, rows)
        return (1.0 - OMEGA) * mid + d[pl.ds(z, n), lo : lo + rows, :] * (s[pl.ds(z, n), lo : lo + rows, :] + total)

    def residual(level, u, s, dg, z, n, lo, rows):
        mid, total = neighbours(level, u, z, n, lo, rows)
        return s[pl.ds(z, n), lo : lo + rows, :] - dg[pl.ds(z, n), lo : lo + rows, :] * mid + total

    def restrict0(fine):
        def body(z):
            a = fine(z)
            for k in range(2):
                T0[(z - 2) // 2 + k] = a[2 * k] + a[2 * k + 1]

        over(2, 20, 4, body)

        def rows(i):
            e = T0[pl.ds(i, 5), pl.ds(0, 24, stride=2), :] + T0[pl.ds(i, 5), pl.ds(1, 24, stride=2), :]
            S1C[pl.ds(4 + i, 5), 8:32, :] = dot(flat(e), Rx[...]).reshape(5, 24, LANES)

        over(0, 10, 5, rows)

    def restrict1(fine, slot):
        def body(z):
            a = fine(z)
            for k in range(4):
                T1[(z - 1) // 2 + k, 4:28, :] = a[2 * k] + a[2 * k + 1]

        over(1, 16, 8, body)
        e = T1[:, pl.ds(0, 16, stride=2), :] + T1[:, pl.ds(1, 16, stride=2), :]
        own = jnp.concatenate([e[2], e[3], e[4], e[5]], axis=1)
        sides = jnp.concatenate([e[6], e[7], e[0], e[1]], axis=1)
        m = dot(jnp.concatenate([own, sides], axis=0), Rx1[...]).reshape(2, 16, LANES)
        G[slot, slab, 0:8, :] = m[0, 4:12]
        G[slot, slab, 8:16, :] = m[1, 4:12]
        for row, part in ((16, m[0, 12:14]), (18, m[1, 12:14]), (20, m[1, 2:4]), (22, m[0, 2:4])):
            G[slot, slab, row : row + 2, :] = part

    upper_half, row8 = lane >= 64, lax.broadcasted_iota(jnp.int32, (8, LANES), 0)
    nothing = jnp.zeros((8, LANES), F32)

    def gathered(slot):
        def rows(c, j, g):
            below = G[slot, 4 * c + j - 1, 16:24, :] if j > 0 else nothing
            above = G[slot, 4 * c + j + 1, 16:24, :] if j < 3 else nothing
            if g:
                below = pltpu.roll(below, 6, 0) if j > 0 else nothing
                above = pltpu.roll(above, 2, 0) if j < 3 else nothing
            near = jnp.where(row8 < 2, below, jnp.where(row8 >= 6, above, nothing))
            return G[slot, 4 * c + j, 8 * g : 8 * g + 8, :] + near

        for j in range(4):
            side = [nothing] + [rows(c, j, 1) for c in range(4)] + [nothing]
            for c in range(4):
                S2[c, 8 * j : 8 * j + 8, :] = rows(c, j, 0) + jnp.where(upper_half, side[c + 2], side[c])

    def restrict2(a):
        T2[...] = a
        even = T2[:, pl.ds(0, 8, stride=4), :] + T2[:, pl.ds(1, 8, stride=4), :]
        odd = T2[:, pl.ds(2, 8, stride=4), :] + T2[:, pl.ds(3, 8, stride=4), :]
        e = jnp.concatenate([even, odd], axis=1)
        return dot(jnp.concatenate([e[0], e[1], e[2], e[3]], axis=1), R3[...])

    first_chunk, last_chunk = lane < 32, lane >= 96
    plane2 = jnp.zeros((1, 32, LANES), F32)

    def neighbours2():
        c = coupling[2]
        mid = U2[1:5, 8:40, :]
        up, down = lane_roll(mid, 32), lane_roll(mid, -32)
        before = jnp.where(first_chunk, jnp.concatenate([plane2, up[:3]], axis=0), up)
        after = jnp.where(last_chunk, jnp.concatenate([down[1:], plane2], axis=0), down)
        total = c[0] * (before + after) + c[1] * (U2[1:5, 7:39, :] + U2[1:5, 9:41, :])
        total += left[2] * lane_roll(mid, 1) + right[2] * lane_roll(mid, -1)
        return mid, total

    def sweep2():
        mid, total = neighbours2()
        U2[1:5, 8:40, :] = (1.0 - OMEGA) * mid + D2[...] * (S2[...] + total)

    row16 = lax.broadcasted_iota(jnp.int32, (16, LANES), 0)
    zeros16, ones16 = jnp.zeros((16, LANES), F32), jnp.ones((16, LANES), F32)
    up3 = jnp.where(row16 != 0, ones16, zeros16) * coupling[3][1]
    down3 = jnp.where(row16 < 15, ones16, zeros16) * coupling[3][1]
    before3 = lane_mask(lane >= 16) * coupling[3][0]
    after3 = lane_mask(lane < 112) * coupling[3][0]

    def coefficients3(d):
        for i, c in enumerate((before3, after3, up3, down3, left[3], right[3])):
            K3[i] = d * c
        D3[...] = d

    def level3(s):
        k = [K3[i] for i in range(6)]
        base = D3[...] * s
        u = base
        for _ in range(COARSE_SWEEPS - 1):
            z = k[0] * lane_roll(u, 16) + k[1] * lane_roll(u, -16)
            even, odd = u[0:8], u[8:16]
            above = jnp.concatenate([pltpu.roll(odd, 1, 0), even], axis=0)
            below = jnp.concatenate([odd, pltpu.roll(even, 7, 0)], axis=0)
            y = k[2] * above + k[3] * below
            x = k[4] * lane_roll(u, 1) + k[5] * lane_roll(u, -1)
            u = (base + (1.0 - OMEGA) * u + y) + (z + x)
        return u

    def inside(level, z, n, lo, rows):
        g = GEOMETRY[level]
        zi = lax.broadcasted_iota(jnp.int32, (n, rows, LANES), 0) + (z - g["own_z"] + g["nz"] * cz)
        yi = lax.broadcasted_iota(jnp.int32, (n, rows, LANES), 1) + (lo - g["own_y"] + g["ny"] * cy)
        keep = (zi >= 0) & (zi < 4 * g["nz"]) & (yi >= 0) & (yi < 4 * g["ny"])
        if level:
            keep = keep & (lax.broadcasted_iota(jnp.int32, (n, rows, LANES), 2) < 64)
        return keep

    finish(reaction_moves)
    own_reaction.wait()
    begin_halo0(1)
    SC[4:20, 16:48, :] = S0[1, 4:20, 16:48, :]
    restrict0(lambda z: SC[pl.ds(z, 4), 8:56, :])
    begin_halo1(1)
    begin(volume_moves)
    begin(weight_moves)
    own_volume.wait()

    def summed1(slot):
        finish_near(halo1(slot))
        S1[1:17, 8:32, :] = S1C[1:17, 8:32, :]
        for k, (dz, dy) in enumerate(DIRECTIONS):
            z0, tiles = {-1: (12, 3), 0: (4, 5), 1: (0, 3)}[dz]
            y = {-1: slice(24, 32), 0: slice(8, 32), 1: slice(8, 16)}[dy]
            for p in range(tiles):
                both = landing1(k, slot)[p]
                for z, part in ((z0 + 2 * p, both), (z0 + 2 * p + 1, lane_roll(both, 64))):
                    if 1 <= z < 17:
                        S1[z, y, :] += jnp.where(upper_half, jnp.zeros_like(part), part)

    finish_halo0(1)

    def diag0(z):
        diag = S0[1, pl.ds(z, 2), 8:56, :] + center[0]
        DG0[pl.ds(z, 2), 8:56, :] = diag
        D0[pl.ds(z, 2), 8:56, :] = jnp.where(inside(0, z, 2, 8, 48), OMEGA / diag, jnp.zeros((2, 48, LANES), F32))

    over(1, 22, 2, diag0)
    summed1(1)

    def diag1(z):
        diag = S1[pl.ds(z, 2), 8:32, :] + center[1]
        DG1[pl.ds(z, 2), 8:32, :] = diag
        D1[pl.ds(z, 2), 8:32, :] = jnp.where(inside(1, z, 2, 8, 24), OMEGA / diag, jnp.zeros((2, 24, LANES), F32))

    over(1, 16, 2, diag1)
    tiles = RG.at[0:15]
    pltpu.make_async_copy(tiles, tiles, rg_sem.at[1]).wait()
    pltpu.make_async_copy(tiles, tiles, rg_sem.at[0]).wait()
    for c in range(4):
        for k in range(4):
            rows = jnp.zeros((8, LANES), F32)
            for j in range(4):
                rows = jnp.where((lane >= 32 * j) & (lane < 32 * j + 32), lane_roll(RG[4 * c + j], 32 * (j - k)), rows)
            S2[c, 8 * k : 8 * k + 8, :] = rows
    DG2[...] = S2[...] + center[2]
    D2[...] = OMEGA / DG2[...]
    coefficients3(OMEGA / (restrict2(S2[...]) + center[3]))
    SC[4:20, 16:48, :] = jnp.ones((16, 32, LANES), F32)
    finish(volume_moves)
    finish(weight_moves)
    weight_total = WS[...]
    for d in range(1, 8):
        weight_total += WB[d]
    IW[...] = 1.0 / weight_total

    def vcycle(n, slot):
        UA[4:20, 16:48, :] = D0[4:20, 16:48, :] * SC[4:20, 16:48, :]

        def own0(z):
            UB[pl.ds(z, 3), 8:56, :] = sweep(0, UA, SC, D0, z, 3, 8, 48)

        over(3, 18, 3, own0)
        restrict0(lambda z: residual(0, UB, SC, DG0, z, 4, 8, 48))
        begin_halo1(slot)
        VA[4:14, 8:32, :] = D1[4:14, 8:32, :] * S1C[4:14, 8:32, :]

        def own1(z):
            VC[pl.ds(z, 6), 8:32, :] = sweep(1, VA, S1C, D1, z, 6, 8, 24)

        over(3, 12, 6, own1)
        restrict1(lambda z: residual(1, VC, S1C, DG1, z, 8, 8, 24), slot)
        begin(gather(slot))

        @pl.when(n > 0)
        def _():
            finish_halo0(slot)

        source0 = S0.at[slot]

        def first0(z):
            U0a[pl.ds(z, 2), 8:56, :] = D0[pl.ds(z, 2), 8:56, :] * source0[pl.ds(z, 2), 8:56, :]

        over(1, 22, 2, first0)

        def pre0(z):
            U0b[pl.ds(z, 4), 8:56, :] = sweep(0, U0a, source0, D0, z, 4, 8, 48)

        over(2, 20, 4, pre0)
        summed1(slot)
        U1a[1:17, 8:32, :] = D1[1:17, 8:32, :] * S1[1:17, 8:32, :]

        def pre1(z):
            U1b[pl.ds(z, 7), 8:32, :] = sweep(1, U1a, S1, D1, z, 7, 8, 24)

        over(2, 14, 7, pre1)

        finish_gather(slot)
        gathered(slot)
        U2[1:5, 8:40, :] = D2[...] * S2[...]
        sweep2()
        mid, total = neighbours2()
        u3 = level3(restrict2(S2[...] - DG2[...] * mid + total))
        p = dot(u3, P3[...])
        for k in range(4):
            for i in range(4):
                r = 8 * (i // 2)
                C2[k, pl.ds(i, 8, stride=4), :] = p[r : r + 8, LANES * k : LANES * k + LANES]
        U2[1:5, 8:40, :] += C2[...]
        sweep2()
        sweep2()

        finish_gather_sends(slot)

        window = pl.ds(pl.multiple_of(8 * cy, 8), 24)
        own = U2[1 + cz, window, :][4:20]
        sides = jnp.where(upper_half, U2[cz, window, :][4:20], U2[2 + cz, window, :][4:20])
        wide = dot(jnp.concatenate([own, sides], axis=0), E1[...])
        for k in range(8):
            r, q = (0, k - 2) if 2 <= k < 6 else (16, (k - 2) % 4)
            C1[k, pl.ds(0, 16, stride=2), :] = wide[r : r + 16, LANES * q : LANES * q + LANES]
            C1[k, pl.ds(1, 16, stride=2), :] = wide[r : r + 16, LANES * q : LANES * q + LANES]
        for k in range(8):
            U1b[1 + 2 * k, 8:32, :] += C1[k, 4:28, :]
            U1b[2 + 2 * k, 8:32, :] += C1[k, 4:28, :]

        def post1a(z):
            U1a[pl.ds(z, 6), 8:32, :] = sweep(1, U1b, S1, D1, z, 6, 8, 24)

        over(3, 12, 6, post1a)

        def post1b(z):
            U1b[pl.ds(z, 5), 8:32, :] = sweep(1, U1a, S1, D1, z, 5, 8, 24)

        over(4, 10, 5, post1b)

        def widen0(i):
            wide = dot(flat(U1b[pl.ds(4 + i, 5), 8:32, :]), Px[...]).reshape(5, 24, LANES)
            C0[:, pl.ds(0, 24, stride=2), :] = wide
            C0[:, pl.ds(1, 24, stride=2), :] = wide
            for k in range(5):
                U0b[2 + 2 * (i + k), 8:56, :] += C0[k]
                U0b[3 + 2 * (i + k), 8:56, :] += C0[k]

        over(0, 10, 5, widen0)

        def post0a(z):
            U0a[pl.ds(z, 3), 8:56, :] = sweep(0, U0b, source0, D0, z, 3, 8, 48)

        over(3, 18, 3, post0a)

        def post0b(z):
            return sweep(0, U0a, source0, D0, z, 4, 16, 32)

        @pl.when(slot == 0)
        def _():
            for z in range(4, 20, 4):
                p = VB[z - 4 : z] / post0b(z)
                S0[1, z : z + 4, 16:48, :] = p
                SC[z : z + 4, 16:48, :] = p

        @pl.when(slot == 1)
        def _():
            for z in range(4, 20, 4):
                MB[z - 4 : z] = post0b(z)

    def centroid(last):
        sibling = (member + 1 - 2 * mc, slab)

        def marginal(at):
            m = S0[0, pl.ds(4 + at, 4), 16:48, :] * MB[pl.ds(at, 4)]
            MB[pl.ds(at, 4)] = m
            LB[pl.ds(at, 4)] = weight_ref[0] * jnp.log(m)

        def update(at):
            p = QB[at] * CB[at]
            S0[0, 4 + at, 16:48, :] = p
            SC[4 + at, 16:48, :] = p

        def along_x(d):
            return (2 * lax.rem(mx + d, 4) + mc, slab)

        swaps, pieces, spread, passed = [], [], [], []
        for q in range(2):
            marginal(8 * q + 4 * (1 - mc))
            theirs, here = LB.at[pl.ds(8 * q + 4 * (1 - mc), 4)], XB.at[pl.ds(4 * q, 4)]
            swaps.append(remote(theirs, here, x_send.at[q], x_recv.at[q], sibling))
            swaps[q].start()
        for q in range(2):
            marginal(8 * q + 4 * mc)

        for q in range(2):
            swaps[q].wait_recv()
            HB[4 * q : 4 * q + 4] = LB[pl.ds(8 * q + 4 * mc, 4)] + XB[4 * q : 4 * q + 4]
            pieces.append([])
            for d in (2, 1, 3):
                part = HB.at[pl.ds(4 * q + lax.rem(mx + d, 4), 1)]
                pieces[q].append(remote(part, PB.at[q, d - 1], p_send.at[q, d - 1], p_recv.at[q, d - 1], along_x(d)))
            begin(pieces[q])

        for z in range(0, 16, 4):
            QB[z : z + 4] = S0[0, 4 + z : 8 + z, 16:48, :] / MB[z : z + 4]

        @pl.when(last)
        def _():
            begin(multiplier_moves())
            mult_out[:, mine, :] = QB[pl.ds(4 * cy, 4)]

        inverse = jnp.broadcast_to(IW[...][None], (4, 8, LANES)).reshape(1, 32, LANES)
        for q in range(2):
            for c in pieces[q]:
                c.wait_recv()
            total = HB[pl.ds(4 * q + mx, 1)] + PB[q, 0] + PB[q, 1] + PB[q, 2]
            own = 8 * q + 4 * mc + mx
            CB[pl.ds(own, 1)] = jnp.exp(total * inverse)
            made = CB.at[pl.ds(own, 1)]
            spread.append([remote(made, made, c_send.at[q, d - 1], c_recv.at[q, d - 1], along_x(d)) for d in (2, 1, 3)])
            passed.append([])
            for d in (0, 1, 3, 2):
                at = CB.at[pl.ds(8 * q + 4 * mc + lax.rem(mx - d + 4, 4), 1)]
                passed[q].append((d, remote(at, at, f_send.at[q, d], f_recv.at[q, d], sibling)))

            @pl.when(jnp.logical_not(last))
            def _():
                begin(spread[q])
                passed[q][0][1].start()
                update(own)

            @pl.when(last)
            def _():
                begin_slabs(q, own)

        @pl.when(jnp.logical_not(last))
        def _():
            for q in range(2):
                for (d, c), arrived in zip(passed[q][1:], spread[q][1:] + spread[q][:1]):
                    arrived.wait_recv()
                    c.start()
                    update(8 * q + 4 * mc + lax.rem(mx - d + 4, 4))
            for q in range(2):
                for d, c in passed[q]:
                    c.wait_recv()
                    update(8 * q + 4 * (1 - mc) + lax.rem(mx - d + 4, 4))
            for q in range(2):
                for c in spread[q] + [f for _, f in passed[q]]:
                    c.wait_send()

        @pl.when(last)
        def _():
            finish_slabs()

        for q in range(2):
            for c in [swaps[q]] + pieces[q]:
                c.wait_send()

    def slab_pieces(q, own):
        made, place = CB.at[pl.ds(own, 1)], cent_out.at[pl.ds(mx, 1), mine]
        return [
            remote(made, place, e_send.at[q, d], e_recv.at[d, cy], (2 * lax.rem(mx + d, 4) + mc, cz * 4 + 2 * q + mc))
            for d in range(4)
        ]

    def begin_slabs(q, own):
        home, copies = cy == 2 * q + mc, slab_pieces(q, own)
        for d in (2, 1, 3):
            copies[d].start()
        pl.when(jnp.logical_not(home))(copies[0].start)

        @pl.when(home)
        def _():
            cent_out[pl.ds(mx, 1), mine, :] = CB[pl.ds(own, 1)]

    def finish_slabs():
        receiver = lax.rem(cy, 2) == mc
        sibling = (member + 1 - 2 * mc, slab)

        def piece(d, e):
            return cent_out.at[pl.ds(lax.rem(mx - d + 4, 4), 1), pl.ds(32 * e, 32)]

        def passing(d, e):
            return remote(piece(d, e), piece(d, e), k_send.at[d, e], k_recv.at[d, e], sibling)

        order = [(d, e) for d in (0, 1, 3, 2) for e in range(4)]

        @pl.when(receiver)
        def _():
            for d, e in order:
                arrival = remote(piece(d, e), piece(d, e), e_send.at[0, d], e_recv.at[d, e], sibling)
                if d == 0:
                    pl.when(cy != e)(arrival.wait_recv)
                else:
                    arrival.wait_recv()
                passing(d, e).start()
            for d, e in order:
                passing(d, e).wait_send()

        @pl.when(jnp.logical_not(receiver))
        def _():
            for d, e in order:
                passing(d, e).wait_recv()

        for q in range(2):
            copies = slab_pieces(q, 8 * q + 4 * mc + mx)
            for d in (1, 2, 3):
                copies[d].wait_send()
            pl.when(cy != 2 * q + mc)(copies[0].wait_send)
        finish(multiplier_moves())

    def multiplier_moves():
        return to_slabs(QB, 0, 0, mult_out, o_send, o_recv)

    def half_step(n, slot):
        vcycle(n, slot)

        @pl.when(slot == 1)
        def _():
            centroid(n == 2 * ITERS - 1)

        @pl.when(n < 2 * ITERS - 1)
        def _():
            begin_halo0(1 - slot)


    def iteration(i, _):
        half_step(2 * i, 0)
        half_step(2 * i + 1, 1)
        return 0

    lax.fori_loop(0, ITERS, iteration, 0)

    mult_out[...] = mult_out[...] * cent_out[...]


def body(nonnegative_volumes, reaction, diffusivity, member_weights):
    vmem, smem = pl.BlockSpec(memory_space=pltpu.VMEM), pl.BlockSpec(memory_space=pltpu.SMEM)
    hbm = pl.BlockSpec(memory_space=pl.ANY)
    field = jax.ShapeDtypeStruct((4, 128, 128), F32)

    def buffer(*shape):
        return pltpu.VMEM((*shape, LANES), F32)

    dma = pltpu.SemaphoreType.DMA
    scratch = [
        buffer(2, 24, 64), *[buffer(24, 64) for _ in range(7)], buffer(5, 48), buffer(10, 48),
        *[buffer(18, 40) for _ in range(8)], buffer(8, 32), buffer(8, 32), buffer(5, 24),
        buffer(2, 2, 3, 24), buffer(2, 2, 5, 8), buffer(2, 4, 3, 8), buffer(2, 8, 8), buffer(2, 2, 8, 8), buffer(2, 4, 1, 8),
        buffer(2, 16, 24), buffer(4, 32), buffer(4, 32), buffer(4, 32), buffer(6, 48), buffer(4, 32), buffer(4, 32), buffer(16), buffer(6, 16),
        buffer(4, 128), buffer(2, 128), buffer(16, 8),
        buffer(16, 32), buffer(16, 32), buffer(16, 32), buffer(16, 32), buffer(8, 32), buffer(8, 32), buffer(2, 3, 1, 32), buffer(16, 32),
        buffer(8), buffer(8, 8), buffer(8),
        *[pltpu.VMEM(shape, BF16) for shape in ((128, 128), (512, 128), (512, 128), (128, 512), (128, 512), (128, 128))],
        dma((2, 8)), dma((2, 8)), dma((2, 8)), dma((2, 8)), dma((2,)), dma((2,)),
        dma((3,)), dma((3,)), dma((3,)), dma((3,)), dma((7,)), dma((7,)),
        dma((3,)), dma((2,)), dma((2,)), dma((2,)), *[dma((2, 3)) for _ in range(4)], dma((2, 4)), dma((2, 4)), dma((3,)), dma((3,)),
        dma((2, 4)), dma((4, 4)), dma((4, 4)), dma((4, 4)),
    ]
    centroid, multipliers = pl.pallas_call(
        kernel,
        out_shape=(field, field),
        in_specs=[hbm, hbm, smem, smem],
        out_specs=(vmem, vmem),
        scratch_shapes=scratch,
        compiler_params=pltpu.CompilerParams(collective_id=0, has_side_effects=True, vmem_limit_bytes=40 * 2**20),
    )(nonnegative_volumes[0], reaction, diffusivity, member_weights)
    return centroid, multipliers[None]


def solution(mesh):
    return jax.shard_map(
        body,
        mesh=mesh,
        in_specs=(P("member", "slab", None, None), P("slab", None, None), P(), P("member")),
        out_specs=(P("slab", None, None), P("member", "slab", None, None)),
        check_vma=False,
    )
```
